32 devices in a mesh: parts: 2 (over y), tensor: 8 (over z, x), dp: 2 (over core).
Axes of the slice: x: 2, y: 2, z: 4, core: 2. Of those that a mesh axis runs over, the one named last changes fastest.
Arguments:
- hidden: bfloat16 [512, 28672], P(('parts', 'dp'), 'tensor'), parts along dimension 0, may hold values from -6 to 6
- frozen_down_weight: bfloat16 [28672, 8192], P('tensor'), may hold values from -8 to 8
- adapter_down_weight: bfloat16 [57344, 64], P(('parts', 'tensor')), parts along dimension 0, may hold values from -0.03125 to 0.03125
- adapter_up_weight: bfloat16 [128, 8192], P('parts'), parts along dimension 0, may hold values from -0.75 to 0.75
- magnitude: float32 [16384], P(('parts', 'tensor')), parts along dimension 0, may hold values from 0.5 to 2
- cotangent: bfloat16 [512, 8192], P(('parts', 'dp'), 'tensor'), parts along dimension 0, may hold values from -6 to 6
Outputs:
- mixed: bfloat16 [512, 8192], P(('parts', 'dp'), 'tensor'), parts along dimension 0
- hidden_gradient: bfloat16 [512, 28672], P(('parts', 'dp'), 'tensor'), parts along dimension 0
- down_weight_gradient: float32 [57344, 64], P(('parts', 'tensor')), parts along dimension 0
- up_weight_gradient: float32 [128, 8192], P('parts', 'tensor'), parts along dimension 0
- grad_magnitude: float32 [16384], P(('parts', 'tensor')), parts along dimension 0
The draws below stay inside these ranges and needn't reach their ends.
There are 2 independent parts, one for each index of `parts`. The reference program is written for one: setup_inputs(seed, part) draws one part's arguments, and reference() takes and returns one part's arrays. A program takes and returns all parts, laid end to end along the dimension named above; an argument that names none is the same for every part. Nothing has to cross between parts.
All inputs are finite; a program needn't handle non-finite values.
Results may differ from the reference program's by a relative error of at most 0.0075.
Values may be sent and summed in bfloat16 or wider, within the bound.
No kernel may reach another device: no remote copies, remote signals or barrier semaphores. Data moves between devices by JAX's collectives and lax.ppermute only.
A program may use at most 192 MiB of HBM per device.

```python
import math
import jax
import jax.numpy as jnp
from jax import lax

MODEL_WIDTH = 8192
FEEDFORWARD_UNITS = 28672
ADAPTER_RANK = 64
TOKENS = 256


def draw_frozen_down_weight(key, part):
    key = jax.random.fold_in(key, 11)
    key_rows, key_cols, key_main = jax.random.split(key, 3)
    trend = jnp.exp(math.log(3.0) * jnp.arange(FEEDFORWARD_UNITS, dtype=jnp.float32) / FEEDFORWARD_UNITS).reshape(FEEDFORWARD_UNITS, 1)
    column_slice = jnp.exp(jax.random.uniform(key_cols, (1, MODEL_WIDTH), jnp.float32) * math.log(10.0))
    rows = jnp.exp(jax.random.uniform(key_rows, (FEEDFORWARD_UNITS, 1), jnp.float32) * math.log(10.0)) * trend
    entries = jnp.clip(jax.random.normal(key_main, (FEEDFORWARD_UNITS, MODEL_WIDTH), jnp.float32), -4.0, 4.0)
    return (entries * rows * column_slice / (16.0 * math.sqrt(FEEDFORWARD_UNITS))).astype(jnp.bfloat16)


def block_levels(rng, dims, cuts, low, top_value):
    loudness = 1.0
    for position, parts in cuts:
        steps = jax.random.uniform(jax.random.fold_in(jax.random.fold_in(rng, 6), position), (parts,), jnp.float32, low / len(cuts), top_value / len(cuts))
        loudness = loudness * jnp.repeat(jnp.exp(steps), dims[position] // parts).reshape((-1,) + (1,) * (len(dims) - 1 - position))
    return loudness


def scatter_about(own_key, extent, spread, most, cuts=(), kind=jnp.bfloat16):
    factor_of = block_levels(own_key, extent, cuts, -0.22, 0.18) if cuts else 1.0
    result = jax.random.normal(own_key, extent, jnp.float32) * spread * factor_of
    return jnp.minimum(jnp.maximum(result, -most), most).astype(kind)


def setup_inputs(seed: int = 0, part: int = 0) -> dict:
    splits = jax.random.split(jax.random.key(seed), 7)
    part_keys = jax.random.split(jax.random.fold_in(splits[6], part), 7)
    return {
        "hidden": scatter_about(part_keys[0], (TOKENS, FEEDFORWARD_UNITS), 1.0, 6.0, ((0, 2), (1, 8))),
        "frozen_down_weight": draw_frozen_down_weight(jax.random.fold_in(splits[6], 71), part),
        "adapter_down_weight": scatter_about(part_keys[2], (FEEDFORWARD_UNITS, ADAPTER_RANK), FEEDFORWARD_UNITS ** -0.5, 0.03125, ((0, 8),)),
        "adapter_up_weight": scatter_about(part_keys[3], (ADAPTER_RANK, MODEL_WIDTH), ADAPTER_RANK ** -0.5, 0.75),
        "magnitude": jnp.clip(jnp.exp(math.log(2.0) - 1.3862944 * jax.random.uniform(part_keys[4], (MODEL_WIDTH,), jnp.float32) ** block_levels(part_keys[4], (MODEL_WIDTH,), ((0, 8),), -0.2, 0.2)), 0.5, 2.0),
        "cotangent": scatter_about(part_keys[5], (TOKENS, MODEL_WIDTH), 1.0, 6.0, ((0, 2), (1, 8))),
    }


adapter_scale = 2.0
stability_floor = 1e-06

def squared_columns(frozen_down_weight, adapter_down_weight, adapter_up_weight):
    current_block = math.gcd(FEEDFORWARD_UNITS, 2048)
    block_count = FEEDFORWARD_UNITS // current_block
    weights = frozen_down_weight.reshape(block_count, current_block, MODEL_WIDTH)
    down_pieces = adapter_down_weight.reshape(block_count, current_block, ADAPTER_RANK)

    def one_block(pair):
        weight_column_block, down_weight_block = pair
        combined_weight = weight_column_block.astype(jnp.float32) + adapter_scale * jnp.dot(down_weight_block, adapter_up_weight, preferred_element_type=jnp.float32)
        return lax.optimization_barrier(jnp.sum(combined_weight * combined_weight, axis=0))
    return lax.optimization_barrier(jnp.sum(lax.map(one_block, (weights, down_pieces)), axis=0))

def reference(hidden, frozen_down_weight, adapter_down_weight, adapter_up_weight, magnitude, cotangent):
    frozen_product = jnp.dot(hidden, frozen_down_weight, preferred_element_type=jnp.float32)
    reduced_rank_product = jnp.dot(hidden, adapter_down_weight, preferred_element_type=jnp.float32)
    unscaled_output = frozen_product + adapter_scale * jnp.dot(reduced_rank_product, adapter_up_weight.astype(jnp.float32), precision=lax.Precision.HIGHEST)
    column_length_norm = jnp.sqrt(squared_columns(frozen_down_weight, adapter_down_weight, adapter_up_weight) + stability_floor)
    rescale = magnitude / column_length_norm
    mixed = (unscaled_output * rescale).astype(jnp.bfloat16)
    upstream = cotangent.astype(jnp.float32)
    scaled_output = (upstream * rescale).astype(jnp.bfloat16)
    grad_magnitude = lax.optimization_barrier(jnp.sum(upstream * unscaled_output, axis=0)) / column_length_norm
    projected_output = jnp.dot(scaled_output, adapter_up_weight.T, preferred_element_type=jnp.float32).astype(jnp.bfloat16)
    hidden_gradient = jnp.dot(scaled_output, frozen_down_weight.T, preferred_element_type=jnp.float32)
    hidden_gradient = hidden_gradient + adapter_scale * jnp.dot(projected_output, adapter_down_weight.T, preferred_element_type=jnp.float32)
    hidden_gradient = hidden_gradient.astype(jnp.bfloat16)
    down_weight_gradient = adapter_scale * jnp.dot(hidden.T, projected_output, preferred_element_type=jnp.float32)
    up_weight_gradient = adapter_scale * jnp.dot(reduced_rank_product.T, scaled_output.astype(jnp.float32), precision=lax.Precision.HIGHEST)
    return (mixed, hidden_gradient, down_weight_gradient, up_weight_gradient, grad_magnitude)
```

```python
import functools

import jax
import jax.numpy as jnp
from jax import lax
from jax.experimental import pallas as pl
from jax.experimental.pallas import tpu as pltpu
from jax.sharding import PartitionSpec as P

adapter_scale = 2.0
stability_floor = 1e-06
pad_rows = 16
vmem_bytes = 50 * 1024 * 1024
f32, bf16 = jnp.float32, jnp.bfloat16
contract_trailing = (((1,), (1,)), ((), ()))
contract_first = (((0,), (0,)), ((), ()))


def dot(a, b, dims=(((1,), (0,)), ((), ()))):
    return lax.dot_general(a, b, dims, preferred_element_type=f32)


def split_pair(x):
    high = x.astype(bf16)
    return high, (x - high.astype(f32)).astype(bf16)


def sum_of_squares(w_ref):
    rows, width = w_ref.shape
    totals = [jnp.zeros((8, width), f32) for _ in range(2)]
    for i in range(rows // 16):
        w = w_ref[i * 16 : (i + 1) * 16, :].astype(f32)
        w = w * w
        totals[0] = totals[0] + w[:8]
        totals[1] = totals[1] + w[8:]
    return jnp.sum(totals[0] + totals[1], axis=0, keepdims=True)


def forward_kernel(tokens, rank, steps, place_ref, own_ref, other_ref, at_ref, w_ref, b_ref, *rest):
    outs, squares_ref, lowrank_ref, lhs_ref, adapter_ref = rest[:steps], *rest[steps:]
    step = pl.program_id(0)
    both = 2 * tokens

    @pl.when(step == 0)
    def _():
        lhs_ref[:tokens, :] = own_ref[...]
        lhs_ref[tokens:both, :] = other_ref[...]
        lhs_ref[both:, :] = at_ref[...]
        lowrank = dot(lhs_ref[...], at_ref[...], contract_trailing)
        high, low = split_pair(lowrank)
        adapter_ref[:, :rank] = high
        adapter_ref[:, rank:] = low
        lowrank_ref[...] = lowrank[:tokens]

    up = b_ref[...]
    product = dot(lhs_ref[...], w_ref[...])
    through = dot(adapter_ref[...], jnp.concatenate([up, up], axis=0))
    result = (product[:both] + adapter_scale * through[:both]).astype(bf16)
    for k in range(steps):

        @pl.when(step == k)
        def _():
            outs[k][...] = result

    cross = jnp.sum(up.astype(f32) * (product[both:] + through[both:]), axis=0, keepdims=True)
    squares_ref[0] = sum_of_squares(w_ref) + (adapter_scale * adapter_scale) * cross


def forward(place, own, other, at, weight, up, half):
    tokens, rows = own.shape
    rank = at.shape[0]
    steps = place.shape[0] // 2
    whole = lambda *shape: pl.BlockSpec(shape, lambda i, p: (0,) * len(shape))
    column = lambda n: pl.BlockSpec((n, half), lambda i, p: (0, p[i]))
    out_shape = [jax.ShapeDtypeStruct((2 * tokens, half), bf16)] * steps + [
        jax.ShapeDtypeStruct((steps, 1, half), f32),
        jax.ShapeDtypeStruct((tokens, rank), f32),
    ]
    return pl.pallas_call(
        functools.partial(forward_kernel, tokens, rank, steps),
        grid_spec=pltpu.PrefetchScalarGridSpec(
            num_scalar_prefetch=1,
            grid=(steps,),
            in_specs=[whole(tokens, rows), whole(tokens, rows), whole(rank, rows), column(rows), column(rank)],
            out_specs=[whole(2 * tokens, half)] * steps
            + [pl.BlockSpec((1, 1, half), lambda i, p: (i, 0, 0)), whole(tokens, rank)],
            scratch_shapes=[
                pltpu.VMEM((2 * tokens + rank, rows), bf16),
                pltpu.VMEM((2 * tokens + rank, 2 * rank), bf16),
            ],
        ),
        out_shape=out_shape,
        compiler_params=pltpu.CompilerParams(vmem_limit_bytes=vmem_bytes),
        cost_estimate=pl.CostEstimate(
            flops=2 * steps * (2 * tokens + rank) * rows * half,
            bytes_accessed=2 * steps * rows * half + 8 * tokens * rows,
            transcendentals=0,
        ),
        name="forward",
    )(place, own, other, at, weight, up)


def backward_kernel(tokens, rank, steps, place_ref, *refs):
    cots, (squares_ref, at_ref, w_ref, b_ref) = refs[:steps], refs[steps : steps + 4]
    own_out, other_out, proj_own, proj_other, cot_ref, acc_ref, proj_ref = refs[steps + 4 :]
    step = pl.program_id(0)
    both = 2 * tokens
    for k in range(steps):

        @pl.when(step == k)
        def _():
            cot_ref[...] = cots[k][...]

    magnitude = jnp.sum(cot_ref[both:, :].astype(f32), axis=0, keepdims=True)
    rescale = magnitude / jnp.sqrt(squares_ref[0] + stability_floor)
    scaled = (cot_ref[:both, :].astype(f32) * rescale).astype(bf16)
    projected = dot(scaled, b_ref[...], contract_trailing)

    @pl.when(step == 0)
    def _():
        proj_ref[...] = projected
        acc_ref[...] = dot(scaled, w_ref[...], contract_trailing)

    @pl.when(step > 0)
    def _():
        proj_ref[...] += projected
        acc_ref[...] += dot(scaled, w_ref[...], contract_trailing)

    @pl.when(step == steps - 1)
    def _():
        proj = proj_ref[...]
        total = acc_ref[...] + adapter_scale * dot(proj.astype(bf16), at_ref[...])
        own_out[...] = total[:tokens]
        other_out[...] = total[tokens:].astype(bf16)
        proj_own[...] = proj[:tokens]
        proj_other[...] = proj[tokens:]


def backward(place, cots, squares, at, weight, up, half):
    steps = len(cots)
    both = cots[0].shape[0] - pad_rows
    tokens = both // 2
    rank, rows = at.shape
    whole = lambda *shape: pl.BlockSpec(shape, lambda i, p: (0,) * len(shape))
    column = lambda n: pl.BlockSpec((n, half), lambda i, p: (0, p[i]))
    out_shape = [
        jax.ShapeDtypeStruct((tokens, rows), f32),
        jax.ShapeDtypeStruct((tokens, rows), bf16),
        jax.ShapeDtypeStruct((tokens, rank), f32),
        jax.ShapeDtypeStruct((tokens, rank), f32),
    ]
    return pl.pallas_call(
        functools.partial(backward_kernel, tokens, rank, steps),
        grid_spec=pltpu.PrefetchScalarGridSpec(
            num_scalar_prefetch=1,
            grid=(steps,),
            in_specs=[whole(both + pad_rows, half)] * steps
            + [
                pl.BlockSpec((1, 1, half), lambda i, p: (p[steps + i], 0, 0)),
                whole(rank, rows),
                column(rows),
                column(rank),
            ],
            out_specs=[whole(*o.shape) for o in out_shape],
            scratch_shapes=[
                pltpu.VMEM((both + pad_rows, half), bf16),
                pltpu.VMEM((both, rows), f32),
                pltpu.VMEM((both, rank), f32),
            ],
        ),
        out_shape=out_shape,
        compiler_params=pltpu.CompilerParams(vmem_limit_bytes=vmem_bytes),
        cost_estimate=pl.CostEstimate(
            flops=2 * steps * both * rows * half,
            bytes_accessed=2 * steps * rows * half,
            transcendentals=0,
        ),
        name="backward",
    )(place, *cots, squares, at, weight, up)


def split_columns(n, hidden, weight, down, up, magnitude, cotangent):
    tokens = hidden.shape[0]
    half = magnitude.shape[0] // 2
    me, core = lax.axis_index("tensor"), lax.axis_index("dp")
    swap = lambda x: lax.ppermute(x, "dp", [(0, 1), (1, 0)])
    send = lambda x, r: lax.ppermute(x, "tensor", [(t, t ^ r) for t in range(n)])
    mine = lambda x, axis: lax.dynamic_slice_in_dim(x, core * half, half, axis)
    theirs = lambda x, axis: lax.dynamic_slice_in_dim(x, (1 - core) * half, half, axis)
    place = lambda rs: jnp.stack([2 * (me ^ r) + core for r in rs] + [me ^ r for r in rs]).astype(jnp.int32)
    at = down.T
    odds, evens = list(range(3, n, 2)) + [1], list(range(2, n, 2)) + [0]

    hidden_other = swap(hidden)
    cot_own, cot_other = mine(cotangent, 1), swap(theirs(cotangent, 1))
    own_magnitude = mine(magnitude, 0)
    first = lax.reduce_precision(own_magnitude, 8, 7)
    second = lax.reduce_precision(own_magnitude - first, 8, 7)
    third = own_magnitude - first - second
    magnitude_rows = jnp.concatenate(
        [jnp.stack([first, second, third]), jnp.zeros((pad_rows - 3, half), f32)]
    ).astype(bf16)
    own_block = jnp.concatenate([cot_own, cot_other, magnitude_rows])

    cots = {0: own_block}
    for r in range(2, n, 2):
        cots[r] = send(own_block, r)
    for r in range(0, n, 2):
        cots[r + 1] = send(cots[r], 1)

    *parts_odd, squares_odd, lowrank = forward(place(odds), hidden, hidden_other, at, weight, up, half)
    arrived = {r - 1: send(p, 1) for r, p in zip(odds, parts_odd)}
    *parts_even, squares_even, _ = forward(place(evens), hidden, hidden_other, at, weight, up, half)
    partial = dict(zip(evens, parts_even))
    total = {r: partial[r].astype(f32) + arrived[r].astype(f32) for r in evens}
    along = [send(total[r].astype(bf16), r) for r in evens if r]

    sq_even, sq_odd = squares_even[:, 0], squares_odd[:, 0]
    got_even, got_odd = send((sq_even, sq_odd), 1)
    sq_even, sq_odd = sq_even + got_odd, sq_odd + got_even
    squares_mine = jnp.stack([sq_even, sq_odd])
    index_of = {r: i for i, r in enumerate(evens)}
    squares = squares_mine
    for r in evens:
        if r:
            order = jnp.array([index_of[e ^ r] for e in evens])
            squares = squares + send(squares_mine, r)[:, order]
    squares_own = squares[0, index_of[0]]
    squares_rows = squares.reshape(n, 1, half)

    lowrank_sum = lowrank + send(lowrank, 1)
    lowrank_own = lowrank_sum
    for r in evens:
        if r:
            lowrank_own = lowrank_own + send(lowrank_sum, r)
    lowrank_all = jnp.concatenate([lowrank_own, swap(lowrank_own)])

    rs = evens + odds
    order_place = jnp.concatenate(
        [jnp.stack([2 * (me ^ r) + core for r in rs]).astype(jnp.int32),
         jnp.array([index_of[r - r % 2] + (r % 2) * len(evens) for r in rs], jnp.int32)]
    )
    grad_own, grad_other, proj_own, proj_other = backward(
        order_place, [cots[r] for r in rs], squares_rows, at, weight, up, half
    )
    hidden_gradient = (grad_own + swap(grad_other).astype(f32)).astype(bf16)
    from_own, from_other = swap((proj_own, proj_other))
    proj_own = (proj_own + from_other).astype(bf16)
    proj_other = (proj_other + from_own).astype(bf16)
    down_weight_gradient = adapter_scale * (
        dot(proj_own, hidden, contract_first) + dot(proj_other, hidden_other, contract_first)
    ).T

    norm = jnp.sqrt(squares_own + stability_floor)
    rescale = own_magnitude / norm
    upstream = own_block[: 2 * tokens].astype(f32)
    scaled = (upstream * rescale).astype(bf16)
    up_half = adapter_scale * lax.dot_general(
        lowrank_all, scaled.astype(f32), contract_first, precision=lax.Precision.HIGHEST
    )
    unscaled = total[0]
    for part in along:
        unscaled = unscaled + part.astype(f32)
    mixed = (unscaled * rescale).astype(bf16)
    magnitude_half = jnp.sum(upstream * unscaled, axis=0) / norm

    def join(own, other, axis):
        pair = jnp.concatenate([own, other, own], axis)
        return lax.dynamic_slice_in_dim(pair, core * half, 2 * half, axis)

    mixed = join(mixed[:tokens], swap(mixed[tokens:]), 1)
    up_weight_gradient = join(up_half, swap(up_half), 1)
    grad_magnitude = join(magnitude_half, swap(magnitude_half), 0)
    return (mixed, hidden_gradient, down_weight_gradient, up_weight_gradient, grad_magnitude)


def by_tokens(hidden, frozen_down_weight, adapter_down_weight, adapter_up_weight, magnitude, cotangent):
    column_slice = magnitude.shape[0]
    block_offset = lax.axis_index("tensor") * column_slice
    combined_weight = frozen_down_weight.astype(f32) + adapter_scale * dot(adapter_down_weight, adapter_up_weight)
    squares_part = jnp.sum(combined_weight * combined_weight, axis=0)
    squares, reduced_rank_product = lax.psum((squares_part, dot(hidden, adapter_down_weight)), "tensor")
    norm_all = jnp.sqrt(squares + stability_floor)
    column_length_norm = lax.dynamic_slice_in_dim(norm_all, block_offset, column_slice)
    up_weight_columns = lax.dynamic_slice_in_dim(adapter_up_weight, block_offset, column_slice, 1)
    summed_output = lax.psum_scatter(dot(hidden, frozen_down_weight), "tensor", scatter_dimension=1, tiled=True)
    unscaled_output = summed_output + adapter_scale * jnp.dot(
        reduced_rank_product, up_weight_columns.astype(f32), precision=lax.Precision.HIGHEST
    )
    rescale = magnitude / column_length_norm
    mixed = (unscaled_output * rescale).astype(bf16)
    upstream = cotangent.astype(f32)
    scaled_output = (upstream * rescale).astype(bf16)
    magnitude_part = jnp.sum(upstream * unscaled_output, axis=0) / column_length_norm
    block_input = lax.all_gather(scaled_output, "tensor", axis=1, tiled=True)
    projected_output = dot(block_input, adapter_up_weight, contract_trailing).astype(bf16)
    hidden_gradient = dot(block_input, frozen_down_weight, contract_trailing)
    hidden_gradient = hidden_gradient + adapter_scale * dot(projected_output, adapter_down_weight, contract_trailing)
    hidden_gradient = hidden_gradient.astype(bf16)
    down_gradient_piece = adapter_scale * dot(hidden, projected_output, contract_first)
    up_gradient_piece = adapter_scale * lax.dot_general(
        reduced_rank_product, scaled_output.astype(f32), contract_first, precision=lax.Precision.HIGHEST
    )
    pieces = (down_gradient_piece, up_gradient_piece, magnitude_part)
    pieces = [lax.psum(p.astype(bf16), "dp").astype(f32) for p in pieces]
    return (mixed, hidden_gradient, *pieces)


def solution(mesh):
    n = mesh.shape["tensor"]

    def local(hidden, weight, down, up, magnitude, cotangent):
        aligned = magnitude.shape[0] % 256 == 0 and weight.shape[0] % 256 == 0 and hidden.shape[0] % 16 == 0
        if aligned and mesh.shape["dp"] == 2 and n in (4, 8, 16) and down.shape[1] == 64:
            return split_columns(n, hidden, weight, down, up, magnitude, cotangent)
        return by_tokens(hidden, weight, down, up, magnitude, cotangent)

    in_specs = (
        P(("parts", "dp"), "tensor"),
        P("tensor", None),
        P(("parts", "tensor"), None),
        P("parts", None),
        P(("parts", "tensor")),
        P(("parts", "dp"), "tensor"),
    )
    out_specs = (
        P(("parts", "dp"), "tensor"),
        P(("parts", "dp"), "tensor"),
        P(("parts", "tensor"), None),
        P("parts", "tensor"),
        P(("parts", "tensor")),
    )
    return jax.shard_map(local, mesh=mesh, in_specs=in_specs, out_specs=out_specs, check_vma=False)
```

```python
import functools

import jax
import jax.numpy as jnp
from jax import lax
from jax.experimental import pallas as pl
from jax.experimental.pallas import tpu as pltpu
from jax.sharding import PartitionSpec as P

adapter_scale = 2.0
stability_floor = 1e-06
pad_rows = 16
vmem_bytes = 28 * 1024 * 1024
f32, bf16 = jnp.float32, jnp.bfloat16
small_cost = pl.CostEstimate(flops=1 << 20, bytes_accessed=1 << 20, transcendentals=0)
contract_trailing = (((1,), (1,)), ((), ()))
contract_first = (((0,), (0,)), ((), ()))


def dot(a, b, dims=(((1,), (0,)), ((), ()))):
    return lax.dot_general(a, b, dims, preferred_element_type=f32)


def split_pair(x):
    high = x.astype(bf16)
    return high, (x - high.astype(f32)).astype(bf16)


def sum_of_squares(w_ref):
    rows, width = w_ref.shape
    totals = [jnp.zeros((8, width), f32) for _ in range(2)]
    for i in range(rows // 16):
        w = w_ref[i * 16 : (i + 1) * 16, :].astype(f32)
        w = w * w
        totals[0] = totals[0] + w[:8]
        totals[1] = totals[1] + w[8:]
    return jnp.sum(totals[0] + totals[1], axis=0, keepdims=True)


def vmem():
    return pl.BlockSpec(memory_space=pltpu.VMEM)


def params():
    return pltpu.CompilerParams(vmem_limit_bytes=vmem_bytes)


def block_kernel(tokens, core_ref, own_ref, other_ref, magnitude_ref, out_ref):
    out_ref[:tokens, :] = own_ref[...]
    out_ref[tokens : 2 * tokens, :] = other_ref[...]
    out_ref[2 * tokens :, :] = magnitude_ref[...]


def own_block(core, cotangent, other, magnitude_rows):
    tokens, columns = cotangent.shape
    half = columns // 2
    padded = 2 * tokens + pad_rows
    return pl.pallas_call(
        functools.partial(block_kernel, tokens),
        grid_spec=pltpu.PrefetchScalarGridSpec(
            num_scalar_prefetch=1,
            grid=(1,),
            in_specs=[
                pl.BlockSpec((tokens, half), lambda i, c: (0, c[0])),
                pl.BlockSpec((tokens, half), lambda i, c: (0, c[0])),
                pl.BlockSpec((pad_rows, half), lambda i, c: (0, c[0])),
            ],
            out_specs=pl.BlockSpec((padded, half), lambda i, c: (0, 0)),
        ),
        out_shape=jax.ShapeDtypeStruct((padded, half), bf16),
        cost_estimate=small_cost,
        name="own_block",
    )(core, cotangent, other, magnitude_rows)


def forward_kernel(tokens, rank, n, first, place_ref, *refs):
    if first:
        own_ref, other_ref, at_ref, b_ref, w_ref, out_ref, stats_ref, lhs_ref, adapter_ref = refs[:-3]
    else:
        lhs_ref, adapter_ref, before_ref, b_ref, w_ref, out_ref, stats_ref = refs[:-3]
    acc_ref, squares_ref, sem = refs[-3:]
    block, step = pl.program_id(0), pl.program_id(1)
    blocks, steps = pl.num_programs(0), pl.num_programs(1)
    both = 2 * tokens
    half = acc_ref.shape[1]
    depth = w_ref.shape[0]

    @pl.when((block == 0) & (step == 0))
    def _():
        if first:
            spans = [(own_ref, 0, tokens), (other_ref, tokens, tokens), (at_ref, both, rank)]
            copies = [
                pltpu.make_async_copy(ref, lhs_ref.at[start : start + size], sem.at[i])
                for i, (ref, start, size) in enumerate(spans)
            ]
            for copy in copies:
                copy.start()
            for copy in copies:
                copy.wait()
            lowrank = dot(lhs_ref[...], lhs_ref[both:, :], contract_trailing)
            high, low = split_pair(lowrank)
            adapter_ref[:, :rank] = high
            adapter_ref[:, rank:] = low
            turned = lowrank[:tokens].T
            lanes = half // tokens
            span = rank // lanes
            stats_ref[:n, :] = jnp.zeros((n, half), f32)
            for j in range(lanes):
                stats_ref[n:, j * tokens : (j + 1) * tokens] = turned[j * span : (j + 1) * span]
        else:
            stats_ref[...] = before_ref[...]

    columns = pl.ds(pl.multiple_of(step * depth, depth), depth)
    product = dot(lhs_ref[:, columns], w_ref[...])
    squares = sum_of_squares(w_ref)

    @pl.when(step == 0)
    def _():
        acc_ref[...] = product
        squares_ref[...] = squares

    @pl.when((step > 0) & (step < steps - 1))
    def _():
        acc_ref[...] += product
        squares_ref[...] += squares

    @pl.when(step == steps - 1)
    def _():
        up = b_ref[:, pl.ds(pl.multiple_of(place_ref[block] * half, half), half)]
        through = dot(adapter_ref[...], jnp.concatenate([up, up], axis=0))
        total = acc_ref[...] + product
        out_ref[0] = (total[:both] + adapter_scale * through[:both]).astype(bf16)
        cross = up.astype(f32) * (2 * adapter_scale * total[both:] + adapter_scale * adapter_scale * through[both:])
        stats_ref[pl.ds(place_ref[blocks + block], 1), :] = (
            squares_ref[...] + squares + jnp.sum(cross, axis=0, keepdims=True)
        )


def forward(n, place, weight, up, half, first=None, later=None):
    blocks = place.shape[0] // 2
    rows = weight.shape[0]
    steps = 2
    if later is None:
        own, other, at = first
        tokens, rank = own.shape[0], at.shape[0]
        operands = [own, other, at]
        specs = [pl.BlockSpec(memory_space=m) for m in (pltpu.HBM, pl.ANY, pltpu.HBM)]
    else:
        lhs, adapter, before = operands = later
        rank = adapter.shape[1] // 2
        tokens = (lhs.shape[0] - rank) // 2
        specs = [vmem()] * 3
    stats = (n + rank * tokens // half, half)
    extra = [((2 * tokens + rank, rows), bf16), ((2 * tokens + rank, 2 * rank), bf16)] if first else []
    return pl.pallas_call(
        functools.partial(forward_kernel, tokens, rank, n, later is None),
        grid_spec=pltpu.PrefetchScalarGridSpec(
            num_scalar_prefetch=1,
            grid=(blocks, steps),
            in_specs=specs
            + [
                vmem(),
                pl.BlockSpec((rows // steps, half), lambda i, j, p: (j, p[i])),
            ],
            out_specs=[pl.BlockSpec((1, 2 * tokens, half), lambda i, j, p: (i, 0, 0)), vmem()] + [vmem()] * len(extra),
            scratch_shapes=[
                pltpu.VMEM((2 * tokens + rank, half), f32),
                pltpu.VMEM((1, half), f32),
                pltpu.SemaphoreType.DMA((3,)),
            ],
        ),
        out_shape=[jax.ShapeDtypeStruct((blocks, 2 * tokens, half), bf16), jax.ShapeDtypeStruct(stats, f32)]
        + [jax.ShapeDtypeStruct(*e) for e in extra],
        compiler_params=params(),
        cost_estimate=small_cost,
        name="forward",
    )(place, *operands, up, weight)


def backward_kernel(tokens, n, first, place_ref, *refs):
    if first:
        cots, (stats_ref, b_ref) = refs[:n], refs[n : n + 2]
        at_ref, *w_refs = refs[n + 2 : 2 * n + 3]
        own_out, other_out, scaled_ref, proj_ref = refs[2 * n + 3 :]
    else:
        scaled_ref, proj_ref, at_ref, *w_refs = refs[: n + 3]
        own_out, other_out = refs[n + 3 :]
    both = 2 * tokens
    half = w_refs[0].shape[1]
    spans = [slice(k * half, (k + 1) * half) for k in range(n)]

    if first:

        @pl.when(pl.program_id(0) == 0)
        def _():
            projected = jnp.zeros(proj_ref.shape, f32)
            for k in range(n):
                magnitude = jnp.sum(cots[k][both:, :].astype(f32), axis=0, keepdims=True)
                squares = stats_ref[pl.ds(place_ref[n + k], 1), :]
                rescale = magnitude / jnp.sqrt(squares + stability_floor)
                scaled = (cots[k][:both, :].astype(f32) * rescale).astype(bf16)
                scaled_ref[:, spans[k]] = scaled
                up = b_ref[:, pl.ds(pl.multiple_of(place_ref[k] * half, half), half)]
                projected = projected + dot(scaled, up, contract_trailing)
            proj_ref[...] = projected

    total = adapter_scale * dot(proj_ref[...].astype(bf16), at_ref[...])
    for k in range(n):
        total = total + dot(scaled_ref[:, spans[k]], w_refs[k][...], contract_trailing)
    own_out[...] = total[:tokens]
    other_out[...] = total[tokens:].astype(bf16)


def backward(place, start, bands, band, at, weight, half, first=None, later=None):
    n = place.shape[0] // 2
    rank, rows = at.shape
    if later is None:
        cots, stats, up = first
        both = cots[0].shape[0] - pad_rows
        operands, specs = [*cots, stats, up], [vmem()] * (n + 2)
        extra = [((both, n * half), bf16), ((both, rank), f32)]
    else:
        operands, specs, extra = later, [vmem()] * 2, []
        both = later[0].shape[0]
    tokens = both // 2
    part = lambda k: pl.BlockSpec((band, half), lambda i, p: (start + i, p[k]))
    return pl.pallas_call(
        functools.partial(backward_kernel, tokens, n, later is None),
        grid_spec=pltpu.PrefetchScalarGridSpec(
            num_scalar_prefetch=1,
            grid=(bands,),
            in_specs=specs
            + [pl.BlockSpec((rank, band), lambda i, p: (0, start + i))]
            + [part(k) for k in range(n)],
            out_specs=[pl.BlockSpec((tokens, band), lambda i, p: (0, i))] * 2 + [vmem()] * len(extra),
        ),
        out_shape=[
            jax.ShapeDtypeStruct((tokens, bands * band), f32),
            jax.ShapeDtypeStruct((tokens, bands * band), bf16),
        ]
        + [jax.ShapeDtypeStruct(*e) for e in extra],
        compiler_params=params(),
        cost_estimate=small_cost,
        name="backward",
    )(place, *operands, at, *[weight] * n)


def split_columns(hidden, weight, down, up, magnitude, cotangent):
    n, bits = 8, 3
    tokens = hidden.shape[0]
    half = magnitude.shape[0] // 2
    rows = weight.shape[0]
    me, core = lax.axis_index("tensor"), lax.axis_index("dp")
    swap = lambda x: lax.ppermute(x, "dp", [(0, 1), (1, 0)])
    orders = [[1, 2, 4], [2, 1, 4]]

    def send(x, k):
        pairs = [(2 * t + c, 2 * (t ^ orders[c][k]) + c) for t in range(n) for c in range(2)]
        return lax.ppermute(x, ("tensor", "dp"), pairs)

    def reach(v, c):
        return sum(orders[c][k] for k in range(bits) if v >> (bits - 1 - k) & 1)

    def place(*vs):
        shard = [me ^ jnp.where(core == 0, reach(v, 0), reach(v, 1)) for v in vs]
        return jnp.stack([2 * s + core for s in shard] + shard).astype(jnp.int32)

    mine = lambda x, axis: lax.dynamic_slice_in_dim(x, core * half, half, axis)
    at = down.T
    tie = lax.optimization_barrier

    cot_other = swap(cotangent)
    hidden_other = swap(hidden)
    first = lax.reduce_precision(magnitude, 8, 7)
    second = lax.reduce_precision(magnitude - first, 8, 7)
    third = magnitude - first - second
    magnitude_rows = jnp.concatenate(
        [jnp.stack([first, second, third]), jnp.zeros((pad_rows - 3, 2 * half), f32)]
    ).astype(bf16)
    block = own_block(core.astype(jnp.int32).reshape(1), cotangent, cot_other, magnitude_rows)

    cots = {0b000: block, 0b001: send(block, 2), 0b010: send(block, 1), 0b100: send(block, 0)}
    run = functools.partial(forward, n, weight=weight, up=up, half=half)

    far1, stats, lhs, adapter = run(place(0b110, 0b111), first=(hidden, hidden_other, at))
    from1 = send(far1, 0)
    far0, stats = run(place(0b100, 0b101), later=(lhs, adapter, stats))
    from0 = send(far0, 0)
    *got, stats = tie((*(cots[v] for v in (0b001, 0b010, 0b100)), stats))
    cots[0b001], cots[0b010], cots[0b100] = got
    cots[0b011], cots[0b101], cots[0b110] = send(cots[0b001], 1), send(cots[0b001], 0), send(cots[0b010], 0)
    near1, stats = run(place(0b010, 0b011), later=(lhs, adapter, stats))
    cots[0b011], from1, stats = tie((cots[0b011], from1, stats))
    cots[0b111] = send(cots[0b011], 0)
    sent = (near1.astype(f32) + from1.astype(f32)).astype(bf16)
    arrived = send(sent, 1)
    near0, stats = run(place(0b000, 0b001), later=(lhs, adapter, stats))
    cots[0b101], cots[0b110], from0, stats = tie((cots[0b101], cots[0b110], from0, stats))

    stats = stats + send(stats, 0)
    stats = stats + send(stats, 1)
    arrived, cots[0b111], stats = tie((arrived, cots[0b111], stats))
    kept = near0.astype(f32) + from0.astype(f32) + arrived.astype(f32)
    last = send(kept[1].astype(bf16), 2)
    stats = stats + send(stats, 2)
    lowrank_rows = stats[n:]
    lowrank_other = swap(lowrank_rows)

    band = 256
    bands = rows // band
    many = (bands + 2) // 2
    order = place(*range(n))
    grad_a, other_a, scaled, proj = backward(
        order, 0, many, band, at, weight, half, first=([cots[v] for v in range(n)], stats, up)
    )
    got_a = swap(other_a)
    last, proj = tie((last, proj))
    unscaled = kept[0] + last.astype(f32)
    grad_b, other_b = backward(order, many, bands - many, band, at, weight, half, later=(scaled, proj))
    got_b = swap(other_b)
    hidden_gradient = jnp.concatenate(
        [(own + got.astype(f32)).astype(bf16) for own, got in ((grad_a, got_a), (grad_b, got_b))], axis=1
    )
    from_sibling = swap(proj)
    proj_own = (proj[:tokens] + from_sibling[tokens:]).astype(bf16)
    proj_other = (proj[tokens:] + from_sibling[:tokens]).astype(bf16)
    down_weight_gradient = adapter_scale * (
        dot(proj_own, hidden, contract_first) + dot(proj_other, hidden_other, contract_first)
    ).T

    norm = jnp.sqrt(lax.dynamic_slice_in_dim(stats, me, 1, 0)[0] + stability_floor)
    rescale = mine(magnitude, 0) / norm
    upstream = block[: 2 * tokens].astype(f32)
    scaled_own = (upstream * rescale).astype(bf16).astype(f32)

    def turned(part):
        lanes = half // tokens
        return jnp.concatenate([part[:, j * tokens : (j + 1) * tokens] for j in range(lanes)])

    up_half = adapter_scale * (
        jnp.dot(turned(lowrank_rows), scaled_own[:tokens], precision=lax.Precision.HIGHEST)
        + jnp.dot(turned(lowrank_other), scaled_own[tokens:], precision=lax.Precision.HIGHEST)
    )
    mixed = (unscaled * rescale).astype(bf16)
    magnitude_half = jnp.sum(upstream * unscaled, axis=0) / norm

    def join(own, other, axis):
        pair = jnp.concatenate([own, other, own], axis)
        return lax.dynamic_slice_in_dim(pair, core * half, 2 * half, axis)

    mixed = join(mixed[:tokens], swap(mixed[tokens:]), 1)
    up_weight_gradient = join(up_half, swap(up_half), 1)
    grad_magnitude = join(magnitude_half, swap(magnitude_half), 0)
    return (mixed, hidden_gradient, down_weight_gradient, up_weight_gradient, grad_magnitude)


def by_tokens(hidden, frozen_down_weight, adapter_down_weight, adapter_up_weight, magnitude, cotangent):
    column_slice = magnitude.shape[0]
    block_offset = lax.axis_index("tensor") * column_slice
    combined_weight = frozen_down_weight.astype(f32) + adapter_scale * dot(adapter_down_weight, adapter_up_weight)
    squares_part = jnp.sum(combined_weight * combined_weight, axis=0)
    squares, reduced_rank_product = lax.psum((squares_part, dot(hidden, adapter_down_weight)), "tensor")
    norm_all = jnp.sqrt(squares + stability_floor)
    column_length_norm = lax.dynamic_slice_in_dim(norm_all, block_offset, column_slice)
    up_weight_columns = lax.dynamic_slice_in_dim(adapter_up_weight, block_offset, column_slice, 1)
    summed_output = lax.psum_scatter(dot(hidden, frozen_down_weight), "tensor", scatter_dimension=1, tiled=True)
    unscaled_output = summed_output + adapter_scale * jnp.dot(
        reduced_rank_product, up_weight_columns.astype(f32), precision=lax.Precision.HIGHEST
    )
    rescale = magnitude / column_length_norm
    mixed = (unscaled_output * rescale).astype(bf16)
    upstream = cotangent.astype(f32)
    scaled_output = (upstream * rescale).astype(bf16)
    magnitude_part = jnp.sum(upstream * unscaled_output, axis=0) / column_length_norm
    block_input = lax.all_gather(scaled_output, "tensor", axis=1, tiled=True)
    projected_output = dot(block_input, adapter_up_weight, contract_trailing).astype(bf16)
    hidden_gradient = dot(block_input, frozen_down_weight, contract_trailing)
    hidden_gradient = hidden_gradient + adapter_scale * dot(projected_output, adapter_down_weight, contract_trailing)
    hidden_gradient = hidden_gradient.astype(bf16)
    down_gradient_piece = adapter_scale * dot(hidden, projected_output, contract_first)
    up_gradient_piece = adapter_scale * lax.dot_general(
        reduced_rank_product, scaled_output.astype(f32), contract_first, precision=lax.Precision.HIGHEST
    )
    pieces = (down_gradient_piece, up_gradient_piece, magnitude_part)
    pieces = [lax.psum(p.astype(bf16), "dp").astype(f32) for p in pieces]
    return (mixed, hidden_gradient, *pieces)


def solution(mesh):
    n = mesh.shape["tensor"]

    def local(hidden, weight, down, up, magnitude, cotangent):
        aligned = magnitude.shape[0] % 256 == 0 and weight.shape[0] % 256 == 0 and hidden.shape[0] % 128 == 0
        if aligned and mesh.shape["dp"] == 2 and n == 8 and down.shape[1] * hidden.shape[0] % (magnitude.shape[0] // 2 * 8) == 0:
            return split_columns(hidden, weight, down, up, magnitude, cotangent)
        return by_tokens(hidden, weight, down, up, magnitude, cotangent)

    in_specs = (
        P(("parts", "dp"), "tensor"),
        P("tensor", None),
        P(("parts", "tensor"), None),
        P("parts", None),
        P(("parts", "tensor")),
        P(("parts", "dp"), "tensor"),
    )
    out_specs = (
        P(("parts", "dp"), "tensor"),
        P(("parts", "dp"), "tensor"),
        P(("parts", "tensor"), None),
        P("parts", "tensor"),
        P(("parts", "tensor")),
    )
    return jax.shard_map(local, mesh=mesh, in_specs=in_specs, out_specs=out_specs, check_vma=False)
```

```python
import functools

import jax
import jax.numpy as jnp
from jax import lax
from jax.experimental import pallas as pl
from jax.experimental.pallas import tpu as pltpu
from jax.sharding import PartitionSpec as P

adapter_scale = 2.0
stability_floor = 1e-06
pad_rows = 16
vmem_bytes = 5 * 1024 * 1024
f32, bf16 = jnp.float32, jnp.bfloat16
small_cost = pl.CostEstimate(flops=1 << 20, bytes_accessed=1 << 20, transcendentals=0)
contract_trailing = (((1,), (1,)), ((), ()))
contract_first = (((0,), (0,)), ((), ()))


def dot(a, b, dims=(((1,), (0,)), ((), ()))):
    return lax.dot_general(a, b, dims, preferred_element_type=f32)


def split_pair(x):
    high = x.astype(bf16)
    return high, (x - high.astype(f32)).astype(bf16)


def sum_of_squares(w_ref):
    rows, width = w_ref.shape
    totals = [jnp.zeros((8, width), f32) for _ in range(2)]
    for i in range(rows // 16):
        w = w_ref[i * 16 : (i + 1) * 16, :].astype(f32)
        w = w * w
        totals[0] = totals[0] + w[:8]
        totals[1] = totals[1] + w[8:]
    return jnp.sum(totals[0] + totals[1], axis=0, keepdims=True)


def vmem():
    return pl.BlockSpec(memory_space=pltpu.VMEM)


def params():
    return pltpu.CompilerParams(vmem_limit_bytes=vmem_bytes)


def block_kernel(tokens, core_ref, own_ref, other_ref, magnitude_ref, out_ref):
    out_ref[:tokens, :] = own_ref[...]
    out_ref[tokens : 2 * tokens, :] = other_ref[...]
    out_ref[2 * tokens :, :] = magnitude_ref[...]


def own_block(core, cotangent, other, magnitude_rows):
    tokens, columns = cotangent.shape
    half = columns // 2
    padded = 2 * tokens + pad_rows
    return pl.pallas_call(
        functools.partial(block_kernel, tokens),
        grid_spec=pltpu.PrefetchScalarGridSpec(
            num_scalar_prefetch=1,
            grid=(1,),
            in_specs=[
                pl.BlockSpec((tokens, half), lambda i, c: (0, c[0])),
                pl.BlockSpec((tokens, half), lambda i, c: (0, c[0])),
                pl.BlockSpec((pad_rows, half), lambda i, c: (0, c[0])),
            ],
            out_specs=pl.BlockSpec((padded, half), lambda i, c: (0, 0)),
        ),
        out_shape=jax.ShapeDtypeStruct((padded, half), bf16),
        cost_estimate=small_cost,
        name="own_block",
    )(core, cotangent, other, magnitude_rows)


def load_kernel(tokens, rank, n, first, place_ref, *refs):
    if first:
        own_ref, at_ref, up_ref, w_hbm, *held, stats_ref, own_out, sem, own_sem = refs
    else:
        before_ref, at_ref, up_ref, w_hbm, *held, stats_ref, sem = refs
    blocks, half = len(held), held[0].shape[1]
    column = lambda k: pl.ds(pl.multiple_of(place_ref[k] * half, half), half)
    copy = lambda k: pltpu.make_async_copy(w_hbm.at[:, column(k)], held[k], sem.at[k])
    if first:
        own_copy = pltpu.make_async_copy(own_ref, own_out, own_sem)
        own_copy.start()
    for k in range(blocks):
        copy(k).start()

    down = at_ref[...]
    high, low = split_pair(dot(down, down, contract_trailing))
    if first:
        own_copy.wait()
        turned = dot(down, own_out[...], contract_trailing)
        lanes = half // tokens
        span = rank // lanes
        stats_ref[:n, :] = jnp.zeros((n, half), f32)
        for j in range(lanes):
            stats_ref[n:, j * tokens : (j + 1) * tokens] = turned[j * span : (j + 1) * span]
    else:
        stats_ref[...] = before_ref[...]

    for k in range(blocks):
        copy(k).wait()
        up = up_ref[:, column(k)]
        cross = 2 * dot(down, held[k][...]) + adapter_scale * (dot(high, up) + dot(low, up))
        cross = jnp.sum(up.astype(f32) * cross, axis=0, keepdims=True)
        stats_ref[pl.ds(place_ref[blocks + k], 1), :] = sum_of_squares(held[k]) + adapter_scale * cross


def load(n, place, weight, at, up, half, own=None, before=None):
    blocks = place.shape[0] // 2
    rows = weight.shape[0]
    rank = at.shape[0]
    any_ = pl.BlockSpec(memory_space=pl.ANY)
    first = before is None
    if first:
        tokens = own.shape[0]
        stats = (n + rank * tokens // half, half)
    else:
        tokens, stats = None, before.shape
    return pl.pallas_call(
        functools.partial(load_kernel, tokens, rank, n, first),
        in_specs=[pl.BlockSpec(memory_space=pltpu.SMEM), any_ if first else vmem(), vmem(), vmem(), any_],
        out_specs=[vmem()] * (blocks + (2 if first else 1)),
        out_shape=[jax.ShapeDtypeStruct((rows, half), bf16)] * blocks
        + [jax.ShapeDtypeStruct(stats, f32)]
        + ([jax.ShapeDtypeStruct(own.shape, bf16)] if first else []),
        scratch_shapes=[pltpu.SemaphoreType.DMA((blocks,))] + ([pltpu.SemaphoreType.DMA] if first else []),
        compiler_params=params(),
        cost_estimate=small_cost,
        name="load",
    )(place, own if first else before, at, up, weight)


def forward_kernel(tokens, rank, blocks, first, place_ref, *refs):
    if first:
        own_ref, other_ref, at_ref, up_ref, *held, out_ref, lhs_ref, adapter_ref, sem = refs
        copy = pltpu.make_async_copy(other_ref, lhs_ref.at[tokens:], sem)
        copy.start()
        lhs_ref[:tokens, :] = own_ref[...]
        copy.wait()
        high, low = split_pair(dot(lhs_ref[...], at_ref[...], contract_trailing))
        adapter_ref[:, :rank] = high
        adapter_ref[:, rank:] = low
    else:
        lhs_ref, adapter_ref, up_ref, *held, out_ref = refs
    half = out_ref.shape[2]
    for i in range(blocks):
        up = up_ref[:, pl.ds(pl.multiple_of(place_ref[i] * half, half), half)]
        through = dot(adapter_ref[...], jnp.concatenate([up, up], axis=0))
        out_ref[i] = (dot(lhs_ref[...], held[i][...]) + adapter_scale * through).astype(bf16)


def forward(place, held, up, first=None, later=None):
    rows, half = held[0].shape
    if later is None:
        own, other, at = operands = first
        tokens, rank = own.shape[0], at.shape[0]
        specs = [vmem(), pl.BlockSpec(memory_space=pl.ANY), vmem()]
    else:
        lhs, adapter = operands = later
        rank, tokens = adapter.shape[1] // 2, lhs.shape[0] // 2
        specs = [vmem()] * 2
    extra = [((2 * tokens, rows), bf16), ((2 * tokens, 2 * rank), bf16)] if first else []
    return pl.pallas_call(
        functools.partial(forward_kernel, tokens, rank, len(held), later is None),
        in_specs=[pl.BlockSpec(memory_space=pltpu.SMEM), *specs] + [vmem()] * (1 + len(held)),
        out_specs=[vmem()] * (1 + len(extra)),
        out_shape=[jax.ShapeDtypeStruct((len(held), 2 * tokens, half), bf16)]
        + [jax.ShapeDtypeStruct(*e) for e in extra],
        scratch_shapes=[pltpu.SemaphoreType.DMA] if first else [],
        compiler_params=params(),
        cost_estimate=small_cost,
        name="forward",
    )(place, *operands, up, *held)


def backward_kernel(tokens, n, start, band, first, place_ref, *refs):
    if first:
        cots, (stats_ref, up_ref, at_ref, *held) = refs[:n], refs[n : 2 * n + 3]
        own_out, other_out, scaled_ref, proj_ref = refs[2 * n + 3 :]
    else:
        scaled_ref, proj_ref, at_ref, *held, own_out, other_out = refs
    both = 2 * tokens
    half = held[0].shape[1]
    spans = [slice(k * half, (k + 1) * half) for k in range(n)]

    if first:

        @pl.when(pl.program_id(0) == 0)
        def _():
            projected = jnp.zeros(proj_ref.shape, f32)
            for k in range(n):
                magnitude = jnp.sum(cots[k][both:, :].astype(f32), axis=0, keepdims=True)
                squares = stats_ref[pl.ds(place_ref[n + k], 1), :]
                rescale = magnitude / jnp.sqrt(squares + stability_floor)
                scaled = (cots[k][:both, :].astype(f32) * rescale).astype(bf16)
                scaled_ref[:, spans[k]] = scaled
                up = up_ref[:, pl.ds(pl.multiple_of(place_ref[k] * half, half), half)]
                projected = projected + dot(scaled, up, contract_trailing)
            proj_ref[...] = projected

    row = pl.ds(pl.multiple_of((start + pl.program_id(0)) * band, band), band)
    total = adapter_scale * dot(proj_ref[...].astype(bf16), at_ref[:, row])
    for k in range(n):
        total = total + dot(scaled_ref[:, spans[k]], held[k][row, :], contract_trailing)
    own_out[...] = total[:tokens]
    other_out[...] = total[tokens:].astype(bf16)


def backward(place, start, bands, band, at, held, first=None, later=None):
    n = place.shape[0] // 2
    half = held[0].shape[1]
    rank = at.shape[0]
    if later is None:
        cots, stats, up = first
        both = cots[0].shape[0] - pad_rows
        operands = [*cots, stats, up]
        extra = [((both, n * half), bf16), ((both, rank), f32)]
    else:
        operands, extra = later, []
        both = later[0].shape[0]
    tokens = both // 2
    return pl.pallas_call(
        functools.partial(backward_kernel, tokens, n, start, band, later is None),
        grid=(bands,),
        in_specs=[pl.BlockSpec(memory_space=pltpu.SMEM)] + [vmem()] * (len(operands) + 1 + n),
        out_specs=[pl.BlockSpec((tokens, band), lambda i: (0, i))] * 2 + [vmem()] * len(extra),
        out_shape=[
            jax.ShapeDtypeStruct((tokens, bands * band), f32),
            jax.ShapeDtypeStruct((tokens, bands * band), bf16),
        ]
        + [jax.ShapeDtypeStruct(*e) for e in extra],
        compiler_params=params(),
        cost_estimate=small_cost,
        name="backward",
    )(place, *operands, at, *held)


def split_columns(hidden, weight, down, up, magnitude, cotangent):
    n, bits = 8, 3
    tokens = hidden.shape[0]
    half = magnitude.shape[0] // 2
    rows = weight.shape[0]
    me, core = lax.axis_index("tensor"), lax.axis_index("dp")
    swap = lambda x: lax.ppermute(x, "dp", [(0, 1), (1, 0)])
    orders = [[1, 2, 4], [2, 1, 4]]

    def send(x, k):
        pairs = [(2 * t + c, 2 * (t ^ orders[c][k]) + c) for t in range(n) for c in range(2)]
        return lax.ppermute(x, ("tensor", "dp"), pairs)

    def reach(v, c):
        return sum(orders[c][k] for k in range(bits) if v >> (bits - 1 - k) & 1)

    def place(*vs):
        shard = [me ^ jnp.where(core == 0, reach(v, 0), reach(v, 1)) for v in vs]
        return jnp.stack([2 * s + core for s in shard] + shard).astype(jnp.int32)

    mine = lambda x, axis: lax.dynamic_slice_in_dim(x, core * half, half, axis)
    at = down.T
    tie = lax.optimization_barrier

    cot_other = swap(cotangent)
    hidden_other = swap(hidden)
    run_load = functools.partial(load, n, weight=weight, at=at, up=up, half=half)
    *far, stats, own = run_load(place(0b100, 0b101, 0b110, 0b111), own=hidden)
    cot_other, stats = tie((cot_other, stats))
    first = lax.reduce_precision(magnitude, 8, 7)
    second = lax.reduce_precision(magnitude - first, 8, 7)
    third = magnitude - first - second
    magnitude_rows = jnp.concatenate(
        [jnp.stack([first, second, third]), jnp.zeros((pad_rows - 3, 2 * half), f32)]
    ).astype(bf16)
    block = own_block(core.astype(jnp.int32).reshape(1), cotangent, cot_other, magnitude_rows)

    cots = {0b000: block, 0b001: send(block, 2), 0b010: send(block, 1), 0b100: send(block, 0)}
    *near, stats = run_load(place(0b000, 0b001, 0b010, 0b011), before=stats)

    got = send(stats, 0)
    far1, lhs, adapter = forward(place(0b110, 0b111), far[2:], up, first=(own, hidden_other, at))
    run = functools.partial(forward, up=up, later=(lhs, adapter))
    got, far1 = tie((got, far1))
    stats = stats + got
    got = send(stats, 1)
    from1 = send(far1, 0)
    far0 = run(place(0b100, 0b101), far[:2])[0]
    *arrived, got, far0 = tie((*(cots[v] for v in (0b001, 0b010, 0b100)), got, far0))
    cots[0b001], cots[0b010], cots[0b100] = arrived
    stats = stats + got
    got = send(stats, 2)
    from0 = send(far0, 0)
    cots[0b011], cots[0b101], cots[0b110] = send(cots[0b001], 1), send(cots[0b001], 0), send(cots[0b010], 0)
    near1 = run(place(0b010, 0b011), near[2:])[0]
    cots[0b011], from1, got, near1 = tie((cots[0b011], from1, got, near1))
    stats = stats + got
    cots[0b111] = send(cots[0b011], 0)
    arrived = send((near1.astype(f32) + from1.astype(f32)).astype(bf16), 1)
    near0 = run(place(0b000, 0b001), near[:2])[0]
    cots[0b101], cots[0b110], cots[0b111], from0, near0, arrived, stats = tie(
        (cots[0b101], cots[0b110], cots[0b111], from0, near0, arrived, stats)
    )
    kept = near0.astype(f32) + from0.astype(f32) + arrived.astype(f32)
    last = send(kept[1].astype(bf16), 2)
    lowrank_rows = stats[n:]
    lowrank_other = swap(lowrank_rows)

    band = 256
    bands = rows // band
    many = (bands + 2) // 2
    order = place(*range(n))
    run = functools.partial(backward, order, band=band, at=at, held=near + far)
    grad_a, other_a, scaled, proj = run(0, many, first=([cots[v] for v in range(n)], stats, up))
    got_a = swap(other_a)
    last, proj = tie((last, proj))
    unscaled = kept[0] + last.astype(f32)
    grad_b, other_b = run(many, bands - many, later=(scaled, proj))
    got_b = swap(other_b)
    hidden_gradient = jnp.concatenate(
        [(own + got.astype(f32)).astype(bf16) for own, got in ((grad_a, got_a), (grad_b, got_b))], axis=1
    )
    from_sibling = swap(proj)
    proj_own = (proj[:tokens] + from_sibling[tokens:]).astype(bf16)
    proj_other = (proj[tokens:] + from_sibling[:tokens]).astype(bf16)
    down_weight_gradient = adapter_scale * (
        dot(proj_own, hidden, contract_first) + dot(proj_other, hidden_other, contract_first)
    ).T

    norm = jnp.sqrt(lax.dynamic_slice_in_dim(stats, me, 1, 0)[0] + stability_floor)
    rescale = mine(magnitude, 0) / norm
    upstream = block[: 2 * tokens].astype(f32)
    scaled_own = (upstream * rescale).astype(bf16).astype(f32)

    def turned(part):
        lanes = half // tokens
        return jnp.concatenate([part[:, j * tokens : (j + 1) * tokens] for j in range(lanes)])

    up_half = adapter_scale * (
        jnp.dot(turned(lowrank_rows), scaled_own[:tokens], precision=lax.Precision.HIGHEST)
        + jnp.dot(turned(lowrank_other), scaled_own[tokens:], precision=lax.Precision.HIGHEST)
    )
    mixed = (unscaled * rescale).astype(bf16)
    magnitude_half = jnp.sum(upstream * unscaled, axis=0) / norm

    def join(own, other, axis):
        pair = jnp.concatenate([own, other, own], axis)
        return lax.dynamic_slice_in_dim(pair, core * half, 2 * half, axis)

    mixed = join(mixed[:tokens], swap(mixed[tokens:]), 1)
    up_weight_gradient = join(up_half, swap(up_half), 1)
    grad_magnitude = join(magnitude_half, swap(magnitude_half), 0)
    return (mixed, hidden_gradient, down_weight_gradient, up_weight_gradient, grad_magnitude)


def by_tokens(hidden, frozen_down_weight, adapter_down_weight, adapter_up_weight, magnitude, cotangent):
    column_slice = magnitude.shape[0]
    block_offset = lax.axis_index("tensor") * column_slice
    combined_weight = frozen_down_weight.astype(f32) + adapter_scale * dot(adapter_down_weight, adapter_up_weight)
    squares_part = jnp.sum(combined_weight * combined_weight, axis=0)
    squares, reduced_rank_product = lax.psum((squares_part, dot(hidden, adapter_down_weight)), "tensor")
    norm_all = jnp.sqrt(squares + stability_floor)
    column_length_norm = lax.dynamic_slice_in_dim(norm_all, block_offset, column_slice)
    up_weight_columns = lax.dynamic_slice_in_dim(adapter_up_weight, block_offset, column_slice, 1)
    summed_output = lax.psum_scatter(dot(hidden, frozen_down_weight), "tensor", scatter_dimension=1, tiled=True)
    unscaled_output = summed_output + adapter_scale * jnp.dot(
        reduced_rank_product, up_weight_columns.astype(f32), precision=lax.Precision.HIGHEST
    )
    rescale = magnitude / column_length_norm
    mixed = (unscaled_output * rescale).astype(bf16)
    upstream = cotangent.astype(f32)
    scaled_output = (upstream * rescale).astype(bf16)
    magnitude_part = jnp.sum(upstream * unscaled_output, axis=0) / column_length_norm
    block_input = lax.all_gather(scaled_output, "tensor", axis=1, tiled=True)
    projected_output = dot(block_input, adapter_up_weight, contract_trailing).astype(bf16)
    hidden_gradient = dot(block_input, frozen_down_weight, contract_trailing)
    hidden_gradient = hidden_gradient + adapter_scale * dot(projected_output, adapter_down_weight, contract_trailing)
    hidden_gradient = hidden_gradient.astype(bf16)
    down_gradient_piece = adapter_scale * dot(hidden, projected_output, contract_first)
    up_gradient_piece = adapter_scale * lax.dot_general(
        reduced_rank_product, scaled_output.astype(f32), contract_first, precision=lax.Precision.HIGHEST
    )
    pieces = (down_gradient_piece, up_gradient_piece, magnitude_part)
    pieces = [lax.psum(p.astype(bf16), "dp").astype(f32) for p in pieces]
    return (mixed, hidden_gradient, *pieces)


def solution(mesh):
    n = mesh.shape["tensor"]

    def local(hidden, weight, down, up, magnitude, cotangent):
        aligned = magnitude.shape[0] % 256 == 0 and weight.shape[0] % 256 == 0 and hidden.shape[0] % 128 == 0
        if aligned and mesh.shape["dp"] == 2 and n == 8 and down.shape[1] * hidden.shape[0] % (magnitude.shape[0] // 2 * 8) == 0:
            return split_columns(hidden, weight, down, up, magnitude, cotangent)
        return by_tokens(hidden, weight, down, up, magnitude, cotangent)

    in_specs = (
        P(("parts", "dp"), "tensor"),
        P("tensor", None),
        P(("parts", "tensor"), None),
        P("parts", None),
        P(("parts", "tensor")),
        P(("parts", "dp"), "tensor"),
    )
    out_specs = (
        P(("parts", "dp"), "tensor"),
        P(("parts", "dp"), "tensor"),
        P(("parts", "tensor"), None),
        P("parts", "tensor"),
        P(("parts", "tensor")),
    )
    return jax.shard_map(local, mesh=mesh, in_specs=in_specs, out_specs=out_specs, check_vma=False)
```

```python
import functools

import jax
import jax.numpy as jnp
from jax import lax
from jax.experimental import pallas as pl
from jax.experimental.pallas import tpu as pltpu
from jax.sharding import PartitionSpec as P

adapter_scale = 2.0
stability_floor = 1e-06
pad_rows = 16
vmem_bytes = 10 * 1024 * 1024
f32, bf16 = jnp.float32, jnp.bfloat16
small_cost = pl.CostEstimate(flops=1 << 20, bytes_accessed=1 << 20, transcendentals=0)
contract_trailing = (((1,), (1,)), ((), ()))
contract_first = (((0,), (0,)), ((), ()))


def dot(a, b, dims=(((1,), (0,)), ((), ()))):
    return lax.dot_general(a, b, dims, preferred_element_type=f32)


def split_pair(x):
    high = x.astype(bf16)
    return high, (x - high.astype(f32)).astype(bf16)


def sum_of_squares(w_ref):
    rows, width = w_ref.shape
    totals = [jnp.zeros((8, width), f32) for _ in range(2)]
    for i in range(rows // 16):
        w = w_ref[i * 16 : (i + 1) * 16, :].astype(f32)
        w = w * w
        totals[0] = totals[0] + w[:8]
        totals[1] = totals[1] + w[8:]
    return jnp.sum(totals[0] + totals[1], axis=0, keepdims=True)


def vmem():
    return pl.BlockSpec(memory_space=pltpu.VMEM)


def anywhere():
    return pl.BlockSpec(memory_space=pl.ANY)


def params(size=vmem_bytes):
    return pltpu.CompilerParams(vmem_limit_bytes=size)


def block_kernel(tokens, core_ref, own_ref, other_ref, magnitude_ref, out_ref):
    out_ref[:tokens, :] = own_ref[...]
    out_ref[tokens : 2 * tokens, :] = other_ref[...]
    out_ref[2 * tokens :, :] = magnitude_ref[...]


def own_block(core, cotangent, other, magnitude_rows):
    tokens, columns = cotangent.shape
    half = columns // 2
    padded = 2 * tokens + pad_rows
    return pl.pallas_call(
        functools.partial(block_kernel, tokens),
        grid_spec=pltpu.PrefetchScalarGridSpec(
            num_scalar_prefetch=1,
            grid=(1,),
            in_specs=[
                pl.BlockSpec((tokens, half), lambda i, c: (0, c[0])),
                pl.BlockSpec((tokens, half), lambda i, c: (0, c[0])),
                pl.BlockSpec((pad_rows, half), lambda i, c: (0, c[0])),
            ],
            out_specs=pl.BlockSpec((padded, half), lambda i, c: (0, 0)),
        ),
        out_shape=jax.ShapeDtypeStruct((padded, half), bf16),
        compiler_params=params(),
        cost_estimate=small_cost,
        name="own_block",
    )(core, cotangent, other, magnitude_rows)


def block_copies(place_ref, w_hbm, held, sem):
    half = held[0].shape[1] if held else 0
    columns = [pl.ds(pl.multiple_of(place_ref[k] * half, half), half) for k in range(len(held))]
    return [pltpu.make_async_copy(w_hbm.at[:, c], h, sem.at[k]) for k, (c, h) in enumerate(zip(columns, held))]


def load_kernel(blocks, place_ref, w_hbm, *refs):
    count = (len(refs) - 1 - blocks) // 2
    whole = refs[:count]
    held, outs, sem = refs[count : count + blocks], refs[count + blocks : -1], refs[-1]
    copies = [pltpu.make_async_copy(x, o, sem.at[blocks + i]) for i, (x, o) in enumerate(zip(whole, outs))]
    copies = block_copies(place_ref, w_hbm, held, sem) + copies
    for copy in copies:
        copy.start()
    for copy in copies:
        copy.wait()


def load(place, weight, half, whole=(), size=vmem_bytes):
    blocks = place.shape[0] // 2
    return pl.pallas_call(
        functools.partial(load_kernel, blocks),
        in_specs=[pl.BlockSpec(memory_space=pltpu.SMEM)] + [anywhere()] * (1 + len(whole)),
        out_specs=[vmem()] * (blocks + len(whole)),
        out_shape=[jax.ShapeDtypeStruct((weight.shape[0], half), bf16)] * blocks
        + [jax.ShapeDtypeStruct(x.shape, x.dtype) for x in whole],
        scratch_shapes=[pltpu.SemaphoreType.DMA((blocks + len(whole),))],
        compiler_params=params(size),
        cost_estimate=small_cost,
        name="load",
    )(place, weight, *whole)


def forward_kernel(tokens, rank, n, blocks, first, place_ref, next_ref, w_hbm, up_ref, *refs):
    held, refs = refs[:blocks], refs[blocks:]
    if first:
        own_ref, other_ref, at_ref, out_ref, stats_ref, *ahead, lhs_ref, adapter_ref, sem, other_sem = refs
    else:
        lhs_ref, adapter_ref, before_ref, out_ref, stats_ref, *ahead, sem = refs
    both = 2 * tokens
    half = out_ref.shape[2]
    copies = block_copies(next_ref, w_hbm, ahead, sem)
    if first:
        other_copy = pltpu.make_async_copy(other_ref, lhs_ref.at[tokens:both], other_sem)
        other_copy.start()
    for copy in copies:
        copy.start()
    if first:
        lhs_ref[:tokens, :] = own_ref[...]
        lhs_ref[both:, :] = at_ref[...]
        other_copy.wait()
        lowrank = dot(lhs_ref[...], at_ref[...], contract_trailing)
        high, low = split_pair(lowrank)
        adapter_ref[:, :rank] = high
        adapter_ref[:, rank:] = low
        turned = lowrank[:tokens].T
        lanes = half // tokens
        span = rank // lanes
        stats_ref[:n, :] = jnp.zeros((n, half), f32)
        for j in range(lanes):
            stats_ref[n:, j * tokens : (j + 1) * tokens] = turned[j * span : (j + 1) * span]
    else:
        stats_ref[...] = before_ref[...]
    for k in range(blocks):
        up = up_ref[:, pl.ds(pl.multiple_of(place_ref[k] * half, half), half)]
        through = adapter_scale * dot(adapter_ref[...], jnp.concatenate([up, up], axis=0))
        product = dot(lhs_ref[...], held[k][...])
        out_ref[k] = (product[:both] + through[:both]).astype(bf16)
        cross = 2 * adapter_scale * product[both:] + adapter_scale * through[both:]
        cross = jnp.sum(up.astype(f32) * cross, axis=0, keepdims=True)
        stats_ref[pl.ds(place_ref[blocks + k], 1), :] = sum_of_squares(held[k]) + cross
    for copy in copies:
        copy.wait()


def forward(n, place, following, held, weight, up, first=None, later=None):
    blocks = len(held)
    rows, half = held[0].shape
    if later is None:
        own, other, at = operands = first
        tokens, rank = own.shape[0], at.shape[0]
        specs = [vmem(), anywhere(), vmem()]
    else:
        lhs, adapter, before = operands = later
        rank = adapter.shape[1] // 2
        tokens = (lhs.shape[0] - rank) // 2
        specs = [vmem()] * 3
    stats = (n + rank * tokens // half, half)
    extra = [((2 * tokens + rank, rows), bf16), ((2 * tokens + rank, 2 * rank), bf16)] if first else []
    ahead = 0 if following is None else blocks
    smem = pl.BlockSpec(memory_space=pltpu.SMEM)
    return pl.pallas_call(
        functools.partial(forward_kernel, tokens, rank, n, blocks, later is None),
        in_specs=[smem, smem, anywhere(), vmem()] + [vmem()] * blocks + specs,
        out_specs=[vmem()] * (2 + ahead + len(extra)),
        out_shape=[jax.ShapeDtypeStruct((blocks, 2 * tokens, half), bf16), jax.ShapeDtypeStruct(stats, f32)]
        + [jax.ShapeDtypeStruct((rows, half), bf16)] * ahead
        + [jax.ShapeDtypeStruct(*e) for e in extra],
        scratch_shapes=[pltpu.SemaphoreType.DMA((blocks,))] + ([pltpu.SemaphoreType.DMA] if first else []),
        compiler_params=params(),
        cost_estimate=small_cost,
        name="forward",
    )(place, place if following is None else following, weight, up, *held, *operands)


def backward_kernel(tokens, n, start, band, first, place_ref, *refs):
    if first:
        cots, (stats_ref, up_ref, at_ref, *w_refs) = refs[:n], refs[n : 2 * n + 3]
        own_out, other_out, scaled_ref, proj_ref = refs[2 * n + 3 :]
    else:
        scaled_ref, proj_ref, at_ref, *w_refs, own_out, other_out = refs
    both = 2 * tokens
    half = w_refs[0].shape[1]
    spans = [slice(k * half, (k + 1) * half) for k in range(n)]

    if first:

        @pl.when(pl.program_id(0) == 0)
        def _():
            projected = jnp.zeros(proj_ref.shape, f32)
            for k in range(n):
                magnitude = jnp.sum(cots[k][both:, :].astype(f32), axis=0, keepdims=True)
                squares = stats_ref[pl.ds(place_ref[n + k], 1), :]
                rescale = magnitude / jnp.sqrt(squares + stability_floor)
                scaled = (cots[k][:both, :].astype(f32) * rescale).astype(bf16)
                scaled_ref[:, spans[k]] = scaled
                up = up_ref[:, pl.ds(pl.multiple_of(place_ref[k] * half, half), half)]
                projected = projected + dot(scaled, up, contract_trailing)
            proj_ref[...] = projected

    row = pl.ds(pl.multiple_of((start + pl.program_id(0)) * band, band), band)
    total = adapter_scale * dot(proj_ref[...].astype(bf16), at_ref[:, row])
    for k in range(n):
        band_ref = w_refs[k] if w_refs[k].shape[0] == band else w_refs[k].at[row]
        total = total + dot(scaled_ref[:, spans[k]], band_ref[...], contract_trailing)
    own_out[...] = total[:tokens]
    other_out[...] = total[tokens:].astype(bf16)


def backward(place, start, bands, band, at, held, weight, first=None, later=None):
    n = place.shape[0] // 2
    half = held[0].shape[1]
    rank = at.shape[0]
    if later is None:
        cots, stats, up = first
        both = cots[0].shape[0] - pad_rows
        operands = [*cots, stats, up]
        extra = [((both, n * half), bf16), ((both, rank), f32)]
    else:
        operands, extra = later, []
        both = later[0].shape[0]
    tokens = both // 2
    part = lambda k: pl.BlockSpec((band, half), lambda i, p: (start + i, p[k]))
    streamed = range(len(held), n)
    return pl.pallas_call(
        functools.partial(backward_kernel, tokens, n, start, band, later is None),
        grid_spec=pltpu.PrefetchScalarGridSpec(
            num_scalar_prefetch=1,
            grid=(bands,),
            in_specs=[vmem()] * (len(operands) + 1 + len(held)) + [part(k) for k in streamed],
            out_specs=[pl.BlockSpec((tokens, band), lambda i, p: (0, i))] * 2 + [vmem()] * len(extra),
        ),
        out_shape=[
            jax.ShapeDtypeStruct((tokens, bands * band), f32),
            jax.ShapeDtypeStruct((tokens, bands * band), bf16),
        ]
        + [jax.ShapeDtypeStruct(*e) for e in extra],
        compiler_params=params(),
        cost_estimate=small_cost,
        name="backward",
    )(place, *operands, at, *held, *[weight] * len(streamed))


def split_columns(hidden, weight, down, up, magnitude, cotangent):
    n, bits = 8, 3
    tokens = hidden.shape[0]
    half = magnitude.shape[0] // 2
    rows = weight.shape[0]
    me, core = lax.axis_index("tensor"), lax.axis_index("dp")
    swap = lambda x: lax.ppermute(x, "dp", [(0, 1), (1, 0)])
    orders = [[1, 2, 4], [2, 1, 4]]

    def send(x, k):
        pairs = [(2 * t + c, 2 * (t ^ orders[c][k]) + c) for t in range(n) for c in range(2)]
        return lax.ppermute(x, ("tensor", "dp"), pairs)

    def reach(v, c):
        return sum(orders[c][k] for k in range(bits) if v >> (bits - 1 - k) & 1)

    def place(*vs):
        shard = [me ^ jnp.where(core == 0, reach(v, 0), reach(v, 1)) for v in vs]
        return jnp.stack([2 * s + core for s in shard] + shard).astype(jnp.int32)

    mine = lambda x, axis: lax.dynamic_slice_in_dim(x, core * half, half, axis)
    tie = lax.optimization_barrier

    cot_other = swap(cotangent)
    hidden_other = swap(hidden)
    pieces = [(0b110, 0b111), (0b100, 0b101), (0b010, 0b011), (0b000, 0b001)]
    places = [place(*vs) for vs in pieces]
    ahead, at = list(load(places[0], weight, half)), down.T
    cot_other, ahead[0] = tie((cot_other, ahead[0]))
    first = lax.reduce_precision(magnitude, 8, 7)
    second = lax.reduce_precision(magnitude - first, 8, 7)
    third = magnitude - first - second
    magnitude_rows = jnp.concatenate(
        [jnp.stack([first, second, third]), jnp.zeros((pad_rows - 3, 2 * half), f32)]
    ).astype(bf16)
    block = own_block(core.astype(jnp.int32).reshape(1), cotangent, cot_other, magnitude_rows)

    cots = {0b000: block, 0b001: send(block, 2), 0b010: send(block, 1), 0b100: send(block, 0)}

    run = lambda i, *rest, **more: forward(n, places[i], *rest, weight=weight, up=up, **more)
    far1, stats, *ahead, lhs, adapter = run(0, places[1], ahead, first=(hidden, hidden_other, at))
    from1 = send(far1, 0)
    far0, stats, *ahead = run(1, places[2], ahead, later=(lhs, adapter, stats))
    from0 = send(far0, 0)
    *got, stats = tie((*(cots[v] for v in (0b001, 0b010, 0b100)), stats))
    cots[0b001], cots[0b010], cots[0b100] = got
    cots[0b011], cots[0b101], cots[0b110] = send(cots[0b001], 1), send(cots[0b001], 0), send(cots[0b010], 0)
    held = ahead
    near1, stats, *ahead = run(2, places[3], ahead, later=(lhs, adapter, stats))
    cots[0b011], from1, stats = tie((cots[0b011], from1, stats))
    cots[0b111] = send(cots[0b011], 0)
    sent = (near1.astype(f32) + from1.astype(f32)).astype(bf16)
    arrived = send(sent, 1)
    held = ahead + held
    near0, stats = run(3, None, ahead, later=(lhs, adapter, stats))
    cots[0b101], cots[0b110], from0, stats = tie((cots[0b101], cots[0b110], from0, stats))

    got = send(stats, 0)
    stats = stats + got
    stats = stats + send(stats, 1)
    arrived, cots[0b111], stats = tie((arrived, cots[0b111], stats))
    kept = near0.astype(f32) + from0.astype(f32) + arrived.astype(f32)
    last = send(kept[1].astype(bf16), 2)
    stats = stats + send(stats, 2)
    lowrank_rows = stats[n:]
    lowrank_other = swap(lowrank_rows)

    band = 256
    bands = rows // band
    many = (bands + 2) // 2
    order = place(*range(n))
    run = functools.partial(backward, order, band=band, at=at, held=held, weight=weight)
    grad_a, other_a, scaled, proj = run(0, many, first=([cots[v] for v in range(n)], stats, up))
    got_a = swap(other_a)
    last, proj = tie((last, proj))
    unscaled = kept[0] + last.astype(f32)
    grad_b, other_b = run(many, bands - many, later=(scaled, proj))
    got_b = swap(other_b)
    hidden_gradient = jnp.concatenate(
        [(own + got.astype(f32)).astype(bf16) for own, got in ((grad_a, got_a), (grad_b, got_b))], axis=1
    )
    from_sibling = swap(proj)
    proj_own = (proj[:tokens] + from_sibling[tokens:]).astype(bf16)
    proj_other = (proj[tokens:] + from_sibling[:tokens]).astype(bf16)
    down_weight_gradient = adapter_scale * (
        dot(proj_own, hidden, contract_first) + dot(proj_other, hidden_other, contract_first)
    ).T

    norm = jnp.sqrt(lax.dynamic_slice_in_dim(stats, me, 1, 0)[0] + stability_floor)
    rescale = mine(magnitude, 0) / norm
    upstream = block[: 2 * tokens].astype(f32)
    scaled_own = (upstream * rescale).astype(bf16).astype(f32)

    def turned(part):
        lanes = half // tokens
        return jnp.concatenate([part[:, j * tokens : (j + 1) * tokens] for j in range(lanes)])

    up_half = adapter_scale * (
        jnp.dot(turned(lowrank_rows), scaled_own[:tokens], precision=lax.Precision.HIGHEST)
        + jnp.dot(turned(lowrank_other), scaled_own[tokens:], precision=lax.Precision.HIGHEST)
    )
    mixed = (unscaled * rescale).astype(bf16)
    magnitude_half = jnp.sum(upstream * unscaled, axis=0) / norm

    def join(own, other, axis):
        pair = jnp.concatenate([own, other, own], axis)
        return lax.dynamic_slice_in_dim(pair, core * half, 2 * half, axis)

    mixed = join(mixed[:tokens], swap(mixed[tokens:]), 1)
    up_weight_gradient = join(up_half, swap(up_half), 1)
    grad_magnitude = join(magnitude_half, swap(magnitude_half), 0)
    return (mixed, hidden_gradient, down_weight_gradient, up_weight_gradient, grad_magnitude)


def by_tokens(hidden, frozen_down_weight, adapter_down_weight, adapter_up_weight, magnitude, cotangent):
    column_slice = magnitude.shape[0]
    block_offset = lax.axis_index("tensor") * column_slice
    combined_weight = frozen_down_weight.astype(f32) + adapter_scale * dot(adapter_down_weight, adapter_up_weight)
    squares_part = jnp.sum(combined_weight * combined_weight, axis=0)
    squares, reduced_rank_product = lax.psum((squares_part, dot(hidden, adapter_down_weight)), "tensor")
    norm_all = jnp.sqrt(squares + stability_floor)
    column_length_norm = lax.dynamic_slice_in_dim(norm_all, block_offset, column_slice)
    up_weight_columns = lax.dynamic_slice_in_dim(adapter_up_weight, block_offset, column_slice, 1)
    summed_output = lax.psum_scatter(dot(hidden, frozen_down_weight), "tensor", scatter_dimension=1, tiled=True)
    unscaled_output = summed_output + adapter_scale * jnp.dot(
        reduced_rank_product, up_weight_columns.astype(f32), precision=lax.Precision.HIGHEST
    )
    rescale = magnitude / column_length_norm
    mixed = (unscaled_output * rescale).astype(bf16)
    upstream = cotangent.astype(f32)
    scaled_output = (upstream * rescale).astype(bf16)
    magnitude_part = jnp.sum(upstream * unscaled_output, axis=0) / column_length_norm
    block_input = lax.all_gather(scaled_output, "tensor", axis=1, tiled=True)
    projected_output = dot(block_input, adapter_up_weight, contract_trailing).astype(bf16)
    hidden_gradient = dot(block_input, frozen_down_weight, contract_trailing)
    hidden_gradient = hidden_gradient + adapter_scale * dot(projected_output, adapter_down_weight, contract_trailing)
    hidden_gradient = hidden_gradient.astype(bf16)
    down_gradient_piece = adapter_scale * dot(hidden, projected_output, contract_first)
    up_gradient_piece = adapter_scale * lax.dot_general(
        reduced_rank_product, scaled_output.astype(f32), contract_first, precision=lax.Precision.HIGHEST
    )
    pieces = (down_gradient_piece, up_gradient_piece, magnitude_part)
    pieces = [lax.psum(p.astype(bf16), "dp").astype(f32) for p in pieces]
    return (mixed, hidden_gradient, *pieces)


def solution(mesh):
    n = mesh.shape["tensor"]

    def local(hidden, weight, down, up, magnitude, cotangent):
        aligned = magnitude.shape[0] % 256 == 0 and weight.shape[0] % 256 == 0 and hidden.shape[0] % 128 == 0
        if aligned and mesh.shape["dp"] == 2 and n == 8 and down.shape[1] * hidden.shape[0] % (magnitude.shape[0] // 2 * 8) == 0:
            return split_columns(hidden, weight, down, up, magnitude, cotangent)
        return by_tokens(hidden, weight, down, up, magnitude, cotangent)

    in_specs = (
        P(("parts", "dp"), "tensor"),
        P("tensor", None),
        P(("parts", "tensor"), None),
        P("parts", None),
        P(("parts", "tensor")),
        P(("parts", "dp"), "tensor"),
    )
    out_specs = (
        P(("parts", "dp"), "tensor"),
        P(("parts", "dp"), "tensor"),
        P(("parts", "tensor"), None),
        P("parts", "tensor"),
        P(("parts", "tensor")),
    )
    return jax.shard_map(local, mesh=mesh, in_specs=in_specs, out_specs=out_specs, check_vma=False)
```

```python
import functools

import jax
import jax.numpy as jnp
from jax import lax
from jax.experimental import pallas as pl
from jax.experimental.pallas import tpu as pltpu
from jax.sharding import PartitionSpec as P

adapter_scale = 2.0
stability_floor = 1e-06
pad_rows = 16
vmem_bytes = 8 * 1024 * 1024
f32, bf16 = jnp.float32, jnp.bfloat16
small_cost = pl.CostEstimate(flops=1 << 20, bytes_accessed=1 << 20, transcendentals=0)
contract_trailing = (((1,), (1,)), ((), ()))
contract_first = (((0,), (0,)), ((), ()))


def dot(a, b, dims=(((1,), (0,)), ((), ()))):
    return lax.dot_general(a, b, dims, preferred_element_type=f32)


def split_pair(x):
    high = x.astype(bf16)
    return high, (x - high.astype(f32)).astype(bf16)


def sum_of_squares(w_ref):
    rows, width = w_ref.shape
    totals = [jnp.zeros((8, width), f32) for _ in range(2)]
    for i in range(rows // 16):
        w = w_ref[i * 16 : (i + 1) * 16, :].astype(f32)
        w = w * w
        totals[0] = totals[0] + w[:8]
        totals[1] = totals[1] + w[8:]
    return jnp.sum(totals[0] + totals[1], axis=0, keepdims=True)


def vmem():
    return pl.BlockSpec(memory_space=pltpu.VMEM)


def params():
    return pltpu.CompilerParams(vmem_limit_bytes=vmem_bytes)


def block_kernel(tokens, order_ref, own_ref, other_ref, magnitude_ref, out_ref):
    out_ref[:tokens, :] = own_ref[...]
    out_ref[tokens : 2 * tokens, :] = other_ref[...]
    out_ref[2 * tokens :, :] = magnitude_ref[...]


def own_block(order, cotangent, other, magnitude_rows):
    tokens, columns = cotangent.shape
    half = columns // 2
    padded = 2 * tokens + pad_rows
    return pl.pallas_call(
        functools.partial(block_kernel, tokens),
        grid_spec=pltpu.PrefetchScalarGridSpec(
            num_scalar_prefetch=1,
            grid=(1,),
            in_specs=[
                pl.BlockSpec((tokens, half), lambda i, p: (0, lax.rem(p[0], 2))),
                pl.BlockSpec((tokens, half), lambda i, p: (0, lax.rem(p[0], 2))),
                pl.BlockSpec((pad_rows, half), lambda i, p: (0, lax.rem(p[0], 2))),
            ],
            out_specs=pl.BlockSpec((padded, half), lambda i, p: (0, 0)),
        ),
        out_shape=jax.ShapeDtypeStruct((padded, half), bf16),
        compiler_params=params(),
        cost_estimate=small_cost,
        name="own_block",
    )(order, cotangent, other, magnitude_rows)


def load_kernel(tokens, rank, n, order_ref, own_ref, at_ref, up_ref, w_hbm, *refs):
    held, (stats_ref, lhs_ref, sem, own_sem) = refs[:n], refs[n:]
    half = held[0].shape[1]
    columns = [pl.ds(pl.multiple_of(order_ref[k] * half, half), half) for k in range(n)]
    copies = [pltpu.make_async_copy(w_hbm.at[:, c], h, sem.at[k]) for k, (c, h) in enumerate(zip(columns, held))]
    own_copy = pltpu.make_async_copy(own_ref, lhs_ref, own_sem)
    own_copy.start()
    for copy in copies:
        copy.start()

    down = at_ref[...]
    high, low = split_pair(dot(down, down, contract_trailing))
    own_copy.wait()
    turned = dot(down, lhs_ref[...], contract_trailing)
    lanes = half // tokens
    span = rank // lanes
    for j in range(lanes):
        stats_ref[n:, j * tokens : (j + 1) * tokens] = turned[j * span : (j + 1) * span]
    for k in range(n):
        copies[k].wait()
        up = up_ref[:, columns[k]]
        cross = 2 * dot(down, held[k][...]) + adapter_scale * (dot(high, up) + dot(low, up))
        cross = jnp.sum(up.astype(f32) * cross, axis=0, keepdims=True)
        stats_ref[pl.ds(order_ref[n + k], 1), :] = sum_of_squares(held[k]) + adapter_scale * cross


def load(order, own, at, up, weight, half):
    n = order.shape[0] // 2
    tokens, rows = own.shape
    rank = at.shape[0]
    any_ = pl.BlockSpec(memory_space=pl.ANY)
    return pl.pallas_call(
        functools.partial(load_kernel, tokens, rank, n),
        in_specs=[pl.BlockSpec(memory_space=pltpu.SMEM), any_, vmem(), vmem(), any_],
        out_specs=[vmem()] * (n + 2),
        out_shape=[jax.ShapeDtypeStruct((rows, half), bf16)] * n
        + [jax.ShapeDtypeStruct((n + rank * tokens // half, half), f32), jax.ShapeDtypeStruct(own.shape, bf16)],
        scratch_shapes=[pltpu.SemaphoreType.DMA((n,)), pltpu.SemaphoreType.DMA],
        compiler_params=params(),
        cost_estimate=small_cost,
        name="load",
    )(order, own, at, up, weight)


def forward_kernel(tokens, rank, vs, first, order_ref, *refs):
    if first:
        own_ref, other_ref, at_ref, up_ref, *held, out_ref, lhs_ref, adapter_ref, sem = refs
        copy = pltpu.make_async_copy(other_ref, lhs_ref.at[tokens:], sem)
        copy.start()
        lhs_ref[:tokens, :] = own_ref[...]
        copy.wait()
        high, low = split_pair(dot(lhs_ref[...], at_ref[...], contract_trailing))
        adapter_ref[:, :rank] = high
        adapter_ref[:, rank:] = low
    else:
        lhs_ref, adapter_ref, up_ref, *held, out_ref = refs
    half = out_ref.shape[2]
    for i, v in enumerate(vs):
        up = up_ref[:, pl.ds(pl.multiple_of(order_ref[v] * half, half), half)]
        through = dot(adapter_ref[...], jnp.concatenate([up, up], axis=0))
        out_ref[i] = (dot(lhs_ref[...], held[i][...]) + adapter_scale * through).astype(bf16)


def forward(vs, order, held, up, first=None, later=None):
    held = [held[v] for v in vs]
    rows, half = held[0].shape
    if later is None:
        own, other, at = operands = first
        tokens, rank = own.shape[0], at.shape[0]
        specs = [vmem(), pl.BlockSpec(memory_space=pl.ANY), vmem()]
    else:
        lhs, adapter = operands = later
        rank, tokens = adapter.shape[1] // 2, lhs.shape[0] // 2
        specs = [vmem()] * 2
    extra = [((2 * tokens, rows), bf16), ((2 * tokens, 2 * rank), bf16)] if first else []
    return pl.pallas_call(
        functools.partial(forward_kernel, tokens, rank, vs, later is None),
        in_specs=[pl.BlockSpec(memory_space=pltpu.SMEM), *specs] + [vmem()] * (1 + len(held)),
        out_specs=[vmem()] * (1 + len(extra)),
        out_shape=[jax.ShapeDtypeStruct((len(held), 2 * tokens, half), bf16)]
        + [jax.ShapeDtypeStruct(*e) for e in extra],
        scratch_shapes=[pltpu.SemaphoreType.DMA] if first else [],
        compiler_params=params(),
        cost_estimate=small_cost,
        name="forward",
    )(order, *operands, up, *held)


def backward_kernel(tokens, n, start, band, first, order_ref, *refs):
    if first:
        cots, (stats_ref, up_ref, at_ref, *held) = refs[:n], refs[n : 2 * n + 3]
        own_out, other_out, scaled_ref, proj_ref, scales_ref, block_ref = refs[2 * n + 3 :]
    else:
        scaled_ref, proj_ref, at_ref, *held, own_out, other_out = refs
    both = 2 * tokens
    half = held[0].shape[1]
    spans = [slice(k * half, (k + 1) * half) for k in range(n)]

    if first:

        @pl.when(pl.program_id(0) == 0)
        def _():
            projected = jnp.zeros(proj_ref.shape, f32)
            for k in range(n):
                magnitude = jnp.sum(cots[k][both:, :].astype(f32), axis=0, keepdims=True)
                squares = stats_ref[pl.ds(order_ref[n + k], 1), :]
                norm = jnp.sqrt(squares + stability_floor)
                rescale = magnitude / norm
                if k == 0:
                    scales_ref[0:1, :] = norm
                    scales_ref[1:2, :] = rescale
                scaled = (cots[k][:both, :].astype(f32) * rescale).astype(bf16)
                if k == 0:
                    block_ref[...] = scaled
                scaled_ref[:, spans[k]] = scaled
                up = up_ref[:, pl.ds(pl.multiple_of(order_ref[k] * half, half), half)]
                projected = projected + dot(scaled, up, contract_trailing)
            proj_ref[...] = projected

    row = pl.ds(pl.multiple_of((start + pl.program_id(0)) * band, band), band)
    total = adapter_scale * dot(proj_ref[...].astype(bf16), at_ref[:, row])
    for k in range(n):
        total = total + dot(scaled_ref[:, spans[k]], held[k][row, :], contract_trailing)
    own_out[...] = total[:tokens]
    other_out[...] = total[tokens:].astype(bf16)


def backward(order, start, bands, band, at, held, first=None, later=None):
    n = order.shape[0] // 2
    half = held[0].shape[1]
    rank = at.shape[0]
    if later is None:
        cots, stats, up = first
        both = cots[0].shape[0] - pad_rows
        operands = [*cots, stats, up]
        extra = [((both, n * half), bf16), ((both, rank), f32), ((2, half), f32), ((both, half), bf16)]
    else:
        operands, extra = later, []
        both = later[0].shape[0]
    tokens = both // 2
    return pl.pallas_call(
        functools.partial(backward_kernel, tokens, n, start, band, later is None),
        grid=(bands,),
        in_specs=[pl.BlockSpec(memory_space=pltpu.SMEM)] + [vmem()] * (len(operands) + 1 + n),
        out_specs=[pl.BlockSpec((tokens, band), lambda i: (0, i))] * 2 + [vmem()] * len(extra),
        out_shape=[
            jax.ShapeDtypeStruct((tokens, bands * band), f32),
            jax.ShapeDtypeStruct((tokens, bands * band), bf16),
        ]
        + [jax.ShapeDtypeStruct(*e) for e in extra],
        compiler_params=params(),
        cost_estimate=small_cost,
        name="backward",
    )(order, *operands, at, *held)


def split_columns(hidden, weight, down, up, magnitude, cotangent):
    n, bits = 8, 3
    tokens = hidden.shape[0]
    half = magnitude.shape[0] // 2
    rows = weight.shape[0]
    me, core = lax.axis_index("tensor"), lax.axis_index("dp")
    swap = lambda x: lax.ppermute(x, "dp", [(0, 1), (1, 0)])
    orders = [[1, 2, 4], [2, 1, 4]]

    def send(x, k):
        pairs = [(2 * t + c, 2 * (t ^ orders[c][k]) + c) for t in range(n) for c in range(2)]
        return lax.ppermute(x, ("tensor", "dp"), pairs)

    def reach(v, c):
        return sum(orders[c][k] for k in range(bits) if v >> (bits - 1 - k) & 1)

    def place(*vs):
        shard = [me ^ jnp.where(core == 0, reach(v, 0), reach(v, 1)) for v in vs]
        return jnp.stack([2 * s + core for s in shard] + shard).astype(jnp.int32)

    tie = lax.optimization_barrier
    at = down.T
    order = place(*range(n))
    low_core = core == 0

    cot_other = swap(cotangent)
    hidden_other = swap(hidden)
    first = lax.reduce_precision(magnitude, 8, 7)
    second = lax.reduce_precision(magnitude - first, 8, 7)
    third = magnitude - first - second
    magnitude_rows = jnp.concatenate(
        [jnp.stack([first, second, third]), jnp.zeros((pad_rows - 3, 2 * half), f32)]
    ).astype(bf16)
    low_core, order, cot_other = tie((low_core, order, cot_other))
    block = own_block(order, cotangent, cot_other, magnitude_rows)

    cots = {0b000: block, 0b001: send(block, 2), 0b010: send(block, 1), 0b100: send(block, 0)}
    block, order = tie((block, order))
    *held, stats, own = load(order, hidden, at, up, weight, half)

    got = send(stats, 0)
    far1, lhs, adapter = forward((0b110, 0b111), order, held, up, first=(own, hidden_other, at))
    run = lambda *vs: forward(vs, order, held, up, later=(lhs, adapter))[0]
    *arrived, got, far1 = tie((*(cots[v] for v in (0b001, 0b010, 0b100)), got, far1))
    cots[0b001], cots[0b010], cots[0b100] = arrived
    stats = stats + got
    got = send(stats, 1)
    from1 = send(far1, 0)
    cots[0b011], cots[0b101], cots[0b110] = send(cots[0b001], 1), send(cots[0b001], 0), send(cots[0b010], 0)
    far0 = run(0b100, 0b101)
    got, far0 = tie((got, far0))
    stats = stats + got
    got = send(stats, 2)
    from0 = send(far0, 0)
    near1 = run(0b010, 0b011)
    cots[0b011], cots[0b101], cots[0b110], from1, got, near1 = tie(
        (cots[0b011], cots[0b101], cots[0b110], from1, got, near1)
    )
    stats = stats + got
    cots[0b111] = send(cots[0b011], 0)
    arrived = send((near1.astype(f32) + from1.astype(f32)).astype(bf16), 1)
    near0 = run(0b000, 0b001)
    cots[0b111], from0, near0, arrived, stats = tie((cots[0b111], from0, near0, arrived, stats))
    kept = near0.astype(f32) + from0.astype(f32) + arrived.astype(f32)
    last = send(kept[1].astype(bf16), 2)
    lowrank_rows = stats[n:]
    lowrank_other = swap(lowrank_rows)

    band = 256
    bands = rows // band
    many = (bands + 2) // 2
    run = functools.partial(backward, order, band=band, at=at, held=held)
    grad_a, other_a, scaled, proj, scales, scaled_own = run(0, many, first=([cots[v] for v in range(n)], stats, up))
    got_a = swap(other_a)
    last, proj = tie((last, proj))
    unscaled = kept[0] + last.astype(f32)
    grad_b, other_b = run(many, bands - many, later=(scaled, proj))
    got_b = swap(other_b)
    hidden_gradient = jnp.concatenate(
        [(own + got.astype(f32)).astype(bf16) for own, got in ((grad_a, got_a), (grad_b, got_b))], axis=1
    )
    from_sibling = swap(proj)
    proj_own = (proj[:tokens] + from_sibling[tokens:]).astype(bf16)
    proj_other = (proj[tokens:] + from_sibling[:tokens]).astype(bf16)
    down_weight_gradient = adapter_scale * (
        dot(proj_own, hidden, contract_first) + dot(proj_other, hidden_other, contract_first)
    ).T

    norm, rescale = scales[0], scales[1]
    upstream = block[: 2 * tokens].astype(f32)
    scaled_own = scaled_own.astype(f32)

    def turned(part):
        lanes = half // tokens
        return jnp.concatenate([part[:, j * tokens : (j + 1) * tokens] for j in range(lanes)])

    up_half = adapter_scale * (
        jnp.dot(turned(lowrank_rows), scaled_own[:tokens], precision=lax.Precision.HIGHEST)
        + jnp.dot(turned(lowrank_other), scaled_own[tokens:], precision=lax.Precision.HIGHEST)
    )
    mixed = (unscaled * rescale).astype(bf16)
    magnitude_half = jnp.sum(upstream * unscaled, axis=0) / norm

    def join(own, other, axis):
        return jnp.where(low_core, jnp.concatenate([own, other], axis), jnp.concatenate([other, own], axis))

    mixed = join(mixed[:tokens], swap(mixed[tokens:]), 1)
    up_weight_gradient = join(up_half, swap(up_half), 1)
    grad_magnitude = join(magnitude_half, swap(magnitude_half), 0)
    return (mixed, hidden_gradient, down_weight_gradient, up_weight_gradient, grad_magnitude)


def by_tokens(hidden, frozen_down_weight, adapter_down_weight, adapter_up_weight, magnitude, cotangent):
    column_slice = magnitude.shape[0]
    block_offset = lax.axis_index("tensor") * column_slice
    combined_weight = frozen_down_weight.astype(f32) + adapter_scale * dot(adapter_down_weight, adapter_up_weight)
    squares_part = jnp.sum(combined_weight * combined_weight, axis=0)
    squares, reduced_rank_product = lax.psum((squares_part, dot(hidden, adapter_down_weight)), "tensor")
    norm_all = jnp.sqrt(squares + stability_floor)
    column_length_norm = lax.dynamic_slice_in_dim(norm_all, block_offset, column_slice)
    up_weight_columns = lax.dynamic_slice_in_dim(adapter_up_weight, block_offset, column_slice, 1)
    summed_output = lax.psum_scatter(dot(hidden, frozen_down_weight), "tensor", scatter_dimension=1, tiled=True)
    unscaled_output = summed_output + adapter_scale * jnp.dot(
        reduced_rank_product, up_weight_columns.astype(f32), precision=lax.Precision.HIGHEST
    )
    rescale = magnitude / column_length_norm
    mixed = (unscaled_output * rescale).astype(bf16)
    upstream = cotangent.astype(f32)
    scaled_output = (upstream * rescale).astype(bf16)
    magnitude_part = jnp.sum(upstream * unscaled_output, axis=0) / column_length_norm
    block_input = lax.all_gather(scaled_output, "tensor", axis=1, tiled=True)
    projected_output = dot(block_input, adapter_up_weight, contract_trailing).astype(bf16)
    hidden_gradient = dot(block_input, frozen_down_weight, contract_trailing)
    hidden_gradient = hidden_gradient + adapter_scale * dot(projected_output, adapter_down_weight, contract_trailing)
    hidden_gradient = hidden_gradient.astype(bf16)
    down_gradient_piece = adapter_scale * dot(hidden, projected_output, contract_first)
    up_gradient_piece = adapter_scale * lax.dot_general(
        reduced_rank_product, scaled_output.astype(f32), contract_first, precision=lax.Precision.HIGHEST
    )
    pieces = (down_gradient_piece, up_gradient_piece, magnitude_part)
    pieces = [lax.psum(p.astype(bf16), "dp").astype(f32) for p in pieces]
    return (mixed, hidden_gradient, *pieces)


def solution(mesh):
    n = mesh.shape["tensor"]

    def local(hidden, weight, down, up, magnitude, cotangent):
        aligned = magnitude.shape[0] % 256 == 0 and weight.shape[0] % 256 == 0 and hidden.shape[0] % 128 == 0
        if aligned and mesh.shape["dp"] == 2 and n == 8 and down.shape[1] * hidden.shape[0] % (magnitude.shape[0] // 2 * 8) == 0:
            return split_columns(hidden, weight, down, up, magnitude, cotangent)
        return by_tokens(hidden, weight, down, up, magnitude, cotangent)

    in_specs = (
        P(("parts", "dp"), "tensor"),
        P("tensor", None),
        P(("parts", "tensor"), None),
        P("parts", None),
        P(("parts", "tensor")),
        P(("parts", "dp"), "tensor"),
    )
    out_specs = (
        P(("parts", "dp"), "tensor"),
        P(("parts", "dp"), "tensor"),
        P(("parts", "tensor"), None),
        P("parts", "tensor"),
        P(("parts", "tensor")),
    )
    return jax.shard_map(local, mesh=mesh, in_specs=in_specs, out_specs=out_specs, check_vma=False)
```

```python
import functools

import jax
import jax.numpy as jnp
from jax import lax
from jax.experimental import pallas as pl
from jax.experimental.pallas import tpu as pltpu
from jax.sharding import PartitionSpec as P

adapter_scale = 2.0
stability_floor = 1e-06
pad_rows = 16
vmem_bytes = 8 * 1024 * 1024
f32, bf16 = jnp.float32, jnp.bfloat16
small_cost = pl.CostEstimate(flops=1 << 20, bytes_accessed=1 << 20, transcendentals=0)
contract_trailing = (((1,), (1,)), ((), ()))
contract_first = (((0,), (0,)), ((), ()))


def dot(a, b, dims=(((1,), (0,)), ((), ()))):
    return lax.dot_general(a, b, dims, preferred_element_type=f32)


def split_pair(x):
    high = x.astype(bf16)
    return high, (x - high.astype(f32)).astype(bf16)


def sum_of_squares(w_ref):
    rows, width = w_ref.shape
    totals = [jnp.zeros((8, width), f32) for _ in range(2)]
    for i in range(rows // 16):
        w = w_ref[i * 16 : (i + 1) * 16, :].astype(f32)
        w = w * w
        totals[0] = totals[0] + w[:8]
        totals[1] = totals[1] + w[8:]
    return jnp.sum(totals[0] + totals[1], axis=0, keepdims=True)


def vmem():
    return pl.BlockSpec(memory_space=pltpu.VMEM)


def anywhere():
    return pl.BlockSpec(memory_space=pl.ANY)


def params():
    return pltpu.CompilerParams(vmem_limit_bytes=vmem_bytes)


def block_kernel(tokens, order_ref, own_ref, other_ref, magnitude_ref, *refs):
    out_ref = refs[-1]
    out_ref[:tokens, :] = own_ref[...]
    out_ref[tokens : 2 * tokens, :] = other_ref[...]
    out_ref[2 * tokens :, :] = magnitude_ref[...]


def own_block(order, cotangent, other, magnitude_rows, *early):
    tokens, columns = cotangent.shape
    half = columns // 2
    padded = 2 * tokens + pad_rows
    return pl.pallas_call(
        functools.partial(block_kernel, tokens),
        grid_spec=pltpu.PrefetchScalarGridSpec(
            num_scalar_prefetch=1,
            grid=(1,),
            in_specs=[
                pl.BlockSpec((tokens, half), lambda i, p: (0, lax.rem(p[0], 2))),
                pl.BlockSpec((tokens, half), lambda i, p: (0, lax.rem(p[0], 2))),
                pl.BlockSpec((pad_rows, half), lambda i, p: (0, lax.rem(p[0], 2))),
                *[vmem()] * len(early),
            ],
            out_specs=pl.BlockSpec((padded, half), lambda i, p: (0, 0)),
        ),
        out_shape=jax.ShapeDtypeStruct((padded, half), bf16),
        compiler_params=params(),
        cost_estimate=small_cost,
        name="own_block",
    )(order, cotangent, other, magnitude_rows, *early)


def load_kernel(tokens, rank, n, vs, first, order_ref, before_ref, at_ref, up_ref, w_hbm, *refs):
    held, (stats_ref, sem) = refs[: len(vs)], refs[len(vs) :]
    half = held[0].shape[1]
    columns = [pl.ds(pl.multiple_of(order_ref[v] * half, half), half) for v in vs]
    copies = [pltpu.make_async_copy(w_hbm.at[:, c], h, sem.at[k]) for k, (c, h) in enumerate(zip(columns, held))]
    for copy in copies:
        copy.start()

    down = at_ref[...]
    high, low = split_pair(dot(down, down, contract_trailing))
    if first:
        turned = dot(down, before_ref[...], contract_trailing)
        lanes = half // tokens
        span = rank // lanes
        stats_ref[:n, :] = jnp.zeros((n, half), f32)
        for j in range(lanes):
            stats_ref[n:, j * tokens : (j + 1) * tokens] = turned[j * span : (j + 1) * span]
    else:
        stats_ref[...] = before_ref[...]
    for k, v in enumerate(vs):
        copies[k].wait()
        up = up_ref[:, columns[k]]
        cross = 2 * dot(down, held[k][...]) + adapter_scale * (dot(high, up) + dot(low, up))
        cross = jnp.sum(up.astype(f32) * cross, axis=0, keepdims=True)
        stats_ref[pl.ds(order_ref[n + v], 1), :] = sum_of_squares(held[k]) + adapter_scale * cross


def load(vs, order, at, up, weight, half, own=None, before=None):
    n = order.shape[0] // 2
    rank, rows = at.shape
    first = before is None
    tokens = own.shape[0] if first else None
    stats = (n + rank * tokens // half, half) if first else before.shape
    return pl.pallas_call(
        functools.partial(load_kernel, tokens, rank, n, vs, first),
        in_specs=[pl.BlockSpec(memory_space=pltpu.SMEM), vmem(), vmem(), vmem(), anywhere()],
        out_specs=[vmem()] * (len(vs) + 1),
        out_shape=[jax.ShapeDtypeStruct((rows, half), bf16)] * len(vs) + [jax.ShapeDtypeStruct(stats, f32)],
        scratch_shapes=[pltpu.SemaphoreType.DMA((len(vs),))],
        compiler_params=params(),
        cost_estimate=small_cost,
        name="load",
    )(order, own if first else before, at, up, weight)


def forward_kernel(tokens, rank, vs, first, order_ref, *refs):
    if first:
        own_ref, other_ref, at_ref, up_ref, *held, out_ref, lhs_ref, adapter_ref, sem = refs
        copy = pltpu.make_async_copy(other_ref, lhs_ref.at[tokens:], sem)
        copy.start()
        lhs_ref[:tokens, :] = own_ref[...]
        copy.wait()
        high, low = split_pair(dot(lhs_ref[...], at_ref[...], contract_trailing))
        adapter_ref[:, :rank] = high
        adapter_ref[:, rank:] = low
    else:
        lhs_ref, adapter_ref, up_ref, *held, out_ref = refs
    half = out_ref.shape[2]
    for i, v in enumerate(vs):
        up = up_ref[:, pl.ds(pl.multiple_of(order_ref[v] * half, half), half)]
        through = dot(adapter_ref[...], jnp.concatenate([up, up], axis=0))
        out_ref[i] = (dot(lhs_ref[...], held[i][...]) + adapter_scale * through).astype(bf16)


def forward(vs, order, held, up, first=None, later=None):
    rows, half = held[0].shape
    if later is None:
        own, other, at = operands = first
        tokens, rank = own.shape[0], at.shape[0]
        specs = [vmem(), anywhere(), vmem()]
    else:
        lhs, adapter = operands = later
        rank, tokens = adapter.shape[1] // 2, lhs.shape[0] // 2
        specs = [vmem()] * 2
    extra = [((2 * tokens, rows), bf16), ((2 * tokens, 2 * rank), bf16)] if first else []
    return pl.pallas_call(
        functools.partial(forward_kernel, tokens, rank, vs, later is None),
        in_specs=[pl.BlockSpec(memory_space=pltpu.SMEM), *specs] + [vmem()] * (1 + len(held)),
        out_specs=[vmem()] * (1 + len(extra)),
        out_shape=[jax.ShapeDtypeStruct((len(held), 2 * tokens, half), bf16)]
        + [jax.ShapeDtypeStruct(*e) for e in extra],
        scratch_shapes=[pltpu.SemaphoreType.DMA] if first else [],
        compiler_params=params(),
        cost_estimate=small_cost,
        name="forward",
    )(order, *operands, up, *held)


def backward_kernel(tokens, n, start, band, first, order_ref, *refs):
    if first:
        cots, (stats_ref, up_ref, at_ref, *held) = refs[:n], refs[n : 2 * n + 3]
        own_out, other_out, scaled_ref, proj_ref, scales_ref, block_ref = refs[2 * n + 3 :]
    else:
        scaled_ref, proj_ref, at_ref, *held, own_out, other_out = refs
    both = 2 * tokens
    half = held[0].shape[1]
    spans = [slice(k * half, (k + 1) * half) for k in range(n)]

    if first:

        @pl.when(pl.program_id(0) == 0)
        def _():
            projected = jnp.zeros(proj_ref.shape, f32)
            for k in range(n):
                magnitude = jnp.sum(cots[k][both:, :].astype(f32), axis=0, keepdims=True)
                squares = stats_ref[pl.ds(order_ref[n + k], 1), :]
                norm = jnp.sqrt(squares + stability_floor)
                rescale = magnitude / norm
                if k == 0:
                    scales_ref[0:1, :] = norm
                    scales_ref[1:2, :] = rescale
                scaled = (cots[k][:both, :].astype(f32) * rescale).astype(bf16)
                if k == 0:
                    block_ref[...] = scaled
                scaled_ref[:, spans[k]] = scaled
                up = up_ref[:, pl.ds(pl.multiple_of(order_ref[k] * half, half), half)]
                projected = projected + dot(scaled, up, contract_trailing)
            proj_ref[...] = projected

    row = pl.ds(pl.multiple_of((start + pl.program_id(0)) * band, band), band)
    total = adapter_scale * dot(proj_ref[...].astype(bf16), at_ref[:, row])
    for k in range(n):
        total = total + dot(scaled_ref[:, spans[k]], held[k][row, :], contract_trailing)
    own_out[...] = total[:tokens]
    other_out[...] = total[tokens:].astype(bf16)


def backward(order, start, bands, band, at, held, first=None, later=None):
    n = order.shape[0] // 2
    half = held[0].shape[1]
    rank = at.shape[0]
    if later is None:
        cots, stats, up = first
        both = cots[0].shape[0] - pad_rows
        operands = [*cots, stats, up]
        extra = [((both, n * half), bf16), ((both, rank), f32), ((2, half), f32), ((both, half), bf16)]
    else:
        operands, extra = later, []
        both = later[0].shape[0]
    tokens = both // 2
    return pl.pallas_call(
        functools.partial(backward_kernel, tokens, n, start, band, later is None),
        grid=(bands,),
        in_specs=[pl.BlockSpec(memory_space=pltpu.SMEM)] + [vmem()] * (len(operands) + 1 + n),
        out_specs=[pl.BlockSpec((tokens, band), lambda i: (0, i))] * 2 + [vmem()] * len(extra),
        out_shape=[
            jax.ShapeDtypeStruct((tokens, bands * band), f32),
            jax.ShapeDtypeStruct((tokens, bands * band), bf16),
        ]
        + [jax.ShapeDtypeStruct(*e) for e in extra],
        compiler_params=params(),
        cost_estimate=small_cost,
        name="backward",
    )(order, *operands, at, *held)


def split_columns(hidden, weight, down, up, magnitude, cotangent):
    n, bits = 8, 3
    tokens = hidden.shape[0]
    half = magnitude.shape[0] // 2
    rows = weight.shape[0]
    me, core = lax.axis_index("tensor"), lax.axis_index("dp")
    swap = lambda x: lax.ppermute(x, "dp", [(0, 1), (1, 0)])
    orders = [[1, 2, 4], [2, 1, 4]]

    def send(x, k):
        pairs = [(2 * t + c, 2 * (t ^ orders[c][k]) + c) for t in range(n) for c in range(2)]
        return lax.ppermute(x, ("tensor", "dp"), pairs)

    def reach(v, c):
        return sum(orders[c][k] for k in range(bits) if v >> (bits - 1 - k) & 1)

    def place(*vs):
        shard = [me ^ jnp.where(core == 0, reach(v, 0), reach(v, 1)) for v in vs]
        return jnp.stack([2 * s + core for s in shard] + shard).astype(jnp.int32)

    tie = lax.optimization_barrier
    at = down.T
    order = place(*range(n))
    low_core = core == 0

    cot_other = swap(cotangent)
    hidden_other = swap(hidden)
    first = lax.reduce_precision(magnitude, 8, 7)
    second = lax.reduce_precision(magnitude - first, 8, 7)
    third = magnitude - first - second
    magnitude_rows = jnp.concatenate(
        [jnp.stack([first, second, third]), jnp.zeros((pad_rows - 3, 2 * half), f32)]
    ).astype(bf16)
    low_core, order, cot_other = tie((low_core, order, cot_other))
    block = own_block(order, cotangent, cot_other, magnitude_rows, at, up, hidden)

    cots = {0b000: block, 0b001: send(block, 2), 0b010: send(block, 1), 0b100: send(block, 0)}

    run_load = functools.partial(load, at=at, up=up, weight=weight, half=half)
    *far, stats = run_load((0b100, 0b101, 0b110, 0b111), order, own=hidden)
    *arrived, stats = tie((*(cots[v] for v in (0b001, 0b010, 0b100)), stats))
    cots[0b001], cots[0b010], cots[0b100] = arrived
    cots[0b011] = send(cots[0b001], 1)
    pair = send(jnp.stack([cots[0b001], cots[0b010]]), 0)
    sent, lhs, adapter = forward((0b100, 0b101, 0b110, 0b111), order, far, up, first=(hidden, hidden_other, at))
    run = lambda vs, held: forward(vs, order, held, up, later=(lhs, adapter))[0]
    cots[0b011], pair, order_after, sent = tie((cots[0b011], pair, order, sent))
    cots[0b101], cots[0b110] = pair[0], pair[1]
    from_far = send(sent, 0)
    cots[0b111] = send(cots[0b011], 0)
    *near, stats = run_load((0b000, 0b001, 0b010, 0b011), order_after, before=stats)
    cots[0b111], stats = tie((cots[0b111], stats))
    got = send(stats, 0)
    near1 = run((0b010, 0b011), near[2:])
    from_far, got, near1 = tie((from_far, got, near1))
    stats = stats + got
    got = send(stats, 1)
    arrived = send((near1.astype(f32) + from_far[2:].astype(f32)).astype(bf16), 1)
    near0 = run((0b000, 0b001), near[:2])
    got, near0 = tie((got, near0))
    stats = stats + got
    got = send(stats, 2)
    arrived, got = tie((arrived, got))
    stats = stats + got
    kept = near0.astype(f32) + from_far[:2].astype(f32) + arrived.astype(f32)
    last = send(kept[1].astype(bf16), 2)
    lowrank_rows = stats[n:]
    lowrank_other = swap(lowrank_rows)
    held = near + far

    band = 256
    bands = rows // band
    many = (bands + 2) // 2
    run = functools.partial(backward, order, band=band, at=at, held=held)
    grad_a, other_a, scaled, proj, scales, scaled_own = run(0, many, first=([cots[v] for v in range(n)], stats, up))
    got_a = swap(other_a)
    from_sibling = swap(proj)
    lowrank_other, scaled_own = tie((lowrank_other, scaled_own))
    scaled_own = scaled_own.astype(f32)

    def turned(part):
        lanes = half // tokens
        return jnp.concatenate([part[:, j * tokens : (j + 1) * tokens] for j in range(lanes)])

    up_half = adapter_scale * (
        jnp.dot(turned(lowrank_rows), scaled_own[:tokens], precision=lax.Precision.HIGHEST)
        + jnp.dot(turned(lowrank_other), scaled_own[tokens:], precision=lax.Precision.HIGHEST)
    )
    up_other = swap(up_half)
    grad_b, other_b = run(many, bands - many, later=(scaled, proj))
    got_a, from_sibling, up_other, last, other_b = tie((got_a, from_sibling, up_other, last, other_b))
    got_b = swap(other_b)
    hidden_gradient = jnp.concatenate(
        [(own + got.astype(f32)).astype(bf16) for own, got in ((grad_a, got_a), (grad_b, got_b))], axis=1
    )
    proj_own = (proj[:tokens] + from_sibling[tokens:]).astype(bf16)
    proj_other = (proj[tokens:] + from_sibling[:tokens]).astype(bf16)
    down_weight_gradient = adapter_scale * (
        dot(proj_own, hidden, contract_first) + dot(proj_other, hidden_other, contract_first)
    ).T

    norm, rescale = scales[0], scales[1]
    unscaled = kept[0] + last.astype(f32)
    mixed = (unscaled * rescale).astype(bf16)
    magnitude_half = jnp.sum(block[: 2 * tokens].astype(f32) * unscaled, axis=0) / norm

    def join(own, other, axis):
        return jnp.where(low_core, jnp.concatenate([own, other], axis), jnp.concatenate([other, own], axis))

    mixed = join(mixed[:tokens], swap(mixed[tokens:]), 1)
    up_weight_gradient = join(up_half, up_other, 1)
    grad_magnitude = join(magnitude_half, swap(magnitude_half), 0)
    return (mixed, hidden_gradient, down_weight_gradient, up_weight_gradient, grad_magnitude)


def by_tokens(hidden, frozen_down_weight, adapter_down_weight, adapter_up_weight, magnitude, cotangent):
    column_slice = magnitude.shape[0]
    block_offset = lax.axis_index("tensor") * column_slice
    combined_weight = frozen_down_weight.astype(f32) + adapter_scale * dot(adapter_down_weight, adapter_up_weight)
    squares_part = jnp.sum(combined_weight * combined_weight, axis=0)
    squares, reduced_rank_product = lax.psum((squares_part, dot(hidden, adapter_down_weight)), "tensor")
    norm_all = jnp.sqrt(squares + stability_floor)
    column_length_norm = lax.dynamic_slice_in_dim(norm_all, block_offset, column_slice)
    up_weight_columns = lax.dynamic_slice_in_dim(adapter_up_weight, block_offset, column_slice, 1)
    summed_output = lax.psum_scatter(dot(hidden, frozen_down_weight), "tensor", scatter_dimension=1, tiled=True)
    unscaled_output = summed_output + adapter_scale * jnp.dot(
        reduced_rank_product, up_weight_columns.astype(f32), precision=lax.Precision.HIGHEST
    )
    rescale = magnitude / column_length_norm
    mixed = (unscaled_output * rescale).astype(bf16)
    upstream = cotangent.astype(f32)
    scaled_output = (upstream * rescale).astype(bf16)
    magnitude_part = jnp.sum(upstream * unscaled_output, axis=0) / column_length_norm
    block_input = lax.all_gather(scaled_output, "tensor", axis=1, tiled=True)
    projected_output = dot(block_input, adapter_up_weight, contract_trailing).astype(bf16)
    hidden_gradient = dot(block_input, frozen_down_weight, contract_trailing)
    hidden_gradient = hidden_gradient + adapter_scale * dot(projected_output, adapter_down_weight, contract_trailing)
    hidden_gradient = hidden_gradient.astype(bf16)
    down_gradient_piece = adapter_scale * dot(hidden, projected_output, contract_first)
    up_gradient_piece = adapter_scale * lax.dot_general(
        reduced_rank_product, scaled_output.astype(f32), contract_first, precision=lax.Precision.HIGHEST
    )
    pieces = (down_gradient_piece, up_gradient_piece, magnitude_part)
    pieces = [lax.psum(p.astype(bf16), "dp").astype(f32) for p in pieces]
    return (mixed, hidden_gradient, *pieces)


def solution(mesh):
    n = mesh.shape["tensor"]

    def local(hidden, weight, down, up, magnitude, cotangent):
        aligned = magnitude.shape[0] % 256 == 0 and weight.shape[0] % 256 == 0 and hidden.shape[0] % 128 == 0
        if aligned and mesh.shape["dp"] == 2 and n == 8 and down.shape[1] * hidden.shape[0] % (magnitude.shape[0] // 2 * 8) == 0:
            return split_columns(hidden, weight, down, up, magnitude, cotangent)
        return by_tokens(hidden, weight, down, up, magnitude, cotangent)

    in_specs = (
        P(("parts", "dp"), "tensor"),
        P("tensor", None),
        P(("parts", "tensor"), None),
        P("parts", None),
        P(("parts", "tensor")),
        P(("parts", "dp"), "tensor"),
    )
    out_specs = (
        P(("parts", "dp"), "tensor"),
        P(("parts", "dp"), "tensor"),
        P(("parts", "tensor"), None),
        P("parts", "tensor"),
        P(("parts", "tensor")),
    )
    return jax.shard_map(local, mesh=mesh, in_specs=in_specs, out_specs=out_specs, check_vma=False)
```

```python
import functools

import jax
import jax.numpy as jnp
from jax import lax
from jax.experimental import pallas as pl
from jax.experimental.pallas import tpu as pltpu
from jax.sharding import PartitionSpec as P

adapter_scale = 2.0
stability_floor = 1e-06
pad_rows = 16
vmem_bytes = 8 * 1024 * 1024
f32, bf16 = jnp.float32, jnp.bfloat16
small_cost = pl.CostEstimate(flops=1 << 20, bytes_accessed=1 << 20, transcendentals=0)
contract_trailing = (((1,), (1,)), ((), ()))
contract_first = (((0,), (0,)), ((), ()))


def dot(a, b, dims=(((1,), (0,)), ((), ()))):
    return lax.dot_general(a, b, dims, preferred_element_type=f32)


def split_pair(x):
    high = x.astype(bf16)
    return high, (x - high.astype(f32)).astype(bf16)


def sum_of_squares(w_ref):
    rows, width = w_ref.shape
    totals = [jnp.zeros((8, width), f32) for _ in range(2)]
    for i in range(rows // 16):
        w = w_ref[i * 16 : (i + 1) * 16, :].astype(f32)
        w = w * w
        totals[0] = totals[0] + w[:8]
        totals[1] = totals[1] + w[8:]
    return jnp.sum(totals[0] + totals[1], axis=0, keepdims=True)


def vmem():
    return pl.BlockSpec(memory_space=pltpu.VMEM)


def anywhere():
    return pl.BlockSpec(memory_space=pl.ANY)


def params():
    return pltpu.CompilerParams(vmem_limit_bytes=vmem_bytes)


def block_kernel(tokens, order_ref, own_ref, other_ref, magnitude_ref, *refs):
    out_ref = refs[-1]
    out_ref[:tokens, :] = own_ref[...]
    out_ref[tokens : 2 * tokens, :] = other_ref[...]
    out_ref[2 * tokens :, :] = magnitude_ref[...]


def own_block(order, cotangent, other, magnitude_rows, *early):
    tokens, columns = cotangent.shape
    half = columns // 2
    padded = 2 * tokens + pad_rows
    return pl.pallas_call(
        functools.partial(block_kernel, tokens),
        grid_spec=pltpu.PrefetchScalarGridSpec(
            num_scalar_prefetch=1,
            grid=(1,),
            in_specs=[
                pl.BlockSpec((tokens, half), lambda i, p: (0, lax.rem(p[0], 2))),
                pl.BlockSpec((tokens, half), lambda i, p: (0, lax.rem(p[0], 2))),
                pl.BlockSpec((pad_rows, half), lambda i, p: (0, lax.rem(p[0], 2))),
                *[vmem()] * len(early),
            ],
            out_specs=pl.BlockSpec((padded, half), lambda i, p: (0, 0)),
        ),
        out_shape=jax.ShapeDtypeStruct((padded, half), bf16),
        compiler_params=params(),
        cost_estimate=small_cost,
        name="own_block",
    )(order, cotangent, other, magnitude_rows, *early)


def load_kernel(tokens, rank, n, vs, first, order_ref, before_ref, at_ref, up_ref, w_hbm, *refs):
    held, (stats_ref, sem) = refs[: len(vs)], refs[len(vs) :]
    half = held[0].shape[1]
    columns = [pl.ds(pl.multiple_of(order_ref[v] * half, half), half) for v in vs]
    copies = [pltpu.make_async_copy(w_hbm.at[:, c], h, sem.at[k]) for k, (c, h) in enumerate(zip(columns, held))]
    for copy in copies:
        copy.start()

    down = at_ref[...]
    high, low = split_pair(dot(down, down, contract_trailing))
    if first:
        turned = dot(down, before_ref[...], contract_trailing)
        lanes = half // tokens
        span = rank // lanes
        stats_ref[:n, :] = jnp.zeros((n, half), f32)
        for j in range(lanes):
            stats_ref[n:, j * tokens : (j + 1) * tokens] = turned[j * span : (j + 1) * span]
    else:
        stats_ref[...] = before_ref[...]
    for k, v in enumerate(vs):
        copies[k].wait()
        up = up_ref[:, columns[k]]
        cross = 2 * dot(down, held[k][...]) + adapter_scale * (dot(high, up) + dot(low, up))
        cross = jnp.sum(up.astype(f32) * cross, axis=0, keepdims=True)
        stats_ref[pl.ds(order_ref[n + v], 1), :] = sum_of_squares(held[k]) + adapter_scale * cross


def load(vs, order, at, up, weight, half, own=None, before=None):
    n = order.shape[0] // 2
    rank, rows = at.shape
    first = before is None
    tokens = own.shape[0] if first else None
    stats = (n + rank * tokens // half, half) if first else before.shape
    return pl.pallas_call(
        functools.partial(load_kernel, tokens, rank, n, vs, first),
        in_specs=[pl.BlockSpec(memory_space=pltpu.SMEM), vmem(), vmem(), vmem(), anywhere()],
        out_specs=[vmem()] * (len(vs) + 1),
        out_shape=[jax.ShapeDtypeStruct((rows, half), bf16)] * len(vs) + [jax.ShapeDtypeStruct(stats, f32)],
        scratch_shapes=[pltpu.SemaphoreType.DMA((len(vs),))],
        compiler_params=params(),
        cost_estimate=small_cost,
        name="load",
    )(order, own if first else before, at, up, weight)


def forward_kernel(tokens, rank, vs, first, order_ref, *refs):
    if first:
        own_ref, other_ref, at_ref, up_ref, *held, out_ref, lhs_ref, adapter_ref, sem = refs
        copy = pltpu.make_async_copy(other_ref, lhs_ref.at[tokens:], sem)
        copy.start()
        lhs_ref[:tokens, :] = own_ref[...]
        copy.wait()
        high, low = split_pair(dot(lhs_ref[...], at_ref[...], contract_trailing))
        adapter_ref[:, :rank] = high
        adapter_ref[:, rank:] = low
    else:
        lhs_ref, adapter_ref, up_ref, *held, out_ref = refs
    half = out_ref.shape[2]
    for i, v in enumerate(vs):
        up = up_ref[:, pl.ds(pl.multiple_of(order_ref[v] * half, half), half)]
        through = dot(adapter_ref[...], jnp.concatenate([up, up], axis=0))
        out_ref[i] = (dot(lhs_ref[...], held[i][...]) + adapter_scale * through).astype(bf16)


def forward(vs, order, held, up, first=None, later=None):
    rows, half = held[0].shape
    if later is None:
        own, other, at = operands = first
        tokens, rank = own.shape[0], at.shape[0]
        specs = [vmem(), anywhere(), vmem()]
    else:
        lhs, adapter = operands = later
        rank, tokens = adapter.shape[1] // 2, lhs.shape[0] // 2
        specs = [vmem()] * 2
    extra = [((2 * tokens, rows), bf16), ((2 * tokens, 2 * rank), bf16)] if first else []
    return pl.pallas_call(
        functools.partial(forward_kernel, tokens, rank, vs, later is None),
        in_specs=[pl.BlockSpec(memory_space=pltpu.SMEM), *specs] + [vmem()] * (1 + len(held)),
        out_specs=[vmem()] * (1 + len(extra)),
        out_shape=[jax.ShapeDtypeStruct((len(held), 2 * tokens, half), bf16)]
        + [jax.ShapeDtypeStruct(*e) for e in extra],
        scratch_shapes=[pltpu.SemaphoreType.DMA] if first else [],
        compiler_params=params(),
        cost_estimate=small_cost,
        name="forward",
    )(order, *operands, up, *held)


def backward_kernel(tokens, n, start, band, first, order_ref, *refs):
    if first:
        cots, (stats_ref, up_ref, at_ref, *held) = refs[:n], refs[n : 2 * n + 3]
        own_out, other_out, scaled_ref, proj_ref, scales_ref, block_ref = refs[2 * n + 3 :]
    else:
        scaled_ref, proj_ref, at_ref, *held, own_out, other_out = refs
    both = 2 * tokens
    half = held[0].shape[1]
    spans = [slice(k * half, (k + 1) * half) for k in range(n)]

    if first:

        @pl.when(pl.program_id(0) == 0)
        def _():
            projected = jnp.zeros(proj_ref.shape, f32)
            for k in range(n):
                magnitude = jnp.sum(cots[k][both:, :].astype(f32), axis=0, keepdims=True)
                squares = stats_ref[pl.ds(order_ref[n + k], 1), :]
                norm = jnp.sqrt(squares + stability_floor)
                rescale = magnitude / norm
                if k == 0:
                    scales_ref[0:1, :] = norm
                    scales_ref[1:2, :] = rescale
                scaled = (cots[k][:both, :].astype(f32) * rescale).astype(bf16)
                if k == 0:
                    block_ref[...] = scaled
                scaled_ref[:, spans[k]] = scaled
                up = up_ref[:, pl.ds(pl.multiple_of(order_ref[k] * half, half), half)]
                projected = projected + dot(scaled, up, contract_trailing)
            proj_ref[...] = projected

    row = pl.ds(pl.multiple_of((start + pl.program_id(0)) * band, band), band)
    total = adapter_scale * dot(proj_ref[...].astype(bf16), at_ref[:, row])
    for k in range(n):
        total = total + dot(scaled_ref[:, spans[k]], held[k][row, :], contract_trailing)
    own_out[...] = total[:tokens]
    other_out[...] = total[tokens:].astype(bf16)


def backward(order, start, bands, band, at, held, first=None, later=None):
    n = order.shape[0] // 2
    half = held[0].shape[1]
    rank = at.shape[0]
    if later is None:
        cots, stats, up = first
        both = cots[0].shape[0] - pad_rows
        operands = [*cots, stats, up]
        extra = [((both, n * half), bf16), ((both, rank), f32), ((2, half), f32), ((both, half), bf16)]
    else:
        operands, extra = later, []
        both = later[0].shape[0]
    tokens = both // 2
    return pl.pallas_call(
        functools.partial(backward_kernel, tokens, n, start, band, later is None),
        grid=(bands,),
        in_specs=[pl.BlockSpec(memory_space=pltpu.SMEM)] + [vmem()] * (len(operands) + 1 + n),
        out_specs=[pl.BlockSpec((tokens, band), lambda i: (0, i))] * 2 + [vmem()] * len(extra),
        out_shape=[
            jax.ShapeDtypeStruct((tokens, bands * band), f32),
            jax.ShapeDtypeStruct((tokens, bands * band), bf16),
        ]
        + [jax.ShapeDtypeStruct(*e) for e in extra],
        compiler_params=params(),
        cost_estimate=small_cost,
        name="backward",
    )(order, *operands, at, *held)


def split_columns(hidden, weight, down, up, magnitude, cotangent):
    n, bits = 8, 3
    tokens = hidden.shape[0]
    half = magnitude.shape[0] // 2
    rows = weight.shape[0]
    me, core = lax.axis_index("tensor"), lax.axis_index("dp")
    swap = lambda x: lax.ppermute(x, "dp", [(0, 1), (1, 0)])
    orders = [[1, 2, 4], [2, 4, 1]]

    def send(x, k):
        pairs = [(2 * t + c, 2 * (t ^ orders[c][k]) + c) for t in range(n) for c in range(2)]
        return lax.ppermute(x, ("tensor", "dp"), pairs)

    def reach(v, c):
        return sum(orders[c][k] for k in range(bits) if v >> (bits - 1 - k) & 1)

    def place(*vs):
        shard = [me ^ jnp.where(core == 0, reach(v, 0), reach(v, 1)) for v in vs]
        return jnp.stack([2 * s + core for s in shard] + shard).astype(jnp.int32)

    tie = lax.optimization_barrier
    at = down.T
    order = place(*range(n))
    low_core = core == 0

    cot_other = swap(cotangent)
    hidden_other = swap(hidden)
    first = lax.reduce_precision(magnitude, 8, 7)
    second = lax.reduce_precision(magnitude - first, 8, 7)
    third = magnitude - first - second
    magnitude_rows = jnp.concatenate(
        [jnp.stack([first, second, third]), jnp.zeros((pad_rows - 3, 2 * half), f32)]
    ).astype(bf16)
    low_core, order, cot_other = tie((low_core, order, cot_other))
    block = own_block(order, cotangent, cot_other, magnitude_rows, at, up, hidden)

    cots = {0b000: block, 0b001: send(block, 2), 0b010: send(block, 1), 0b100: send(block, 0)}

    run_load = functools.partial(load, at=at, up=up, weight=weight, half=half)
    *far, stats = run_load((0b100, 0b101, 0b110, 0b111), order, own=hidden)
    cots[0b100], cots[0b010], cots[0b001], stats = tie((cots[0b100], cots[0b010], cots[0b001], stats))
    cots[0b011] = send(cots[0b001], 1)
    pair = send(jnp.stack([cots[0b001], cots[0b010]]), 0)
    *near, stats = run_load((0b000, 0b001, 0b010, 0b011), order, before=stats)
    cots[0b011], stats = tie((cots[0b011], stats))
    got = send(stats, 0)
    cots[0b111] = send(cots[0b011], 0)
    far1, lhs, adapter = forward((0b110, 0b111), order, far[2:], up, first=(hidden, hidden_other, at))
    run = lambda order, vs, held: forward(vs, order, held, up, later=(lhs, adapter))[0]
    got, pair, cots[0b111], far1, order = tie((got, pair, cots[0b111], far1, order))
    cots[0b101], cots[0b110] = pair[0], pair[1]
    stats = stats + got
    got = send(stats, 1)
    from1 = send(far1, 0)
    far0 = run(order, (0b100, 0b101), far[:2])
    got, far0, order = tie((got, far0, order))
    stats = stats + got
    got = send(stats, 2)
    from0 = send(far0, 0)
    near1 = run(order, (0b010, 0b011), near[2:])
    got, from1, near1, order = tie((got, from1, near1, order))
    stats = stats + got
    arrived = send((near1.astype(f32) + from1.astype(f32)).astype(bf16), 1)
    lowrank_rows = stats[n:]
    lowrank_other = swap(lowrank_rows)
    near0 = run(order, (0b000, 0b001), near[:2])
    from0, lowrank_other, near0, order = tie((from0, lowrank_other, near0, order))
    kept = near0.astype(f32) + from0.astype(f32)
    held = near + far

    band = 256
    bands = rows // band
    many = bands // 2
    run = functools.partial(backward, order, band=band, at=at, held=held)
    grad_a, other_a, scaled, proj, scales, scaled_own = run(0, many, first=([cots[v] for v in range(n)], stats, up))
    got_a = swap(other_a)
    from_sibling = swap(proj)
    arrived, scaled_own = tie((arrived, scaled_own))
    kept = kept + arrived.astype(f32)
    last = send(kept[1].astype(bf16), 2)
    scaled_own = scaled_own.astype(f32)

    def turned(part):
        lanes = half // tokens
        return jnp.concatenate([part[:, j * tokens : (j + 1) * tokens] for j in range(lanes)])

    up_half = adapter_scale * (
        jnp.dot(turned(lowrank_rows), scaled_own[:tokens], precision=lax.Precision.HIGHEST)
        + jnp.dot(turned(lowrank_other), scaled_own[tokens:], precision=lax.Precision.HIGHEST)
    )
    up_other = swap(up_half)
    grad_b, other_b = run(many, bands - many, later=(scaled, proj))
    got_a, from_sibling, up_other, last, other_b = tie((got_a, from_sibling, up_other, last, other_b))
    got_b = swap(other_b)
    hidden_gradient = jnp.concatenate(
        [(own + got.astype(f32)).astype(bf16) for own, got in ((grad_a, got_a), (grad_b, got_b))], axis=1
    )
    proj_own = (proj[:tokens] + from_sibling[tokens:]).astype(bf16)
    proj_other = (proj[tokens:] + from_sibling[:tokens]).astype(bf16)
    down_weight_gradient = adapter_scale * (
        dot(proj_own, hidden, contract_first) + dot(proj_other, hidden_other, contract_first)
    ).T

    norm, rescale = scales[0], scales[1]
    unscaled = kept[0] + last.astype(f32)
    mixed = (unscaled * rescale).astype(bf16)
    magnitude_half = jnp.sum(block[: 2 * tokens].astype(f32) * unscaled, axis=0) / norm

    def join(own, other, axis):
        return jnp.where(low_core, jnp.concatenate([own, other], axis), jnp.concatenate([other, own], axis))

    mixed = join(mixed[:tokens], swap(mixed[tokens:]), 1)
    up_weight_gradient = join(up_half, up_other, 1)
    grad_magnitude = join(magnitude_half, swap(magnitude_half), 0)
    return (mixed, hidden_gradient, down_weight_gradient, up_weight_gradient, grad_magnitude)


def by_tokens(hidden, frozen_down_weight, adapter_down_weight, adapter_up_weight, magnitude, cotangent):
    column_slice = magnitude.shape[0]
    block_offset = lax.axis_index("tensor") * column_slice
    combined_weight = frozen_down_weight.astype(f32) + adapter_scale * dot(adapter_down_weight, adapter_up_weight)
    squares_part = jnp.sum(combined_weight * combined_weight, axis=0)
    squares, reduced_rank_product = lax.psum((squares_part, dot(hidden, adapter_down_weight)), "tensor")
    norm_all = jnp.sqrt(squares + stability_floor)
    column_length_norm = lax.dynamic_slice_in_dim(norm_all, block_offset, column_slice)
    up_weight_columns = lax.dynamic_slice_in_dim(adapter_up_weight, block_offset, column_slice, 1)
    summed_output = lax.psum_scatter(dot(hidden, frozen_down_weight), "tensor", scatter_dimension=1, tiled=True)
    unscaled_output = summed_output + adapter_scale * jnp.dot(
        reduced_rank_product, up_weight_columns.astype(f32), precision=lax.Precision.HIGHEST
    )
    rescale = magnitude / column_length_norm
    mixed = (unscaled_output * rescale).astype(bf16)
    upstream = cotangent.astype(f32)
    scaled_output = (upstream * rescale).astype(bf16)
    magnitude_part = jnp.sum(upstream * unscaled_output, axis=0) / column_length_norm
    block_input = lax.all_gather(scaled_output, "tensor", axis=1, tiled=True)
    projected_output = dot(block_input, adapter_up_weight, contract_trailing).astype(bf16)
    hidden_gradient = dot(block_input, frozen_down_weight, contract_trailing)
    hidden_gradient = hidden_gradient + adapter_scale * dot(projected_output, adapter_down_weight, contract_trailing)
    hidden_gradient = hidden_gradient.astype(bf16)
    down_gradient_piece = adapter_scale * dot(hidden, projected_output, contract_first)
    up_gradient_piece = adapter_scale * lax.dot_general(
        reduced_rank_product, scaled_output.astype(f32), contract_first, precision=lax.Precision.HIGHEST
    )
    pieces = (down_gradient_piece, up_gradient_piece, magnitude_part)
    pieces = [lax.psum(p.astype(bf16), "dp").astype(f32) for p in pieces]
    return (mixed, hidden_gradient, *pieces)


def solution(mesh):
    n = mesh.shape["tensor"]

    def local(hidden, weight, down, up, magnitude, cotangent):
        aligned = magnitude.shape[0] % 256 == 0 and weight.shape[0] % 256 == 0 and hidden.shape[0] % 128 == 0
        if aligned and mesh.shape["dp"] == 2 and n == 8 and down.shape[1] * hidden.shape[0] % (magnitude.shape[0] // 2 * 8) == 0:
            return split_columns(hidden, weight, down, up, magnitude, cotangent)
        return by_tokens(hidden, weight, down, up, magnitude, cotangent)

    in_specs = (
        P(("parts", "dp"), "tensor"),
        P("tensor", None),
        P(("parts", "tensor"), None),
        P("parts", None),
        P(("parts", "tensor")),
        P(("parts", "dp"), "tensor"),
    )
    out_specs = (
        P(("parts", "dp"), "tensor"),
        P(("parts", "dp"), "tensor"),
        P(("parts", "tensor"), None),
        P("parts", "tensor"),
        P(("parts", "tensor")),
    )
    return jax.shard_map(local, mesh=mesh, in_specs=in_specs, out_specs=out_specs, check_vma=False)
```

```python
import functools

import jax
import jax.numpy as jnp
from jax import lax
from jax.experimental import pallas as pl
from jax.experimental.pallas import tpu as pltpu
from jax.sharding import PartitionSpec as P

adapter_scale = 2.0
stability_floor = 1e-06
pad_rows = 16
vmem_bytes = 8 * 1024 * 1024
f32, bf16 = jnp.float32, jnp.bfloat16
small_cost = pl.CostEstimate(flops=1 << 20, bytes_accessed=1 << 20, transcendentals=0)
contract_trailing = (((1,), (1,)), ((), ()))
contract_first = (((0,), (0,)), ((), ()))


def dot(a, b, dims=(((1,), (0,)), ((), ()))):
    return lax.dot_general(a, b, dims, preferred_element_type=f32)


def split_pair(x):
    high = x.astype(bf16)
    return high, (x - high.astype(f32)).astype(bf16)


def sum_of_squares(w_ref):
    rows, width = w_ref.shape
    totals = [jnp.zeros((8, width), f32) for _ in range(2)]
    for i in range(rows // 16):
        w = w_ref[i * 16 : (i + 1) * 16, :].astype(f32)
        w = w * w
        totals[0] = totals[0] + w[:8]
        totals[1] = totals[1] + w[8:]
    return jnp.sum(totals[0] + totals[1], axis=0, keepdims=True)


def vmem():
    return pl.BlockSpec(memory_space=pltpu.VMEM)


def anywhere():
    return pl.BlockSpec(memory_space=pl.ANY)


def params():
    return pltpu.CompilerParams(vmem_limit_bytes=vmem_bytes)


def block_kernel(tokens, order_ref, own_ref, other_ref, magnitude_ref, *refs):
    out_ref = refs[-1]
    out_ref[:tokens, :] = own_ref[...]
    out_ref[tokens : 2 * tokens, :] = other_ref[...]
    out_ref[2 * tokens :, :] = magnitude_ref[...]


def own_block(order, cotangent, other, magnitude_rows, *early):
    tokens, columns = cotangent.shape
    half = columns // 2
    padded = 2 * tokens + pad_rows
    return pl.pallas_call(
        functools.partial(block_kernel, tokens),
        grid_spec=pltpu.PrefetchScalarGridSpec(
            num_scalar_prefetch=1,
            grid=(1,),
            in_specs=[
                pl.BlockSpec((tokens, half), lambda i, p: (0, lax.rem(p[0], 2))),
                pl.BlockSpec((tokens, half), lambda i, p: (0, lax.rem(p[0], 2))),
                pl.BlockSpec((pad_rows, half), lambda i, p: (0, lax.rem(p[0], 2))),
                *[vmem()] * len(early),
            ],
            out_specs=pl.BlockSpec((padded, half), lambda i, p: (0, 0)),
        ),
        out_shape=jax.ShapeDtypeStruct((padded, half), bf16),
        compiler_params=params(),
        cost_estimate=small_cost,
        name="own_block",
    )(order, cotangent, other, magnitude_rows, *early)


def load_kernel(tokens, rank, n, vs, first, order_ref, before_ref, at_ref, up_ref, w_hbm, *refs):
    held, (stats_ref, sem) = refs[: len(vs)], refs[len(vs) :]
    half = held[0].shape[1]
    columns = [pl.ds(pl.multiple_of(order_ref[v] * half, half), half) for v in vs]
    copies = [pltpu.make_async_copy(w_hbm.at[:, c], h, sem.at[k]) for k, (c, h) in enumerate(zip(columns, held))]
    for copy in copies:
        copy.start()

    down = at_ref[...]
    high, low = split_pair(dot(down, down, contract_trailing))
    if first:
        turned = dot(down, before_ref[...], contract_trailing)
        lanes = half // tokens
        span = rank // lanes
        stats_ref[:n, :] = jnp.zeros((n, half), f32)
        for j in range(lanes):
            stats_ref[n:, j * tokens : (j + 1) * tokens] = turned[j * span : (j + 1) * span]
    else:
        stats_ref[...] = before_ref[...]
    for k, v in enumerate(vs):
        copies[k].wait()
        up = up_ref[:, columns[k]]
        cross = 2 * dot(down, held[k][...]) + adapter_scale * (dot(high, up) + dot(low, up))
        cross = jnp.sum(up.astype(f32) * cross, axis=0, keepdims=True)
        stats_ref[pl.ds(order_ref[n + v], 1), :] = sum_of_squares(held[k]) + adapter_scale * cross


def load(vs, order, at, up, weight, half, own=None, before=None):
    n = order.shape[0] // 2
    rank, rows = at.shape
    first = before is None
    tokens = own.shape[0] if first else None
    stats = (n + rank * tokens // half, half) if first else before.shape
    return pl.pallas_call(
        functools.partial(load_kernel, tokens, rank, n, vs, first),
        in_specs=[pl.BlockSpec(memory_space=pltpu.SMEM), vmem(), vmem(), vmem(), anywhere()],
        out_specs=[vmem()] * (len(vs) + 1),
        out_shape=[jax.ShapeDtypeStruct((rows, half), bf16)] * len(vs) + [jax.ShapeDtypeStruct(stats, f32)],
        scratch_shapes=[pltpu.SemaphoreType.DMA((len(vs),))],
        compiler_params=params(),
        cost_estimate=small_cost,
        name="load",
    )(order, own if first else before, at, up, weight)


def forward_kernel(tokens, rank, vs, first, order_ref, *refs):
    if first:
        own_ref, other_ref, at_ref, up_ref, *held, out_ref, lhs_ref, adapter_ref, sem = refs
        copy = pltpu.make_async_copy(other_ref, lhs_ref.at[tokens:], sem)
        copy.start()
        lhs_ref[:tokens, :] = own_ref[...]
        copy.wait()
        high, low = split_pair(dot(lhs_ref[...], at_ref[...], contract_trailing))
        adapter_ref[:, :rank] = high
        adapter_ref[:, rank:] = low
    else:
        lhs_ref, adapter_ref, up_ref, *held, out_ref = refs
    half = out_ref.shape[2]
    for i, v in enumerate(vs):
        up = up_ref[:, pl.ds(pl.multiple_of(order_ref[v] * half, half), half)]
        through = dot(adapter_ref[...], jnp.concatenate([up, up], axis=0))
        out_ref[i] = (dot(lhs_ref[...], held[i][...]) + adapter_scale * through).astype(bf16)


def forward(vs, order, held, up, first=None, later=None):
    rows, half = held[0].shape
    if later is None:
        own, other, at = operands = first
        tokens, rank = own.shape[0], at.shape[0]
        specs = [vmem(), anywhere(), vmem()]
    else:
        lhs, adapter = operands = later
        rank, tokens = adapter.shape[1] // 2, lhs.shape[0] // 2
        specs = [vmem()] * 2
    extra = [((2 * tokens, rows), bf16), ((2 * tokens, 2 * rank), bf16)] if first else []
    return pl.pallas_call(
        functools.partial(forward_kernel, tokens, rank, vs, later is None),
        in_specs=[pl.BlockSpec(memory_space=pltpu.SMEM), *specs] + [vmem()] * (1 + len(held)),
        out_specs=[vmem()] * (1 + len(extra)),
        out_shape=[jax.ShapeDtypeStruct((len(held), 2 * tokens, half), bf16)]
        + [jax.ShapeDtypeStruct(*e) for e in extra],
        scratch_shapes=[pltpu.SemaphoreType.DMA] if first else [],
        compiler_params=params(),
        cost_estimate=small_cost,
        name="forward",
    )(order, *operands, up, *held)


def backward_kernel(tokens, n, start, band, first, order_ref, *refs):
    if first:
        cots, (stats_ref, up_ref, at_ref, *held) = refs[:n], refs[n : 2 * n + 3]
        own_out, other_out, scaled_ref, proj_ref, scales_ref, block_ref = refs[2 * n + 3 :]
    else:
        scaled_ref, proj_ref, at_ref, *held, own_out, other_out = refs
    both = 2 * tokens
    half = held[0].shape[1]
    spans = [slice(k * half, (k + 1) * half) for k in range(n)]

    if first:

        @pl.when(pl.program_id(0) == 0)
        def _():
            projected = jnp.zeros(proj_ref.shape, f32)
            for k in range(n):
                magnitude = jnp.sum(cots[k][both:, :].astype(f32), axis=0, keepdims=True)
                squares = stats_ref[pl.ds(order_ref[n + k], 1), :]
                norm = jnp.sqrt(squares + stability_floor)
                rescale = magnitude / norm
                if k == 0:
                    scales_ref[0:1, :] = norm
                    scales_ref[1:2, :] = rescale
                scaled = (cots[k][:both, :].astype(f32) * rescale).astype(bf16)
                if k == 0:
                    block_ref[...] = scaled
                scaled_ref[:, spans[k]] = scaled
                up = up_ref[:, pl.ds(pl.multiple_of(order_ref[k] * half, half), half)]
                projected = projected + dot(scaled, up, contract_trailing)
            proj_ref[...] = projected

    row = pl.ds(pl.multiple_of((start + pl.program_id(0)) * band, band), band)
    total = adapter_scale * dot(proj_ref[...].astype(bf16), at_ref[:, row])
    for k in range(n):
        total = total + dot(scaled_ref[:, spans[k]], held[k][row, :], contract_trailing)
    own_out[...] = total[:tokens]
    other_out[...] = total[tokens:].astype(bf16)


def backward(order, start, bands, band, at, held, first=None, later=None):
    n = order.shape[0] // 2
    half = held[0].shape[1]
    rank = at.shape[0]
    if later is None:
        cots, stats, up = first
        both = cots[0].shape[0] - pad_rows
        operands = [*cots, stats, up]
        extra = [((both, n * half), bf16), ((both, rank), f32), ((2, half), f32), ((both, half), bf16)]
    else:
        operands, extra = later, []
        both = later[0].shape[0]
    tokens = both // 2
    return pl.pallas_call(
        functools.partial(backward_kernel, tokens, n, start, band, later is None),
        grid=(bands,),
        in_specs=[pl.BlockSpec(memory_space=pltpu.SMEM)] + [vmem()] * (len(operands) + 1 + n),
        out_specs=[pl.BlockSpec((tokens, band), lambda i: (0, i))] * 2 + [vmem()] * len(extra),
        out_shape=[
            jax.ShapeDtypeStruct((tokens, bands * band), f32),
            jax.ShapeDtypeStruct((tokens, bands * band), bf16),
        ]
        + [jax.ShapeDtypeStruct(*e) for e in extra],
        compiler_params=params(),
        cost_estimate=small_cost,
        name="backward",
    )(order, *operands, at, *held)


def core_halves(order_ref, ref, own, other, axis):
    half = own.shape[axis]
    low, high = (slice(None),) * axis + (slice(0, half),), (slice(None),) * axis + (slice(half, 2 * half),)
    core = lax.rem(order_ref[0], 2)

    @pl.when(core == 0)
    def _():
        ref[low] = own
        ref[high] = other

    @pl.when(core == 1)
    def _():
        ref[low] = other
        ref[high] = own


def weights_kernel(tokens, order_ref, proj_ref, from_ref, own_ref, other_ref, up_ref, up_other_ref, down_out, up_out):
    proj_own = (proj_ref[:tokens, :] + from_ref[tokens:, :]).astype(bf16)
    proj_other = (proj_ref[tokens:, :] + from_ref[:tokens, :]).astype(bf16)
    down_out[...] = adapter_scale * (
        dot(proj_own, own_ref[...], contract_first) + dot(proj_other, other_ref[...], contract_first)
    )
    core_halves(order_ref, up_out, up_ref[...], up_other_ref[...], 1)


def tokens_kernel(order_ref, ga_ref, ra_ref, gb_ref, rb_ref, m_ref, m_other_ref, g_ref, g_other_ref, *outs):
    hidden_out, mixed_out, magnitude_out = outs
    tokens, split = ga_ref.shape
    hidden_out[:, :split] = (ga_ref[...] + ra_ref[...].astype(f32)).astype(bf16)
    hidden_out[:, split:] = (gb_ref[...] + rb_ref[...].astype(f32)).astype(bf16)
    core_halves(order_ref, mixed_out, m_ref[:tokens, :], m_other_ref[...], 1)
    rows = g_ref.shape[1] // 128
    stacked = [jnp.concatenate([r[:, i * 128 : (i + 1) * 128] for i in range(rows)]) for r in (g_ref, g_other_ref)]
    core_halves(order_ref, magnitude_out, *stacked, 0)


def finish(kernel, name, out_shape, order, *operands):
    whole = lambda x: pl.BlockSpec(x.shape, lambda i, p: (0,) * len(x.shape))
    return pl.pallas_call(
        kernel,
        grid_spec=pltpu.PrefetchScalarGridSpec(
            num_scalar_prefetch=1,
            grid=(1,),
            in_specs=[vmem()] * len(operands),
            out_specs=[whole(x) for x in out_shape],
        ),
        out_shape=out_shape,
        compiler_params=params(),
        cost_estimate=small_cost,
        name=name,
    )(order, *operands)


def finish_weights(order, proj, from_sibling, own, other, up_half, up_other):
    tokens, rows = own.shape
    rank, half = up_half.shape
    shapes = [jax.ShapeDtypeStruct((rank, rows), f32), jax.ShapeDtypeStruct((rank, 2 * half), f32)]
    kernel = functools.partial(weights_kernel, tokens)
    return finish(kernel, "weights", shapes, order, proj, from_sibling, own, other, up_half, up_other)


def finish_tokens(order, grad_a, got_a, grad_b, got_b, mixed, mixed_other, magnitude, magnitude_other):
    tokens, half = mixed_other.shape
    rows = grad_a.shape[1] + grad_b.shape[1]
    shapes = [
        jax.ShapeDtypeStruct((tokens, rows), bf16),
        jax.ShapeDtypeStruct((tokens, 2 * half), bf16),
        jax.ShapeDtypeStruct((2 * half // 128, 128), f32),
    ]
    operands = (grad_a, got_a, grad_b, got_b, mixed, mixed_other, magnitude, magnitude_other)
    return finish(tokens_kernel, "tokens", shapes, order, *operands)


def split_columns(hidden, weight, down, up, magnitude, cotangent):
    n, bits = 8, 3
    tokens = hidden.shape[0]
    half = magnitude.shape[0] // 2
    rows = weight.shape[0]
    me, core = lax.axis_index("tensor"), lax.axis_index("dp")
    swap = lambda x: lax.ppermute(x, "dp", [(0, 1), (1, 0)])
    orders = [[1, 2, 4], [2, 1, 4]]

    def send(x, k):
        pairs = [(2 * t + c, 2 * (t ^ orders[c][k]) + c) for t in range(n) for c in range(2)]
        return lax.ppermute(x, ("tensor", "dp"), pairs)

    def reach(v, c):
        return sum(orders[c][k] for k in range(bits) if v >> (bits - 1 - k) & 1)

    def place(*vs):
        shard = [me ^ jnp.where(core == 0, reach(v, 0), reach(v, 1)) for v in vs]
        return jnp.stack([2 * s + core for s in shard] + shard).astype(jnp.int32)

    tie = lax.optimization_barrier
    at = down.T
    order = place(*range(n))
    low_core = core == 0

    cot_other = swap(cotangent)
    hidden_other = swap(hidden)
    first = lax.reduce_precision(magnitude, 8, 7)
    second = lax.reduce_precision(magnitude - first, 8, 7)
    third = magnitude - first - second
    magnitude_rows = jnp.concatenate(
        [jnp.stack([first, second, third]), jnp.zeros((pad_rows - 3, 2 * half), f32)]
    ).astype(bf16)
    low_core, order, cot_other = tie((low_core, order, cot_other))
    block = own_block(order, cotangent, cot_other, magnitude_rows)

    cots = {0b000: block, 0b001: send(block, 2), 0b010: send(block, 1), 0b100: send(block, 0)}

    run_load = functools.partial(load, at=at, up=up, weight=weight, half=half)
    block, order = tie((block, order))
    *held, stats = run_load(tuple(range(n)), order, own=hidden)
    near, far = held[: n // 2], held[n // 2 :]
    cots[0b100], cots[0b010], cots[0b001], stats = tie((cots[0b100], cots[0b010], cots[0b001], stats))
    cots[0b011] = send(cots[0b001], 1)
    pair = send(jnp.stack([cots[0b001], cots[0b010]]), 0)
    got = send(stats, 0)
    far1, lhs, adapter = forward((0b110, 0b111), order, far[2:], up, first=(hidden, hidden_other, at))
    run = lambda order, vs, held: forward(vs, order, held, up, later=(lhs, adapter))[0]
    got, cots[0b011], far1, order = tie((got, cots[0b011], far1, order))
    cots[0b111] = send(cots[0b011], 0)
    stats = stats + got
    got = send(stats, 1)
    from1 = send(far1, 0)
    far0 = run(order, (0b100, 0b101), far[:2])
    got, pair, far0, order = tie((got, pair, far0, order))
    cots[0b101], cots[0b110] = pair[0], pair[1]
    stats = stats + got
    got = send(stats, 2)
    from0 = send(far0, 0)
    near1 = run(order, (0b010, 0b011), near[2:])
    got, from1, cots[0b111], near1, order = tie((got, from1, cots[0b111], near1, order))
    stats = stats + got
    arrived = send((near1.astype(f32) + from1.astype(f32)).astype(bf16), 1)
    lowrank_rows = stats[n:]
    lowrank_other = swap(lowrank_rows)
    near0 = run(order, (0b000, 0b001), near[:2])
    near0, order = tie((near0, order))

    band = 256
    bands = rows // band
    many = max(bands * 5 // 14, 1)
    run = functools.partial(backward, order, band=band, at=at, held=held)
    grad_a, other_a, scaled, proj, scales, scaled_own = run(0, many, first=([cots[v] for v in range(n)], stats, up))
    got_a = swap(other_a)
    from_sibling = swap(proj)
    arrived, from0, lowrank_other, scaled_own = tie((arrived, from0, lowrank_other, scaled_own))
    kept = near0.astype(f32) + from0.astype(f32) + arrived.astype(f32)
    last = send(kept[1].astype(bf16), 2)
    scaled_own = scaled_own.astype(f32)

    def turned(part):
        lanes = half // tokens
        return jnp.concatenate([part[:, j * tokens : (j + 1) * tokens] for j in range(lanes)])

    up_half = adapter_scale * (
        jnp.dot(turned(lowrank_rows), scaled_own[:tokens], precision=lax.Precision.HIGHEST)
        + jnp.dot(turned(lowrank_other), scaled_own[tokens:], precision=lax.Precision.HIGHEST)
    )
    up_other = swap(up_half)
    grad_b, other_b = backward(order, many, bands - many, band, at, held, later=(scaled, proj))
    got_a, from_sibling, up_other, last, other_b = tie((got_a, from_sibling, up_other, last, other_b))
    got_b = swap(other_b)

    unscaled = kept[0] + last.astype(f32)
    mixed = (unscaled * scales[1]).astype(bf16)
    magnitude_half = jnp.sum(block[: 2 * tokens].astype(f32) * unscaled, axis=0, keepdims=True) / scales[0:1]
    mixed_other, magnitude_other = swap(mixed[tokens:]), swap(magnitude_half)
    down_weight_gradient, up_weight_gradient = finish_weights(
        order, proj, from_sibling, hidden, hidden_other, up_half, up_other
    )
    hidden_gradient, mixed, grad_magnitude = finish_tokens(
        order, grad_a, got_a, grad_b, got_b, mixed, mixed_other, magnitude_half, magnitude_other
    )
    down_weight_gradient, grad_magnitude = down_weight_gradient.T, grad_magnitude.reshape(2 * half)
    return (mixed, hidden_gradient, down_weight_gradient, up_weight_gradient, grad_magnitude)


def by_tokens(hidden, frozen_down_weight, adapter_down_weight, adapter_up_weight, magnitude, cotangent):
    column_slice = magnitude.shape[0]
    block_offset = lax.axis_index("tensor") * column_slice
    combined_weight = frozen_down_weight.astype(f32) + adapter_scale * dot(adapter_down_weight, adapter_up_weight)
    squares_part = jnp.sum(combined_weight * combined_weight, axis=0)
    squares, reduced_rank_product = lax.psum((squares_part, dot(hidden, adapter_down_weight)), "tensor")
    norm_all = jnp.sqrt(squares + stability_floor)
    column_length_norm = lax.dynamic_slice_in_dim(norm_all, block_offset, column_slice)
    up_weight_columns = lax.dynamic_slice_in_dim(adapter_up_weight, block_offset, column_slice, 1)
    summed_output = lax.psum_scatter(dot(hidden, frozen_down_weight), "tensor", scatter_dimension=1, tiled=True)
    unscaled_output = summed_output + adapter_scale * jnp.dot(
        reduced_rank_product, up_weight_columns.astype(f32), precision=lax.Precision.HIGHEST
    )
    rescale = magnitude / column_length_norm
    mixed = (unscaled_output * rescale).astype(bf16)
    upstream = cotangent.astype(f32)
    scaled_output = (upstream * rescale).astype(bf16)
    magnitude_part = jnp.sum(upstream * unscaled_output, axis=0) / column_length_norm
    block_input = lax.all_gather(scaled_output, "tensor", axis=1, tiled=True)
    projected_output = dot(block_input, adapter_up_weight, contract_trailing).astype(bf16)
    hidden_gradient = dot(block_input, frozen_down_weight, contract_trailing)
    hidden_gradient = hidden_gradient + adapter_scale * dot(projected_output, adapter_down_weight, contract_trailing)
    hidden_gradient = hidden_gradient.astype(bf16)
    down_gradient_piece = adapter_scale * dot(hidden, projected_output, contract_first)
    up_gradient_piece = adapter_scale * lax.dot_general(
        reduced_rank_product, scaled_output.astype(f32), contract_first, precision=lax.Precision.HIGHEST
    )
    pieces = (down_gradient_piece, up_gradient_piece, magnitude_part)
    pieces = [lax.psum(p.astype(bf16), "dp").astype(f32) for p in pieces]
    return (mixed, hidden_gradient, *pieces)


def solution(mesh):
    n = mesh.shape["tensor"]

    def local(hidden, weight, down, up, magnitude, cotangent):
        aligned = magnitude.shape[0] % 256 == 0 and weight.shape[0] % 256 == 0 and hidden.shape[0] % 128 == 0
        if aligned and mesh.shape["dp"] == 2 and n == 8 and down.shape[1] * hidden.shape[0] % (magnitude.shape[0] // 2 * 8) == 0:
            return split_columns(hidden, weight, down, up, magnitude, cotangent)
        return by_tokens(hidden, weight, down, up, magnitude, cotangent)

    in_specs = (
        P(("parts", "dp"), "tensor"),
        P("tensor", None),
        P(("parts", "tensor"), None),
        P("parts", None),
        P(("parts", "tensor")),
        P(("parts", "dp"), "tensor"),
    )
    out_specs = (
        P(("parts", "dp"), "tensor"),
        P(("parts", "dp"), "tensor"),
        P(("parts", "tensor"), None),
        P("parts", "tensor"),
        P(("parts", "tensor")),
    )
    return jax.shard_map(local, mesh=mesh, in_specs=in_specs, out_specs=out_specs, check_vma=False)
```

```python
import functools

import jax
import jax.numpy as jnp
from jax import lax
from jax.experimental import pallas as pl
from jax.experimental.pallas import tpu as pltpu
from jax.sharding import PartitionSpec as P

adapter_scale = 2.0
stability_floor = 1e-06
pad_rows = 16
vmem_bytes = 8 * 1024 * 1024
f32, bf16 = jnp.float32, jnp.bfloat16
small_cost = pl.CostEstimate(flops=0, bytes_accessed=0, transcendentals=0)
contract_trailing = (((1,), (1,)), ((), ()))
contract_first = (((0,), (0,)), ((), ()))


def dot(a, b, dims=(((1,), (0,)), ((), ()))):
    return lax.dot_general(a, b, dims, preferred_element_type=f32)


def split_pair(x):
    high = x.astype(bf16)
    return high, (x - high.astype(f32)).astype(bf16)


def sum_of_squares(w_ref):
    rows, width = w_ref.shape
    totals = [jnp.zeros((8, width), f32) for _ in range(2)]
    for i in range(rows // 16):
        w = w_ref[i * 16 : (i + 1) * 16, :].astype(f32)
        w = w * w
        totals[0] = totals[0] + w[:8]
        totals[1] = totals[1] + w[8:]
    return jnp.sum(totals[0] + totals[1], axis=0, keepdims=True)


def vmem():
    return pl.BlockSpec(memory_space=pltpu.VMEM)


def anywhere():
    return pl.BlockSpec(memory_space=pl.ANY)


def params():
    return pltpu.CompilerParams(vmem_limit_bytes=vmem_bytes)


def block_kernel(tokens, order_ref, own_ref, other_ref, magnitude_ref, *refs):
    out_ref = refs[-1]
    out_ref[:tokens, :] = own_ref[...]
    out_ref[tokens : 2 * tokens, :] = other_ref[...]
    out_ref[2 * tokens :, :] = magnitude_ref[...]


def own_block(order, cotangent, other, magnitude_rows, *early):
    tokens, columns = cotangent.shape
    half = columns // 2
    padded = 2 * tokens + pad_rows
    return pl.pallas_call(
        functools.partial(block_kernel, tokens),
        grid_spec=pltpu.PrefetchScalarGridSpec(
            num_scalar_prefetch=1,
            grid=(1,),
            in_specs=[
                pl.BlockSpec((tokens, half), lambda i, p: (0, lax.rem(p[0], 2))),
                pl.BlockSpec((tokens, half), lambda i, p: (0, lax.rem(p[0], 2))),
                pl.BlockSpec((pad_rows, half), lambda i, p: (0, lax.rem(p[0], 2))),
                *[vmem()] * len(early),
            ],
            out_specs=pl.BlockSpec((padded, half), lambda i, p: (0, 0)),
        ),
        out_shape=jax.ShapeDtypeStruct((padded, half), bf16),
        compiler_params=params(),
        cost_estimate=small_cost,
        name="own_block",
    )(order, cotangent, other, magnitude_rows, *early)


def load_kernel(tokens, rank, n, vs, first, order_ref, before_ref, at_ref, up_ref, w_hbm, *refs):
    held, (stats_ref, sem) = refs[: len(vs)], refs[len(vs) :]
    half = held[0].shape[1]
    columns = [pl.ds(pl.multiple_of(order_ref[v] * half, half), half) for v in vs]
    copies = [pltpu.make_async_copy(w_hbm.at[:, c], h, sem.at[k]) for k, (c, h) in enumerate(zip(columns, held))]
    for copy in copies:
        copy.start()

    down = at_ref[...]
    high, low = split_pair(dot(down, down, contract_trailing))
    if first:
        turned = dot(down, before_ref[...], contract_trailing)
        lanes = half // tokens
        span = rank // lanes
        stats_ref[:n, :] = jnp.zeros((n, half), f32)
        for j in range(lanes):
            stats_ref[n:, j * tokens : (j + 1) * tokens] = turned[j * span : (j + 1) * span]
    else:
        stats_ref[...] = before_ref[...]
    for k, v in enumerate(vs):
        copies[k].wait()
        up = up_ref[:, columns[k]]
        cross = 2 * dot(down, held[k][...]) + adapter_scale * (dot(high, up) + dot(low, up))
        cross = jnp.sum(up.astype(f32) * cross, axis=0, keepdims=True)
        stats_ref[pl.ds(order_ref[n + v], 1), :] = sum_of_squares(held[k]) + adapter_scale * cross


def load(vs, order, at, up, weight, half, own=None, before=None):
    n = order.shape[0] // 2
    rank, rows = at.shape
    first = before is None
    tokens = own.shape[0] if first else None
    stats = (n + rank * tokens // half, half) if first else before.shape
    return pl.pallas_call(
        functools.partial(load_kernel, tokens, rank, n, vs, first),
        in_specs=[pl.BlockSpec(memory_space=pltpu.SMEM), vmem(), vmem(), vmem(), anywhere()],
        out_specs=[vmem()] * (len(vs) + 1),
        out_shape=[jax.ShapeDtypeStruct((rows, half), bf16)] * len(vs) + [jax.ShapeDtypeStruct(stats, f32)],
        scratch_shapes=[pltpu.SemaphoreType.DMA((len(vs),))],
        compiler_params=params(),
        cost_estimate=small_cost,
        name="load",
    )(order, own if first else before, at, up, weight)


def forward_kernel(tokens, rank, vs, first, order_ref, *refs):
    if first:
        own_ref, other_ref, at_ref, up_ref, *held, out_ref, lhs_ref, adapter_ref, sem = refs
        copy = pltpu.make_async_copy(other_ref, lhs_ref.at[tokens:], sem)
        copy.start()
        lhs_ref[:tokens, :] = own_ref[...]
        copy.wait()
        high, low = split_pair(dot(lhs_ref[...], at_ref[...], contract_trailing))
        adapter_ref[:, :rank] = high
        adapter_ref[:, rank:] = low
    else:
        lhs_ref, adapter_ref, up_ref, *held, out_ref = refs
    half = out_ref.shape[2]
    for i, v in enumerate(vs):
        up = up_ref[:, pl.ds(pl.multiple_of(order_ref[v] * half, half), half)]
        through = dot(adapter_ref[...], jnp.concatenate([up, up], axis=0))
        out_ref[i] = (dot(lhs_ref[...], held[i][...]) + adapter_scale * through).astype(bf16)


def forward(vs, order, held, up, first=None, later=None):
    rows, half = held[0].shape
    if later is None:
        own, other, at = operands = first
        tokens, rank = own.shape[0], at.shape[0]
        specs = [vmem(), anywhere(), vmem()]
    else:
        lhs, adapter = operands = later
        rank, tokens = adapter.shape[1] // 2, lhs.shape[0] // 2
        specs = [vmem()] * 2
    extra = [((2 * tokens, rows), bf16), ((2 * tokens, 2 * rank), bf16)] if first else []
    return pl.pallas_call(
        functools.partial(forward_kernel, tokens, rank, vs, later is None),
        in_specs=[pl.BlockSpec(memory_space=pltpu.SMEM), *specs] + [vmem()] * (1 + len(held)),
        out_specs=[vmem()] * (1 + len(extra)),
        out_shape=[jax.ShapeDtypeStruct((len(held), 2 * tokens, half), bf16)]
        + [jax.ShapeDtypeStruct(*e) for e in extra],
        scratch_shapes=[pltpu.SemaphoreType.DMA] if first else [],
        compiler_params=params(),
        cost_estimate=small_cost,
        name="forward",
    )(order, *operands, up, *held)


def backward_kernel(tokens, n, start, band, first, order_ref, *refs):
    if first:
        cots, (stats_ref, up_ref, at_ref, *held) = refs[:n], refs[n : 2 * n + 3]
        own_out, other_out, scaled_ref, proj_ref, scales_ref, block_ref = refs[2 * n + 3 :]
    else:
        scaled_ref, proj_ref, at_ref, *held, own_out, other_out = refs
    both = 2 * tokens
    half = held[0].shape[1]
    spans = [slice(k * half, (k + 1) * half) for k in range(n)]

    if first:

        @pl.when(pl.program_id(0) == 0)
        def _():
            projected = jnp.zeros(proj_ref.shape, f32)
            for k in range(n):
                magnitude = jnp.sum(cots[k][both:, :].astype(f32), axis=0, keepdims=True)
                squares = stats_ref[pl.ds(order_ref[n + k], 1), :]
                norm = jnp.sqrt(squares + stability_floor)
                rescale = magnitude / norm
                if k == 0:
                    scales_ref[0:1, :] = norm
                    scales_ref[1:2, :] = rescale
                scaled = (cots[k][:both, :].astype(f32) * rescale).astype(bf16)
                if k == 0:
                    block_ref[...] = scaled
                scaled_ref[:, spans[k]] = scaled
                up = up_ref[:, pl.ds(pl.multiple_of(order_ref[k] * half, half), half)]
                projected = projected + dot(scaled, up, contract_trailing)
            proj_ref[...] = projected

    row = pl.ds(pl.multiple_of((start + pl.program_id(0)) * band, band), band)
    total = adapter_scale * dot(proj_ref[...].astype(bf16), at_ref[:, row])
    for k in range(n):
        total = total + dot(scaled_ref[:, spans[k]], held[k][row, :], contract_trailing)
    own_out[...] = total[:tokens]
    other_out[...] = total[tokens:].astype(bf16)


def backward(order, start, bands, band, at, held, first=None, later=None):
    n = order.shape[0] // 2
    half = held[0].shape[1]
    rank = at.shape[0]
    if later is None:
        cots, stats, up = first
        both = cots[0].shape[0] - pad_rows
        operands = [*cots, stats, up]
        extra = [((both, n * half), bf16), ((both, rank), f32), ((2, half), f32), ((both, half), bf16)]
    else:
        operands, extra = later, []
        both = later[0].shape[0]
    tokens = both // 2
    return pl.pallas_call(
        functools.partial(backward_kernel, tokens, n, start, band, later is None),
        grid=(bands,),
        in_specs=[pl.BlockSpec(memory_space=pltpu.SMEM)] + [vmem()] * (len(operands) + 1 + n),
        out_specs=[pl.BlockSpec((tokens, band), lambda i: (0, i))] * 2 + [vmem()] * len(extra),
        out_shape=[
            jax.ShapeDtypeStruct((tokens, bands * band), f32),
            jax.ShapeDtypeStruct((tokens, bands * band), bf16),
        ]
        + [jax.ShapeDtypeStruct(*e) for e in extra],
        compiler_params=params(),
        cost_estimate=small_cost,
        name="backward",
    )(order, *operands, at, *held)


def core_halves(order_ref, ref, own, other, axis):
    half = own.shape[axis]
    low, high = (slice(None),) * axis + (slice(0, half),), (slice(None),) * axis + (slice(half, 2 * half),)
    core = lax.rem(order_ref[0], 2)

    @pl.when(core == 0)
    def _():
        ref[low] = own
        ref[high] = other

    @pl.when(core == 1)
    def _():
        ref[low] = other
        ref[high] = own


def weights_kernel(tokens, order_ref, proj_ref, from_ref, own_ref, other_ref, up_ref, up_other_ref, down_out, up_out):
    proj_own = (proj_ref[:tokens, :] + from_ref[tokens:, :]).astype(bf16)
    proj_other = (proj_ref[tokens:, :] + from_ref[:tokens, :]).astype(bf16)
    down_out[...] = adapter_scale * (
        dot(proj_own, own_ref[...], contract_first) + dot(proj_other, other_ref[...], contract_first)
    )
    core_halves(order_ref, up_out, up_ref[...], up_other_ref[...], 1)


def hidden_kernel(order_ref, ga_ref, ra_ref, gb_ref, rb_ref, out_ref):
    split = ga_ref.shape[1]
    out_ref[:, :split] = (ga_ref[...] + ra_ref[...].astype(f32)).astype(bf16)
    out_ref[:, split:] = (gb_ref[...] + rb_ref[...].astype(f32)).astype(bf16)


def mixed_kernel(order_ref, m_ref, m_other_ref, g_ref, g_other_ref, mixed_out, magnitude_out):
    tokens = m_other_ref.shape[0]
    core_halves(order_ref, mixed_out, m_ref[:tokens, :], m_other_ref[...], 1)
    rows = g_ref.shape[1] // 128
    stacked = [jnp.concatenate([r[:, i * 128 : (i + 1) * 128] for i in range(rows)]) for r in (g_ref, g_other_ref)]
    core_halves(order_ref, magnitude_out, *stacked, 0)


def finish(kernel, name, out_shape, order, *operands):
    whole = lambda x: pl.BlockSpec(x.shape, lambda i, p: (0,) * len(x.shape))
    return pl.pallas_call(
        kernel,
        grid_spec=pltpu.PrefetchScalarGridSpec(
            num_scalar_prefetch=1,
            grid=(1,),
            in_specs=[vmem()] * len(operands),
            out_specs=[whole(x) for x in out_shape],
        ),
        out_shape=out_shape,
        compiler_params=params(),
        cost_estimate=small_cost,
        name=name,
    )(order, *operands)


def finish_weights(order, proj, from_sibling, own, other, up_half, up_other):
    tokens, rows = own.shape
    rank, half = up_half.shape
    shapes = [jax.ShapeDtypeStruct((rank, rows), f32), jax.ShapeDtypeStruct((rank, 2 * half), f32)]
    kernel = functools.partial(weights_kernel, tokens)
    return finish(kernel, "weights", shapes, order, proj, from_sibling, own, other, up_half, up_other)


def finish_hidden(order, grad_a, got_a, grad_b, got_b):
    tokens = grad_a.shape[0]
    shape = jax.ShapeDtypeStruct((tokens, grad_a.shape[1] + grad_b.shape[1]), bf16)
    return finish(hidden_kernel, "hidden", [shape], order, grad_a, got_a, grad_b, got_b)[0]


def finish_mixed(order, mixed, mixed_other, magnitude, magnitude_other):
    tokens, half = mixed_other.shape
    shapes = [
        jax.ShapeDtypeStruct((tokens, 2 * half), bf16),
        jax.ShapeDtypeStruct((2 * half // 128, 128), f32),
    ]
    return finish(mixed_kernel, "mixed", shapes, order, mixed, mixed_other, magnitude, magnitude_other)


def split_columns(hidden, weight, down, up, magnitude, cotangent):
    n, bits = 8, 3
    tokens = hidden.shape[0]
    half = magnitude.shape[0] // 2
    rows = weight.shape[0]
    me, core = lax.axis_index("tensor"), lax.axis_index("dp")
    swap = lambda x: lax.ppermute(x, "dp", [(0, 1), (1, 0)])
    orders = [[1, 2, 4], [2, 4, 1]]

    def send(x, k):
        pairs = [(2 * t + c, 2 * (t ^ orders[c][k]) + c) for t in range(n) for c in range(2)]
        return lax.ppermute(x, ("tensor", "dp"), pairs)

    def reach(v, c):
        return sum(orders[c][k] for k in range(bits) if v >> (bits - 1 - k) & 1)

    def place(*vs):
        shard = [me ^ jnp.where(core == 0, reach(v, 0), reach(v, 1)) for v in vs]
        return jnp.stack([2 * s + core for s in shard] + shard).astype(jnp.int32)

    tie = lax.optimization_barrier
    at = down.T
    order = place(*range(n))
    low_core = core == 0

    cot_other = swap(cotangent)
    hidden_other = swap(hidden)
    first = lax.reduce_precision(magnitude, 8, 7)
    second = lax.reduce_precision(magnitude - first, 8, 7)
    third = magnitude - first - second
    magnitude_rows = jnp.concatenate(
        [jnp.stack([first, second, third]), jnp.zeros((pad_rows - 3, 2 * half), f32)]
    ).astype(bf16)
    low_core, order, cot_other = tie((low_core, order, cot_other))
    block = own_block(order, cotangent, cot_other, magnitude_rows)

    cots = {0b000: block, 0b001: send(block, 2), 0b010: send(block, 1), 0b100: send(block, 0)}

    run_load = functools.partial(load, at=at, up=up, weight=weight, half=half)
    block, order = tie((block, order))
    *far_pair, stats = run_load((0b110, 0b111), order, own=hidden)
    cots[0b001], cots[0b010], stats = tie((cots[0b001], cots[0b010], stats))
    cots[0b011] = send(cots[0b001], 1)
    pair = send(jnp.stack([cots[0b001], cots[0b010]]), 0)
    *held, stats = run_load(tuple(range(n - 2)), order, before=stats)
    held = held + far_pair
    near, far = held[: n // 2], held[n // 2 :]
    cots[0b100], cots[0b011], pair, stats = tie((cots[0b100], cots[0b011], pair, stats))
    cots[0b101], cots[0b110] = pair[0], pair[1]
    got = send(stats, 0)
    cots[0b111] = send(cots[0b011], 0)
    far1, lhs, adapter = forward((0b110, 0b111), order, far[2:], up, first=(hidden, hidden_other, at))
    run = lambda order, vs, held: forward(vs, order, held, up, later=(lhs, adapter))[0]
    got, cots[0b111], far1, order = tie((got, cots[0b111], far1, order))
    stats = stats + got
    got = send(stats, 1)
    from1 = send(far1, 0)
    far0 = run(order, (0b100, 0b101), far[:2])
    got, far0, order = tie((got, far0, order))
    stats = stats + got
    got = send(stats, 2)
    from0 = send(far0, 0)
    near1 = run(order, (0b010, 0b011), near[2:])
    got, from1, near1, order = tie((got, from1, near1, order))
    stats = stats + got
    arrived = send((near1.astype(f32) + from1.astype(f32)).astype(bf16), 1)
    lowrank_rows = stats[n:]
    lowrank_other = swap(lowrank_rows)
    near0 = run(order, (0b000, 0b001), near[:2])
    near0, order = tie((near0, order))

    band = 256
    bands = rows // band
    many = max(bands * 5 // 14, 1)
    run = functools.partial(backward, order, band=band, at=at, held=held)
    grad_a, other_a, scaled, proj, scales, scaled_own = run(0, many, first=([cots[v] for v in range(n)], stats, up))
    got_a = swap(other_a)
    from_sibling = swap(proj)
    arrived, from0, lowrank_other, scaled_own = tie((arrived, from0, lowrank_other, scaled_own))
    kept = near0.astype(f32) + from0.astype(f32) + arrived.astype(f32)
    last = send(kept[1].astype(bf16), 2)
    scaled_own = scaled_own.astype(f32)

    def turned(part):
        lanes = half // tokens
        return jnp.concatenate([part[:, j * tokens : (j + 1) * tokens] for j in range(lanes)])

    up_half = adapter_scale * (
        jnp.dot(turned(lowrank_rows), scaled_own[:tokens], precision=lax.Precision.HIGHEST)
        + jnp.dot(turned(lowrank_other), scaled_own[tokens:], precision=lax.Precision.HIGHEST)
    )
    up_other = swap(up_half)
    grad_b, other_b = backward(order, many, bands - many, band, at, held, later=(scaled, proj))
    got_a, from_sibling, up_other, other_b = tie((got_a, from_sibling, up_other, other_b))
    got_b = swap(other_b)

    down_weight_gradient, up_weight_gradient = finish_weights(
        order, proj, from_sibling, hidden, hidden_other, up_half, up_other
    )

    last, down_weight_gradient = tie((last, down_weight_gradient))
    unscaled = kept[0] + last.astype(f32)
    mixed = (unscaled * scales[1]).astype(bf16)
    magnitude_half = jnp.sum(block[: 2 * tokens].astype(f32) * unscaled, axis=0, keepdims=True) / scales[0:1]
    mixed_other, magnitude_other = swap(mixed[tokens:]), swap(magnitude_half)
    hidden_gradient = finish_hidden(order, grad_a, got_a, grad_b, got_b)
    mixed_other, magnitude_other, hidden_gradient = tie((mixed_other, magnitude_other, hidden_gradient))
    mixed, grad_magnitude = finish_mixed(order, mixed, mixed_other, magnitude_half, magnitude_other)
    down_weight_gradient, grad_magnitude = down_weight_gradient.T, grad_magnitude.reshape(2 * half)
    return (mixed, hidden_gradient, down_weight_gradient, up_weight_gradient, grad_magnitude)


def by_tokens(hidden, frozen_down_weight, adapter_down_weight, adapter_up_weight, magnitude, cotangent):
    column_slice = magnitude.shape[0]
    block_offset = lax.axis_index("tensor") * column_slice
    combined_weight = frozen_down_weight.astype(f32) + adapter_scale * dot(adapter_down_weight, adapter_up_weight)
    squares_part = jnp.sum(combined_weight * combined_weight, axis=0)
    squares, reduced_rank_product = lax.psum((squares_part, dot(hidden, adapter_down_weight)), "tensor")
    norm_all = jnp.sqrt(squares + stability_floor)
    column_length_norm = lax.dynamic_slice_in_dim(norm_all, block_offset, column_slice)
    up_weight_columns = lax.dynamic_slice_in_dim(adapter_up_weight, block_offset, column_slice, 1)
    summed_output = lax.psum_scatter(dot(hidden, frozen_down_weight), "tensor", scatter_dimension=1, tiled=True)
    unscaled_output = summed_output + adapter_scale * jnp.dot(
        reduced_rank_product, up_weight_columns.astype(f32), precision=lax.Precision.HIGHEST
    )
    rescale = magnitude / column_length_norm
    mixed = (unscaled_output * rescale).astype(bf16)
    upstream = cotangent.astype(f32)
    scaled_output = (upstream * rescale).astype(bf16)
    magnitude_part = jnp.sum(upstream * unscaled_output, axis=0) / column_length_norm
    block_input = lax.all_gather(scaled_output, "tensor", axis=1, tiled=True)
    projected_output = dot(block_input, adapter_up_weight, contract_trailing).astype(bf16)
    hidden_gradient = dot(block_input, frozen_down_weight, contract_trailing)
    hidden_gradient = hidden_gradient + adapter_scale * dot(projected_output, adapter_down_weight, contract_trailing)
    hidden_gradient = hidden_gradient.astype(bf16)
    down_gradient_piece = adapter_scale * dot(hidden, projected_output, contract_first)
    up_gradient_piece = adapter_scale * lax.dot_general(
        reduced_rank_product, scaled_output.astype(f32), contract_first, precision=lax.Precision.HIGHEST
    )
    pieces = (down_gradient_piece, up_gradient_piece, magnitude_part)
    pieces = [lax.psum(p.astype(bf16), "dp").astype(f32) for p in pieces]
    return (mixed, hidden_gradient, *pieces)


def solution(mesh):
    n = mesh.shape["tensor"]

    def local(hidden, weight, down, up, magnitude, cotangent):
        aligned = magnitude.shape[0] % 256 == 0 and weight.shape[0] % 256 == 0 and hidden.shape[0] % 128 == 0
        if aligned and mesh.shape["dp"] == 2 and n == 8 and down.shape[1] * hidden.shape[0] % (magnitude.shape[0] // 2 * 8) == 0:
            return split_columns(hidden, weight, down, up, magnitude, cotangent)
        return by_tokens(hidden, weight, down, up, magnitude, cotangent)

    in_specs = (
        P(("parts", "dp"), "tensor"),
        P("tensor", None),
        P(("parts", "tensor"), None),
        P("parts", None),
        P(("parts", "tensor")),
        P(("parts", "dp"), "tensor"),
    )
    out_specs = (
        P(("parts", "dp"), "tensor"),
        P(("parts", "dp"), "tensor"),
        P(("parts", "tensor"), None),
        P("parts", "tensor"),
        P(("parts", "tensor")),
    )
    return jax.shard_map(local, mesh=mesh, in_specs=in_specs, out_specs=out_specs, check_vma=False)
```

```python
import functools

import jax
import jax.numpy as jnp
from jax import lax
from jax.experimental import pallas as pl
from jax.experimental.pallas import tpu as pltpu
from jax.sharding import PartitionSpec as P

adapter_scale = 2.0
stability_floor = 1e-06
pad_rows = 16
vmem_bytes = 8 * 1024 * 1024
f32, bf16 = jnp.float32, jnp.bfloat16
small_cost = pl.CostEstimate(flops=0, bytes_accessed=0, transcendentals=0)
contract_trailing = (((1,), (1,)), ((), ()))
contract_first = (((0,), (0,)), ((), ()))


def dot(a, b, dims=(((1,), (0,)), ((), ()))):
    return lax.dot_general(a, b, dims, preferred_element_type=f32)


def split_pair(x):
    high = x.astype(bf16)
    return high, (x - high.astype(f32)).astype(bf16)


def sum_of_squares(w_ref):
    rows, width = w_ref.shape
    totals = [jnp.zeros((8, width), f32) for _ in range(2)]
    for i in range(rows // 16):
        w = w_ref[i * 16 : (i + 1) * 16, :].astype(f32)
        w = w * w
        totals[0] = totals[0] + w[:8]
        totals[1] = totals[1] + w[8:]
    return jnp.sum(totals[0] + totals[1], axis=0, keepdims=True)


def vmem():
    return pl.BlockSpec(memory_space=pltpu.VMEM)


def anywhere():
    return pl.BlockSpec(memory_space=pl.ANY)


def params():
    return pltpu.CompilerParams(vmem_limit_bytes=vmem_bytes)


def block_kernel(tokens, order_ref, own_ref, other_ref, magnitude_ref, *refs):
    out_ref = refs[-1]
    out_ref[:tokens, :] = own_ref[...]
    out_ref[tokens : 2 * tokens, :] = other_ref[...]
    out_ref[2 * tokens :, :] = magnitude_ref[...]


def own_block(order, cotangent, other, magnitude_rows, *early):
    tokens, columns = cotangent.shape
    half = columns // 2
    padded = 2 * tokens + pad_rows
    return pl.pallas_call(
        functools.partial(block_kernel, tokens),
        grid_spec=pltpu.PrefetchScalarGridSpec(
            num_scalar_prefetch=1,
            grid=(1,),
            in_specs=[
                pl.BlockSpec((tokens, half), lambda i, p: (0, lax.rem(p[0], 2))),
                pl.BlockSpec((tokens, half), lambda i, p: (0, lax.rem(p[0], 2))),
                pl.BlockSpec((pad_rows, half), lambda i, p: (0, lax.rem(p[0], 2))),
                *[vmem()] * len(early),
            ],
            out_specs=pl.BlockSpec((padded, half), lambda i, p: (0, 0)),
        ),
        out_shape=jax.ShapeDtypeStruct((padded, half), bf16),
        compiler_params=params(),
        cost_estimate=small_cost,
        name="own_block",
    )(order, cotangent, other, magnitude_rows, *early)


def load_kernel(tokens, rank, n, vs, first, order_ref, before_ref, at_ref, up_ref, w_hbm, *refs):
    held, (stats_ref, sem) = refs[: len(vs)], refs[len(vs) :]
    half = held[0].shape[1]
    columns = [pl.ds(pl.multiple_of(order_ref[v] * half, half), half) for v in vs]
    copies = [pltpu.make_async_copy(w_hbm.at[:, c], h, sem.at[k]) for k, (c, h) in enumerate(zip(columns, held))]
    for copy in copies:
        copy.start()

    down = at_ref[...]
    high, low = split_pair(dot(down, down, contract_trailing))
    if first:
        turned = dot(down, before_ref[...], contract_trailing)
        lanes = half // tokens
        span = rank // lanes
        stats_ref[:n, :] = jnp.zeros((n, half), f32)
        for j in range(lanes):
            stats_ref[n:, j * tokens : (j + 1) * tokens] = turned[j * span : (j + 1) * span]
    else:
        stats_ref[...] = before_ref[...]
    for k, v in enumerate(vs):
        copies[k].wait()
        up = up_ref[:, columns[k]]
        cross = 2 * dot(down, held[k][...]) + adapter_scale * (dot(high, up) + dot(low, up))
        cross = jnp.sum(up.astype(f32) * cross, axis=0, keepdims=True)
        stats_ref[pl.ds(order_ref[n + v], 1), :] = sum_of_squares(held[k]) + adapter_scale * cross


def load(vs, order, at, up, weight, half, own=None, before=None):
    n = order.shape[0] // 2
    rank, rows = at.shape
    first = before is None
    tokens = own.shape[0] if first else None
    stats = (n + rank * tokens // half, half) if first else before.shape
    return pl.pallas_call(
        functools.partial(load_kernel, tokens, rank, n, vs, first),
        in_specs=[pl.BlockSpec(memory_space=pltpu.SMEM), vmem(), vmem(), vmem(), anywhere()],
        out_specs=[vmem()] * (len(vs) + 1),
        out_shape=[jax.ShapeDtypeStruct((rows, half), bf16)] * len(vs) + [jax.ShapeDtypeStruct(stats, f32)],
        scratch_shapes=[pltpu.SemaphoreType.DMA((len(vs),))],
        compiler_params=params(),
        cost_estimate=small_cost,
        name="load",
    )(order, own if first else before, at, up, weight)


def forward_kernel(tokens, rank, vs, first, order_ref, *refs):
    if first:
        own_ref, other_ref, at_ref, up_ref, *held, out_ref, lhs_ref, adapter_ref, sem = refs
        copy = pltpu.make_async_copy(other_ref, lhs_ref.at[tokens:], sem)
        copy.start()
        lhs_ref[:tokens, :] = own_ref[...]
        copy.wait()
        high, low = split_pair(dot(lhs_ref[...], at_ref[...], contract_trailing))
        adapter_ref[:, :rank] = high
        adapter_ref[:, rank:] = low
    else:
        lhs_ref, adapter_ref, up_ref, *held, out_ref = refs
    half = out_ref.shape[2]
    for i, v in enumerate(vs):
        up = up_ref[:, pl.ds(pl.multiple_of(order_ref[v] * half, half), half)]
        through = dot(adapter_ref[...], jnp.concatenate([up, up], axis=0))
        out_ref[i] = (dot(lhs_ref[...], held[i][...]) + adapter_scale * through).astype(bf16)


def forward(vs, order, held, up, first=None, later=None):
    rows, half = held[0].shape
    if later is None:
        own, other, at = operands = first
        tokens, rank = own.shape[0], at.shape[0]
        specs = [vmem(), anywhere(), vmem()]
    else:
        lhs, adapter = operands = later
        rank, tokens = adapter.shape[1] // 2, lhs.shape[0] // 2
        specs = [vmem()] * 2
    extra = [((2 * tokens, rows), bf16), ((2 * tokens, 2 * rank), bf16)] if first else []
    return pl.pallas_call(
        functools.partial(forward_kernel, tokens, rank, vs, later is None),
        in_specs=[pl.BlockSpec(memory_space=pltpu.SMEM), *specs] + [vmem()] * (1 + len(held)),
        out_specs=[vmem()] * (1 + len(extra)),
        out_shape=[jax.ShapeDtypeStruct((len(held), 2 * tokens, half), bf16)]
        + [jax.ShapeDtypeStruct(*e) for e in extra],
        scratch_shapes=[pltpu.SemaphoreType.DMA] if first else [],
        compiler_params=params(),
        cost_estimate=small_cost,
        name="forward",
    )(order, *operands, up, *held)


def backward_kernel(tokens, n, start, band, first, order_ref, *refs):
    if first:
        cots, (stats_ref, up_ref, at_ref, *held) = refs[:n], refs[n : 2 * n + 3]
        own_out, other_out, scaled_ref, proj_ref, scales_ref, block_ref = refs[2 * n + 3 :]
    else:
        scaled_ref, proj_ref, at_ref, *held, own_out, other_out = refs
    both = 2 * tokens
    half = held[0].shape[1]
    spans = [slice(k * half, (k + 1) * half) for k in range(n)]

    if first:

        @pl.when(pl.program_id(0) == 0)
        def _():
            projected = jnp.zeros(proj_ref.shape, f32)
            for k in range(n):
                magnitude = jnp.sum(cots[k][both:, :].astype(f32), axis=0, keepdims=True)
                squares = stats_ref[pl.ds(order_ref[n + k], 1), :]
                norm = jnp.sqrt(squares + stability_floor)
                rescale = magnitude / norm
                if k == 0:
                    scales_ref[0:1, :] = norm
                    scales_ref[1:2, :] = rescale
                scaled = (cots[k][:both, :].astype(f32) * rescale).astype(bf16)
                if k == 0:
                    block_ref[...] = scaled
                scaled_ref[:, spans[k]] = scaled
                up = up_ref[:, pl.ds(pl.multiple_of(order_ref[k] * half, half), half)]
                projected = projected + dot(scaled, up, contract_trailing)
            proj_ref[...] = projected

    row = pl.ds(pl.multiple_of((start + pl.program_id(0)) * band, band), band)
    total = adapter_scale * dot(proj_ref[...].astype(bf16), at_ref[:, row])
    for k in range(n):
        total = total + dot(scaled_ref[:, spans[k]], held[k][row, :], contract_trailing)
    own_out[...] = total[:tokens]
    other_out[...] = total[tokens:].astype(bf16)


def backward(order, start, bands, band, at, held, first=None, later=None):
    n = order.shape[0] // 2
    half = held[0].shape[1]
    rank = at.shape[0]
    if later is None:
        cots, stats, up = first
        both = cots[0].shape[0] - pad_rows
        operands = [*cots, stats, up]
        extra = [((both, n * half), bf16), ((both, rank), f32), ((2, half), f32), ((both, half), bf16)]
    else:
        operands, extra = later, []
        both = later[0].shape[0]
    tokens = both // 2
    return pl.pallas_call(
        functools.partial(backward_kernel, tokens, n, start, band, later is None),
        grid=(bands,),
        in_specs=[pl.BlockSpec(memory_space=pltpu.SMEM)] + [vmem()] * (len(operands) + 1 + n),
        out_specs=[pl.BlockSpec((tokens, band), lambda i: (0, i))] * 2 + [vmem()] * len(extra),
        out_shape=[
            jax.ShapeDtypeStruct((tokens, bands * band), f32),
            jax.ShapeDtypeStruct((tokens, bands * band), bf16),
        ]
        + [jax.ShapeDtypeStruct(*e) for e in extra],
        compiler_params=params(),
        cost_estimate=small_cost,
        name="backward",
    )(order, *operands, at, *held)


def core_halves(order_ref, ref, own, other, axis):
    half = own.shape[axis]
    low, high = (slice(None),) * axis + (slice(0, half),), (slice(None),) * axis + (slice(half, 2 * half),)
    core = lax.rem(order_ref[0], 2)

    @pl.when(core == 0)
    def _():
        ref[low] = own
        ref[high] = other

    @pl.when(core == 1)
    def _():
        ref[low] = other
        ref[high] = own


def weights_kernel(tokens, order_ref, proj_ref, from_ref, own_ref, other_ref, up_ref, up_other_ref, down_out, up_out):
    proj_own = (proj_ref[:tokens, :] + from_ref[tokens:, :]).astype(bf16)
    proj_other = (proj_ref[tokens:, :] + from_ref[:tokens, :]).astype(bf16)
    down_out[...] = adapter_scale * (
        dot(proj_own, own_ref[...], contract_first) + dot(proj_other, other_ref[...], contract_first)
    )
    core_halves(order_ref, up_out, up_ref[...], up_other_ref[...], 1)


def hidden_kernel(order_ref, ga_ref, ra_ref, gb_ref, rb_ref, out_ref):
    split = ga_ref.shape[1]
    out_ref[:, :split] = (ga_ref[...] + ra_ref[...].astype(f32)).astype(bf16)
    out_ref[:, split:] = (gb_ref[...] + rb_ref[...].astype(f32)).astype(bf16)


def mixed_kernel(order_ref, m_ref, m_other_ref, g_ref, g_other_ref, mixed_out, magnitude_out):
    tokens = m_other_ref.shape[0]
    core_halves(order_ref, mixed_out, m_ref[:tokens, :], m_other_ref[...], 1)
    rows = g_ref.shape[1] // 128
    stacked = [jnp.concatenate([r[:, i * 128 : (i + 1) * 128] for i in range(rows)]) for r in (g_ref, g_other_ref)]
    core_halves(order_ref, magnitude_out, *stacked, 0)


def finish(kernel, name, out_shape, order, *operands):
    whole = lambda x: pl.BlockSpec(x.shape, lambda i, p: (0,) * len(x.shape))
    return pl.pallas_call(
        kernel,
        grid_spec=pltpu.PrefetchScalarGridSpec(
            num_scalar_prefetch=1,
            grid=(1,),
            in_specs=[vmem()] * len(operands),
            out_specs=[whole(x) for x in out_shape],
        ),
        out_shape=out_shape,
        compiler_params=params(),
        cost_estimate=small_cost,
        name=name,
    )(order, *operands)


def finish_weights(order, proj, from_sibling, own, other, up_half, up_other):
    tokens, rows = own.shape
    rank, half = up_half.shape
    shapes = [jax.ShapeDtypeStruct((rank, rows), f32), jax.ShapeDtypeStruct((rank, 2 * half), f32)]
    kernel = functools.partial(weights_kernel, tokens)
    return finish(kernel, "weights", shapes, order, proj, from_sibling, own, other, up_half, up_other)


def finish_hidden(order, grad_a, got_a, grad_b, got_b):
    tokens = grad_a.shape[0]
    shape = jax.ShapeDtypeStruct((tokens, grad_a.shape[1] + grad_b.shape[1]), bf16)
    return finish(hidden_kernel, "hidden", [shape], order, grad_a, got_a, grad_b, got_b)[0]


def finish_mixed(order, mixed, mixed_other, magnitude, magnitude_other):
    tokens, half = mixed_other.shape
    shapes = [
        jax.ShapeDtypeStruct((tokens, 2 * half), bf16),
        jax.ShapeDtypeStruct((2 * half // 128, 128), f32),
    ]
    return finish(mixed_kernel, "mixed", shapes, order, mixed, mixed_other, magnitude, magnitude_other)


def split_columns(hidden, weight, down, up, magnitude, cotangent):
    n, bits = 8, 3
    tokens = hidden.shape[0]
    half = magnitude.shape[0] // 2
    rows = weight.shape[0]
    me, core = lax.axis_index("tensor"), lax.axis_index("dp")
    swap = lambda x: lax.ppermute(x, "dp", [(0, 1), (1, 0)])
    orders = [[1, 2, 4], [2, 1, 4]]

    def send(x, k):
        pairs = [(2 * t + c, 2 * (t ^ orders[c][k]) + c) for t in range(n) for c in range(2)]
        return lax.ppermute(x, ("tensor", "dp"), pairs)

    def reach(v, c):
        return sum(orders[c][k] for k in range(bits) if v >> (bits - 1 - k) & 1)

    def place(*vs):
        shard = [me ^ jnp.where(core == 0, reach(v, 0), reach(v, 1)) for v in vs]
        return jnp.stack([2 * s + core for s in shard] + shard).astype(jnp.int32)

    tie = lax.optimization_barrier
    at = down.T
    order = place(*range(n))
    low_core = core == 0

    cot_other = swap(cotangent)
    hidden_other = swap(hidden)
    first = lax.reduce_precision(magnitude, 8, 7)
    second = lax.reduce_precision(magnitude - first, 8, 7)
    third = magnitude - first - second
    magnitude_rows = jnp.concatenate(
        [jnp.stack([first, second, third]), jnp.zeros((pad_rows - 3, 2 * half), f32)]
    ).astype(bf16)
    low_core, order, cot_other = tie((low_core, order, cot_other))
    block = own_block(order, cotangent, cot_other, magnitude_rows)

    cots = {0b000: block, 0b001: send(block, 2), 0b010: send(block, 1), 0b100: send(block, 0)}

    run_load = functools.partial(load, at=at, up=up, weight=weight, half=half)
    block, order = tie((block, order))
    *far, stats = run_load(tuple(range(n // 2, n)), order, own=hidden)
    cots[0b001], cots[0b010], cots[0b100], stats = tie((cots[0b001], cots[0b010], cots[0b100], stats))
    cots[0b011] = send(cots[0b001], 1)
    pair = send(jnp.stack([cots[0b001], cots[0b010]]), 0)
    *near, stats = run_load(tuple(range(n // 2)), order, before=stats)
    held = near + far
    cots[0b011], pair, stats = tie((cots[0b011], pair, stats))
    cots[0b101], cots[0b110] = pair[0], pair[1]
    got = send(stats, 0)
    cots[0b111] = send(cots[0b011], 0)
    far1, lhs, adapter = forward((0b110, 0b111), order, far[2:], up, first=(hidden, hidden_other, at))
    run = lambda order, vs, held: forward(vs, order, held, up, later=(lhs, adapter))[0]
    got, cots[0b111], far1, order = tie((got, cots[0b111], far1, order))
    stats = stats + got
    got = send(stats, 1)
    from1 = send(far1, 0)
    far0 = run(order, (0b100, 0b101), far[:2])
    got, far0, order = tie((got, far0, order))
    stats = stats + got
    got = send(stats, 2)
    from0 = send(far0, 0)
    near1 = run(order, (0b010, 0b011), near[2:])
    got, from1, near1, order = tie((got, from1, near1, order))
    stats = stats + got
    arrived = send((near1.astype(f32) + from1.astype(f32)).astype(bf16), 1)
    lowrank_rows = stats[n:]
    lowrank_other = swap(lowrank_rows)
    near0 = run(order, (0b000, 0b001), near[:2])
    near0, order = tie((near0, order))

    band = 256
    bands = rows // band
    many = max(bands * 5 // 14, 1)
    run = functools.partial(backward, order, band=band, at=at, held=held)
    grad_a, other_a, scaled, proj, scales, scaled_own = run(0, many, first=([cots[v] for v in range(n)], stats, up))
    got_a = swap(other_a)
    from_sibling = swap(proj)
    arrived, from0, lowrank_other, scaled_own = tie((arrived, from0, lowrank_other, scaled_own))
    kept = near0.astype(f32) + from0.astype(f32) + arrived.astype(f32)
    last = send(kept[1].astype(bf16), 2)
    scaled_own = scaled_own.astype(f32)

    def turned(part):
        lanes = half // tokens
        return jnp.concatenate([part[:, j * tokens : (j + 1) * tokens] for j in range(lanes)])

    up_half = adapter_scale * (
        jnp.dot(turned(lowrank_rows), scaled_own[:tokens], precision=lax.Precision.HIGHEST)
        + jnp.dot(turned(lowrank_other), scaled_own[tokens:], precision=lax.Precision.HIGHEST)
    )
    up_other = swap(up_half)
    grad_b, other_b = backward(order, many, bands - many, band, at, held, later=(scaled, proj))
    got_a, from_sibling, up_other, other_b = tie((got_a, from_sibling, up_other, other_b))
    got_b = swap(other_b)

    down_weight_gradient, up_weight_gradient = finish_weights(
        order, proj, from_sibling, hidden, hidden_other, up_half, up_other
    )

    last, down_weight_gradient = tie((last, down_weight_gradient))
    unscaled = kept[0] + last.astype(f32)
    mixed = (unscaled * scales[1]).astype(bf16)
    magnitude_half = jnp.sum(block[: 2 * tokens].astype(f32) * unscaled, axis=0, keepdims=True) / scales[0:1]
    mixed_other, magnitude_other = swap(mixed[tokens:]), swap(magnitude_half)
    hidden_gradient = finish_hidden(order, grad_a, got_a, grad_b, got_b)
    mixed_other, magnitude_other, hidden_gradient = tie((mixed_other, magnitude_other, hidden_gradient))
    mixed, grad_magnitude = finish_mixed(order, mixed, mixed_other, magnitude_half, magnitude_other)
    down_weight_gradient, grad_magnitude = down_weight_gradient.T, grad_magnitude.reshape(2 * half)
    return (mixed, hidden_gradient, down_weight_gradient, up_weight_gradient, grad_magnitude)


def by_tokens(hidden, frozen_down_weight, adapter_down_weight, adapter_up_weight, magnitude, cotangent):
    column_slice = magnitude.shape[0]
    block_offset = lax.axis_index("tensor") * column_slice
    combined_weight = frozen_down_weight.astype(f32) + adapter_scale * dot(adapter_down_weight, adapter_up_weight)
    squares_part = jnp.sum(combined_weight * combined_weight, axis=0)
    squares, reduced_rank_product = lax.psum((squares_part, dot(hidden, adapter_down_weight)), "tensor")
    norm_all = jnp.sqrt(squares + stability_floor)
    column_length_norm = lax.dynamic_slice_in_dim(norm_all, block_offset, column_slice)
    up_weight_columns = lax.dynamic_slice_in_dim(adapter_up_weight, block_offset, column_slice, 1)
    summed_output = lax.psum_scatter(dot(hidden, frozen_down_weight), "tensor", scatter_dimension=1, tiled=True)
    unscaled_output = summed_output + adapter_scale * jnp.dot(
        reduced_rank_product, up_weight_columns.astype(f32), precision=lax.Precision.HIGHEST
    )
    rescale = magnitude / column_length_norm
    mixed = (unscaled_output * rescale).astype(bf16)
    upstream = cotangent.astype(f32)
    scaled_output = (upstream * rescale).astype(bf16)
    magnitude_part = jnp.sum(upstream * unscaled_output, axis=0) / column_length_norm
    block_input = lax.all_gather(scaled_output, "tensor", axis=1, tiled=True)
    projected_output = dot(block_input, adapter_up_weight, contract_trailing).astype(bf16)
    hidden_gradient = dot(block_input, frozen_down_weight, contract_trailing)
    hidden_gradient = hidden_gradient + adapter_scale * dot(projected_output, adapter_down_weight, contract_trailing)
    hidden_gradient = hidden_gradient.astype(bf16)
    down_gradient_piece = adapter_scale * dot(hidden, projected_output, contract_first)
    up_gradient_piece = adapter_scale * lax.dot_general(
        reduced_rank_product, scaled_output.astype(f32), contract_first, precision=lax.Precision.HIGHEST
    )
    pieces = (down_gradient_piece, up_gradient_piece, magnitude_part)
    pieces = [lax.psum(p.astype(bf16), "dp").astype(f32) for p in pieces]
    return (mixed, hidden_gradient, *pieces)


def solution(mesh):
    n = mesh.shape["tensor"]

    def local(hidden, weight, down, up, magnitude, cotangent):
        aligned = magnitude.shape[0] % 256 == 0 and weight.shape[0] % 256 == 0 and hidden.shape[0] % 128 == 0
        if aligned and mesh.shape["dp"] == 2 and n == 8 and down.shape[1] * hidden.shape[0] % (magnitude.shape[0] // 2 * 8) == 0:
            return split_columns(hidden, weight, down, up, magnitude, cotangent)
        return by_tokens(hidden, weight, down, up, magnitude, cotangent)

    in_specs = (
        P(("parts", "dp"), "tensor"),
        P("tensor", None),
        P(("parts", "tensor"), None),
        P("parts", None),
        P(("parts", "tensor")),
        P(("parts", "dp"), "tensor"),
    )
    out_specs = (
        P(("parts", "dp"), "tensor"),
        P(("parts", "dp"), "tensor"),
        P(("parts", "tensor"), None),
        P("parts", "tensor"),
        P(("parts", "tensor")),
    )
    return jax.shard_map(local, mesh=mesh, in_specs=in_specs, out_specs=out_specs, check_vma=False)
```

```python
import functools

import jax
import jax.numpy as jnp
from jax import lax
from jax.experimental import pallas as pl
from jax.experimental.pallas import tpu as pltpu
from jax.sharding import PartitionSpec as P

adapter_scale = 2.0
stability_floor = 1e-06
pad_rows = 16
vmem_bytes = 8 * 1024 * 1024
f32, bf16 = jnp.float32, jnp.bfloat16
small_cost = pl.CostEstimate(flops=0, bytes_accessed=0, transcendentals=0)
contract_trailing = (((1,), (1,)), ((), ()))
contract_first = (((0,), (0,)), ((), ()))


def dot(a, b, dims=(((1,), (0,)), ((), ()))):
    return lax.dot_general(a, b, dims, preferred_element_type=f32)


def split_pair(x):
    high = x.astype(bf16)
    return high, (x - high.astype(f32)).astype(bf16)


def sum_of_squares(w_ref):
    rows, width = w_ref.shape
    totals = [jnp.zeros((8, width), f32) for _ in range(2)]
    for i in range(rows // 16):
        w = w_ref[i * 16 : (i + 1) * 16, :].astype(f32)
        w = w * w
        totals[0] = totals[0] + w[:8]
        totals[1] = totals[1] + w[8:]
    return jnp.sum(totals[0] + totals[1], axis=0, keepdims=True)


def vmem():
    return pl.BlockSpec(memory_space=pltpu.VMEM)


def anywhere():
    return pl.BlockSpec(memory_space=pl.ANY)


def params():
    return pltpu.CompilerParams(vmem_limit_bytes=vmem_bytes)


def block_kernel(tokens, order_ref, own_ref, other_ref, magnitude_ref, *refs):
    out_ref = refs[-1]
    out_ref[:tokens, :] = own_ref[...]
    out_ref[tokens : 2 * tokens, :] = other_ref[...]
    out_ref[2 * tokens :, :] = magnitude_ref[...]


def own_block(order, cotangent, other, magnitude_rows, *early):
    tokens, columns = cotangent.shape
    half = columns // 2
    padded = 2 * tokens + pad_rows
    return pl.pallas_call(
        functools.partial(block_kernel, tokens),
        grid_spec=pltpu.PrefetchScalarGridSpec(
            num_scalar_prefetch=1,
            grid=(1,),
            in_specs=[
                pl.BlockSpec((tokens, half), lambda i, p: (0, lax.rem(p[0], 2))),
                pl.BlockSpec((tokens, half), lambda i, p: (0, lax.rem(p[0], 2))),
                pl.BlockSpec((pad_rows, half), lambda i, p: (0, lax.rem(p[0], 2))),
                *[vmem()] * len(early),
            ],
            out_specs=pl.BlockSpec((padded, half), lambda i, p: (0, 0)),
        ),
        out_shape=jax.ShapeDtypeStruct((padded, half), bf16),
        compiler_params=params(),
        cost_estimate=small_cost,
        name="own_block",
    )(order, cotangent, other, magnitude_rows, *early)


def load_kernel(tokens, rank, n, vs, first, order_ref, before_ref, at_ref, up_ref, w_hbm, *refs):
    held, (stats_ref, sem) = refs[: len(vs)], refs[len(vs) :]
    half = held[0].shape[1]
    columns = [pl.ds(pl.multiple_of(order_ref[v] * half, half), half) for v in vs]
    copies = [pltpu.make_async_copy(w_hbm.at[:, c], h, sem.at[k]) for k, (c, h) in enumerate(zip(columns, held))]
    for copy in copies:
        copy.start()

    down = at_ref[...]
    high, low = split_pair(dot(down, down, contract_trailing))
    if first:
        turned = dot(down, before_ref[...], contract_trailing)
        lanes = half // tokens
        span = rank // lanes
        stats_ref[:n, :] = jnp.zeros((n, half), f32)
        for j in range(lanes):
            stats_ref[n:, j * tokens : (j + 1) * tokens] = turned[j * span : (j + 1) * span]
    else:
        stats_ref[...] = before_ref[...]
    for k, v in enumerate(vs):
        copies[k].wait()
        up = up_ref[:, columns[k]]
        cross = 2 * dot(down, held[k][...]) + adapter_scale * (dot(high, up) + dot(low, up))
        cross = jnp.sum(up.astype(f32) * cross, axis=0, keepdims=True)
        stats_ref[pl.ds(order_ref[n + v], 1), :] = sum_of_squares(held[k]) + adapter_scale * cross


def load(vs, order, at, up, weight, half, own=None, before=None):
    n = order.shape[0] // 2
    rank, rows = at.shape
    first = before is None
    tokens = own.shape[0] if first else None
    stats = (n + rank * tokens // half, half) if first else before.shape
    return pl.pallas_call(
        functools.partial(load_kernel, tokens, rank, n, vs, first),
        in_specs=[pl.BlockSpec(memory_space=pltpu.SMEM), vmem(), vmem(), vmem(), anywhere()],
        out_specs=[vmem()] * (len(vs) + 1),
        out_shape=[jax.ShapeDtypeStruct((rows, half), bf16)] * len(vs) + [jax.ShapeDtypeStruct(stats, f32)],
        scratch_shapes=[pltpu.SemaphoreType.DMA((len(vs),))],
        compiler_params=params(),
        cost_estimate=small_cost,
        name="load",
    )(order, own if first else before, at, up, weight)


def forward_kernel(tokens, rank, vs, first, order_ref, *refs):
    if first:
        own_ref, other_ref, at_ref, up_ref, *held, out_ref, lhs_ref, adapter_ref, sem = refs
        copy = pltpu.make_async_copy(other_ref, lhs_ref.at[tokens:], sem)
        copy.start()
        lhs_ref[:tokens, :] = own_ref[...]
        copy.wait()
        high, low = split_pair(dot(lhs_ref[...], at_ref[...], contract_trailing))
        adapter_ref[:, :rank] = high
        adapter_ref[:, rank:] = low
    else:
        lhs_ref, adapter_ref, up_ref, *held, out_ref = refs
    half = out_ref.shape[2]
    for i, v in enumerate(vs):
        up = up_ref[:, pl.ds(pl.multiple_of(order_ref[v] * half, half), half)]
        through = dot(adapter_ref[...], jnp.concatenate([up, up], axis=0))
        out_ref[i] = (dot(lhs_ref[...], held[i][...]) + adapter_scale * through).astype(bf16)


def forward(vs, order, held, up, first=None, later=None):
    rows, half = held[0].shape
    if later is None:
        own, other, at = operands = first
        tokens, rank = own.shape[0], at.shape[0]
        specs = [vmem(), anywhere(), vmem()]
    else:
        lhs, adapter = operands = later
        rank, tokens = adapter.shape[1] // 2, lhs.shape[0] // 2
        specs = [vmem()] * 2
    extra = [((2 * tokens, rows), bf16), ((2 * tokens, 2 * rank), bf16)] if first else []
    return pl.pallas_call(
        functools.partial(forward_kernel, tokens, rank, vs, later is None),
        in_specs=[pl.BlockSpec(memory_space=pltpu.SMEM), *specs] + [vmem()] * (1 + len(held)),
        out_specs=[vmem()] * (1 + len(extra)),
        out_shape=[jax.ShapeDtypeStruct((len(held), 2 * tokens, half), bf16)]
        + [jax.ShapeDtypeStruct(*e) for e in extra],
        scratch_shapes=[pltpu.SemaphoreType.DMA] if first else [],
        compiler_params=params(),
        cost_estimate=small_cost,
        name="forward",
    )(order, *operands, up, *held)


def backward_kernel(tokens, n, start, band, first, order_ref, *refs):
    if first:
        cots, (stats_ref, up_ref, at_ref, *held) = refs[:n], refs[n : 2 * n + 3]
        own_out, other_out, scaled_ref, proj_ref, scales_ref, block_ref = refs[2 * n + 3 :]
    else:
        scaled_ref, proj_ref, at_ref, *held, own_out, other_out = refs
    both = 2 * tokens
    half = held[0].shape[1]
    spans = [slice(k * half, (k + 1) * half) for k in range(n)]

    if first:

        @pl.when(pl.program_id(0) == 0)
        def _():
            projected = jnp.zeros(proj_ref.shape, f32)
            for k in range(n):
                magnitude = jnp.sum(cots[k][both:, :].astype(f32), axis=0, keepdims=True)
                squares = stats_ref[pl.ds(order_ref[n + k], 1), :]
                norm = jnp.sqrt(squares + stability_floor)
                rescale = magnitude / norm
                if k == 0:
                    scales_ref[0:1, :] = norm
                    scales_ref[1:2, :] = rescale
                scaled = (cots[k][:both, :].astype(f32) * rescale).astype(bf16)
                if k == 0:
                    block_ref[...] = scaled
                scaled_ref[:, spans[k]] = scaled
                up = up_ref[:, pl.ds(pl.multiple_of(order_ref[k] * half, half), half)]
                projected = projected + dot(scaled, up, contract_trailing)
            proj_ref[...] = projected

    row = pl.ds(pl.multiple_of((start + pl.program_id(0)) * band, band), band)
    total = adapter_scale * dot(proj_ref[...].astype(bf16), at_ref[:, row])
    for k in range(n):
        total = total + dot(scaled_ref[:, spans[k]], held[k][row, :], contract_trailing)
    own_out[...] = total[:tokens]
    other_out[...] = total[tokens:].astype(bf16)


def backward(order, start, bands, band, at, held, first=None, later=None):
    n = order.shape[0] // 2
    half = held[0].shape[1]
    rank = at.shape[0]
    if later is None:
        cots, stats, up = first
        both = cots[0].shape[0] - pad_rows
        operands = [*cots, stats, up]
        extra = [((both, n * half), bf16), ((both, rank), f32), ((2, half), f32), ((both, half), bf16)]
    else:
        operands, extra = later, []
        both = later[0].shape[0]
    tokens = both // 2
    return pl.pallas_call(
        functools.partial(backward_kernel, tokens, n, start, band, later is None),
        grid=(bands,),
        in_specs=[pl.BlockSpec(memory_space=pltpu.SMEM)] + [vmem()] * (len(operands) + 1 + n),
        out_specs=[pl.BlockSpec((tokens, band), lambda i: (0, i))] * 2 + [vmem()] * len(extra),
        out_shape=[
            jax.ShapeDtypeStruct((tokens, bands * band), f32),
            jax.ShapeDtypeStruct((tokens, bands * band), bf16),
        ]
        + [jax.ShapeDtypeStruct(*e) for e in extra],
        compiler_params=params(),
        cost_estimate=small_cost,
        name="backward",
    )(order, *operands, at, *held)


def core_halves(order_ref, ref, own, other, axis):
    half = own.shape[axis]
    low, high = (slice(None),) * axis + (slice(0, half),), (slice(None),) * axis + (slice(half, 2 * half),)
    core = lax.rem(order_ref[0], 2)

    @pl.when(core == 0)
    def _():
        ref[low] = own
        ref[high] = other

    @pl.when(core == 1)
    def _():
        ref[low] = other
        ref[high] = own


def weights_kernel(tokens, order_ref, proj_ref, from_ref, own_ref, other_ref, up_ref, up_other_ref, down_out, up_out):
    proj_own = (proj_ref[:tokens, :] + from_ref[tokens:, :]).astype(bf16)
    proj_other = (proj_ref[tokens:, :] + from_ref[:tokens, :]).astype(bf16)
    down_out[...] = adapter_scale * (
        dot(proj_own, own_ref[...], contract_first) + dot(proj_other, other_ref[...], contract_first)
    )
    core_halves(order_ref, up_out, up_ref[...], up_other_ref[...], 1)


def hidden_kernel(order_ref, ga_ref, ra_ref, gb_ref, rb_ref, out_ref):
    split = ga_ref.shape[1]
    out_ref[:, :split] = (ga_ref[...] + ra_ref[...].astype(f32)).astype(bf16)
    out_ref[:, split:] = (gb_ref[...] + rb_ref[...].astype(f32)).astype(bf16)


def mixed_kernel(order_ref, m_ref, m_other_ref, g_ref, g_other_ref, mixed_out, magnitude_out):
    tokens = m_other_ref.shape[0]
    core_halves(order_ref, mixed_out, m_ref[:tokens, :], m_other_ref[...], 1)
    rows = g_ref.shape[1] // 128
    stacked = [jnp.concatenate([r[:, i * 128 : (i + 1) * 128] for i in range(rows)]) for r in (g_ref, g_other_ref)]
    core_halves(order_ref, magnitude_out, *stacked, 0)


def finish(kernel, name, out_shape, order, *operands):
    whole = lambda x: pl.BlockSpec(x.shape, lambda i, p: (0,) * len(x.shape))
    return pl.pallas_call(
        kernel,
        grid_spec=pltpu.PrefetchScalarGridSpec(
            num_scalar_prefetch=1,
            grid=(1,),
            in_specs=[vmem()] * len(operands),
            out_specs=[whole(x) for x in out_shape],
        ),
        out_shape=out_shape,
        compiler_params=params(),
        cost_estimate=small_cost,
        name=name,
    )(order, *operands)


def finish_weights(order, proj, from_sibling, own, other, up_half, up_other):
    tokens, rows = own.shape
    rank, half = up_half.shape
    shapes = [jax.ShapeDtypeStruct((rank, rows), f32), jax.ShapeDtypeStruct((rank, 2 * half), f32)]
    kernel = functools.partial(weights_kernel, tokens)
    return finish(kernel, "weights", shapes, order, proj, from_sibling, own, other, up_half, up_other)


def finish_hidden(order, grad_a, got_a, grad_b, got_b):
    tokens = grad_a.shape[0]
    shape = jax.ShapeDtypeStruct((tokens, grad_a.shape[1] + grad_b.shape[1]), bf16)
    return finish(hidden_kernel, "hidden", [shape], order, grad_a, got_a, grad_b, got_b)[0]


def finish_mixed(order, mixed, mixed_other, magnitude, magnitude_other):
    tokens, half = mixed_other.shape
    shapes = [
        jax.ShapeDtypeStruct((tokens, 2 * half), bf16),
        jax.ShapeDtypeStruct((2 * half // 128, 128), f32),
    ]
    return finish(mixed_kernel, "mixed", shapes, order, mixed, mixed_other, magnitude, magnitude_other)


def split_columns(hidden, weight, down, up, magnitude, cotangent):
    n, bits = 8, 3
    tokens = hidden.shape[0]
    half = magnitude.shape[0] // 2
    rows = weight.shape[0]
    me, core = lax.axis_index("tensor"), lax.axis_index("dp")
    swap = lambda x: lax.ppermute(x, "dp", [(0, 1), (1, 0)])
    orders = [[1, 2, 4], [2, 1, 4]]

    def send(x, k):
        pairs = [(2 * t + c, 2 * (t ^ orders[c][k]) + c) for t in range(n) for c in range(2)]
        return lax.ppermute(x, ("tensor", "dp"), pairs)

    def reach(v, c):
        return sum(orders[c][k] for k in range(bits) if v >> (bits - 1 - k) & 1)

    def place(*vs):
        shard = [me ^ jnp.where(core == 0, reach(v, 0), reach(v, 1)) for v in vs]
        return jnp.stack([2 * s + core for s in shard] + shard).astype(jnp.int32)

    tie = lax.optimization_barrier
    at = down.T
    order = place(*range(n))
    low_core = core == 0

    cot_other = swap(cotangent)
    hidden_other = swap(hidden)
    first = lax.reduce_precision(magnitude, 8, 7)
    second = lax.reduce_precision(magnitude - first, 8, 7)
    third = magnitude - first - second
    magnitude_rows = jnp.concatenate(
        [jnp.stack([first, second, third]), jnp.zeros((pad_rows - 3, 2 * half), f32)]
    ).astype(bf16)
    low_core, order, cot_other = tie((low_core, order, cot_other))
    block = own_block(order, cotangent, cot_other, magnitude_rows)

    cots = {0b000: block, 0b001: send(block, 2), 0b010: send(block, 1), 0b100: send(block, 0)}
    across = [(2 * t + c, 2 * (t ^ orders[c][0] ^ orders[c][1]) + c) for t in range(n) for c in range(2)]
    cots[0b110] = lax.ppermute(block, ("tensor", "dp"), across)

    run_load = functools.partial(load, at=at, up=up, weight=weight, half=half)
    block, order = tie((block, order))
    *held, stats = run_load(tuple(range(n)), order, own=hidden)
    near, far = held[: n // 2], held[n // 2 :]
    cots[0b001], cots[0b010], cots[0b100], cots[0b110], stats = tie(
        (cots[0b001], cots[0b010], cots[0b100], cots[0b110], stats)
    )
    cots[0b011], cots[0b101] = send(cots[0b001], 1), send(cots[0b001], 0)
    got = send(stats, 0)
    far1, lhs, adapter = forward((0b110, 0b111), order, far[2:], up, first=(hidden, hidden_other, at))
    run = lambda order, vs, held: forward(vs, order, held, up, later=(lhs, adapter))[0]
    got, cots[0b011], far1, order = tie((got, cots[0b011], far1, order))
    cots[0b111] = send(cots[0b011], 0)
    stats = stats + got
    got = send(stats, 1)
    from1 = send(far1, 0)
    far0 = run(order, (0b100, 0b101), far[:2])
    got, cots[0b101], far0, order = tie((got, cots[0b101], far0, order))
    stats = stats + got
    got = send(stats, 2)
    from0 = send(far0, 0)
    near1 = run(order, (0b010, 0b011), near[2:])
    got, from1, cots[0b111], near1, order = tie((got, from1, cots[0b111], near1, order))
    stats = stats + got
    arrived = send((near1.astype(f32) + from1.astype(f32)).astype(bf16), 1)
    lowrank_rows = stats[n:]
    lowrank_other = swap(lowrank_rows)
    near0 = run(order, (0b000, 0b001), near[:2])
    near0, order = tie((near0, order))

    band = 256
    bands = rows // band
    many = max(bands * 5 // 14, 1)
    run = functools.partial(backward, order, band=band, at=at, held=held)
    grad_a, other_a, scaled, proj, scales, scaled_own = run(0, many, first=([cots[v] for v in range(n)], stats, up))
    got_a = swap(other_a)
    from_sibling = swap(proj)
    arrived, from0, lowrank_other, scaled_own = tie((arrived, from0, lowrank_other, scaled_own))
    kept = near0.astype(f32) + from0.astype(f32) + arrived.astype(f32)
    last = send(kept[1].astype(bf16), 2)
    scaled_own = scaled_own.astype(f32)

    def turned(part):
        lanes = half // tokens
        return jnp.concatenate([part[:, j * tokens : (j + 1) * tokens] for j in range(lanes)])

    up_half = adapter_scale * (
        jnp.dot(turned(lowrank_rows), scaled_own[:tokens], precision=lax.Precision.HIGHEST)
        + jnp.dot(turned(lowrank_other), scaled_own[tokens:], precision=lax.Precision.HIGHEST)
    )
    up_other = swap(up_half)
    grad_b, other_b = backward(order, many, bands - many, band, at, held, later=(scaled, proj))
    got_a, from_sibling, up_other, other_b = tie((got_a, from_sibling, up_other, other_b))
    got_b = swap(other_b)

    down_weight_gradient, up_weight_gradient = finish_weights(
        order, proj, from_sibling, hidden, hidden_other, up_half, up_other
    )

    last, down_weight_gradient = tie((last, down_weight_gradient))
    unscaled = kept[0] + last.astype(f32)
    mixed = (unscaled * scales[1]).astype(bf16)
    magnitude_half = jnp.sum(block[: 2 * tokens].astype(f32) * unscaled, axis=0, keepdims=True) / scales[0:1]
    mixed_other, magnitude_other = swap(mixed[tokens:]), swap(magnitude_half)
    hidden_gradient = finish_hidden(order, grad_a, got_a, grad_b, got_b)
    mixed_other, magnitude_other, hidden_gradient = tie((mixed_other, magnitude_other, hidden_gradient))
    mixed, grad_magnitude = finish_mixed(order, mixed, mixed_other, magnitude_half, magnitude_other)
    down_weight_gradient, grad_magnitude = down_weight_gradient.T, grad_magnitude.reshape(2 * half)
    return (mixed, hidden_gradient, down_weight_gradient, up_weight_gradient, grad_magnitude)


def by_tokens(hidden, frozen_down_weight, adapter_down_weight, adapter_up_weight, magnitude, cotangent):
    column_slice = magnitude.shape[0]
    block_offset = lax.axis_index("tensor") * column_slice
    combined_weight = frozen_down_weight.astype(f32) + adapter_scale * dot(adapter_down_weight, adapter_up_weight)
    squares_part = jnp.sum(combined_weight * combined_weight, axis=0)
    squares, reduced_rank_product = lax.psum((squares_part, dot(hidden, adapter_down_weight)), "tensor")
    norm_all = jnp.sqrt(squares + stability_floor)
    column_length_norm = lax.dynamic_slice_in_dim(norm_all, block_offset, column_slice)
    up_weight_columns = lax.dynamic_slice_in_dim(adapter_up_weight, block_offset, column_slice, 1)
    summed_output = lax.psum_scatter(dot(hidden, frozen_down_weight), "tensor", scatter_dimension=1, tiled=True)
    unscaled_output = summed_output + adapter_scale * jnp.dot(
        reduced_rank_product, up_weight_columns.astype(f32), precision=lax.Precision.HIGHEST
    )
    rescale = magnitude / column_length_norm
    mixed = (unscaled_output * rescale).astype(bf16)
    upstream = cotangent.astype(f32)
    scaled_output = (upstream * rescale).astype(bf16)
    magnitude_part = jnp.sum(upstream * unscaled_output, axis=0) / column_length_norm
    block_input = lax.all_gather(scaled_output, "tensor", axis=1, tiled=True)
    projected_output = dot(block_input, adapter_up_weight, contract_trailing).astype(bf16)
    hidden_gradient = dot(block_input, frozen_down_weight, contract_trailing)
    hidden_gradient = hidden_gradient + adapter_scale * dot(projected_output, adapter_down_weight, contract_trailing)
    hidden_gradient = hidden_gradient.astype(bf16)
    down_gradient_piece = adapter_scale * dot(hidden, projected_output, contract_first)
    up_gradient_piece = adapter_scale * lax.dot_general(
        reduced_rank_product, scaled_output.astype(f32), contract_first, precision=lax.Precision.HIGHEST
    )
    pieces = (down_gradient_piece, up_gradient_piece, magnitude_part)
    pieces = [lax.psum(p.astype(bf16), "dp").astype(f32) for p in pieces]
    return (mixed, hidden_gradient, *pieces)


def solution(mesh):
    n = mesh.shape["tensor"]

    def local(hidden, weight, down, up, magnitude, cotangent):
        aligned = magnitude.shape[0] % 256 == 0 and weight.shape[0] % 256 == 0 and hidden.shape[0] % 128 == 0
        if aligned and mesh.shape["dp"] == 2 and n == 8 and down.shape[1] * hidden.shape[0] % (magnitude.shape[0] // 2 * 8) == 0:
            return split_columns(hidden, weight, down, up, magnitude, cotangent)
        return by_tokens(hidden, weight, down, up, magnitude, cotangent)

    in_specs = (
        P(("parts", "dp"), "tensor"),
        P("tensor", None),
        P(("parts", "tensor"), None),
        P("parts", None),
        P(("parts", "tensor")),
        P(("parts", "dp"), "tensor"),
    )
    out_specs = (
        P(("parts", "dp"), "tensor"),
        P(("parts", "dp"), "tensor"),
        P(("parts", "tensor"), None),
        P("parts", "tensor"),
        P(("parts", "tensor")),
    )
    return jax.shard_map(local, mesh=mesh, in_specs=in_specs, out_specs=out_specs, check_vma=False)
```

```python
import functools

import jax
import jax.numpy as jnp
from jax import lax
from jax.experimental import pallas as pl
from jax.experimental.pallas import tpu as pltpu
from jax.sharding import PartitionSpec as P

adapter_scale = 2.0
stability_floor = 1e-06
pad_rows = 16
vmem_bytes = 8 * 1024 * 1024
f32, bf16 = jnp.float32, jnp.bfloat16
small_cost = pl.CostEstimate(flops=0, bytes_accessed=0, transcendentals=0)
contract_trailing = (((1,), (1,)), ((), ()))
contract_first = (((0,), (0,)), ((), ()))


def dot(a, b, dims=(((1,), (0,)), ((), ()))):
    return lax.dot_general(a, b, dims, preferred_element_type=f32)


def split_pair(x):
    high = x.astype(bf16)
    return high, (x - high.astype(f32)).astype(bf16)


def sum_of_squares(w_ref):
    rows, width = w_ref.shape
    totals = [jnp.zeros((8, width), f32) for _ in range(2)]
    for i in range(rows // 16):
        w = w_ref[i * 16 : (i + 1) * 16, :].astype(f32)
        w = w * w
        totals[0] = totals[0] + w[:8]
        totals[1] = totals[1] + w[8:]
    return jnp.sum(totals[0] + totals[1], axis=0, keepdims=True)


def vmem():
    return pl.BlockSpec(memory_space=pltpu.VMEM)


def anywhere():
    return pl.BlockSpec(memory_space=pl.ANY)


def params():
    return pltpu.CompilerParams(vmem_limit_bytes=vmem_bytes)


def block_kernel(tokens, order_ref, own_ref, other_ref, magnitude_ref, *refs):
    out_ref = refs[-1]
    out_ref[:tokens, :] = own_ref[...]
    out_ref[tokens : 2 * tokens, :] = other_ref[...]
    out_ref[2 * tokens :, :] = magnitude_ref[...]


def own_block(order, cotangent, other, magnitude_rows, *early):
    tokens, columns = cotangent.shape
    half = columns // 2
    padded = 2 * tokens + pad_rows
    return pl.pallas_call(
        functools.partial(block_kernel, tokens),
        grid_spec=pltpu.PrefetchScalarGridSpec(
            num_scalar_prefetch=1,
            grid=(1,),
            in_specs=[
                pl.BlockSpec((tokens, half), lambda i, p: (0, lax.rem(p[0], 2))),
                pl.BlockSpec((tokens, half), lambda i, p: (0, lax.rem(p[0], 2))),
                pl.BlockSpec((pad_rows, half), lambda i, p: (0, lax.rem(p[0], 2))),
                *[vmem()] * len(early),
            ],
            out_specs=pl.BlockSpec((padded, half), lambda i, p: (0, 0)),
        ),
        out_shape=jax.ShapeDtypeStruct((padded, half), bf16),
        compiler_params=params(),
        cost_estimate=small_cost,
        name="own_block",
    )(order, cotangent, other, magnitude_rows, *early)


def load_kernel(tokens, rank, n, vs, first, order_ref, before_ref, at_ref, up_ref, w_hbm, *refs):
    held, (stats_ref, sem) = refs[: len(vs)], refs[len(vs) :]
    half = held[0].shape[1]
    columns = [pl.ds(pl.multiple_of(order_ref[v] * half, half), half) for v in vs]
    copies = [pltpu.make_async_copy(w_hbm.at[:, c], h, sem.at[k]) for k, (c, h) in enumerate(zip(columns, held))]
    for copy in copies:
        copy.start()

    down = at_ref[...]
    high, low = split_pair(dot(down, down, contract_trailing))
    if first:
        turned = dot(down, before_ref[...], contract_trailing)
        lanes = half // tokens
        span = rank // lanes
        stats_ref[:n, :] = jnp.zeros((n, half), f32)
        for j in range(lanes):
            stats_ref[n:, j * tokens : (j + 1) * tokens] = turned[j * span : (j + 1) * span]
    else:
        stats_ref[...] = before_ref[...]
    for k, v in enumerate(vs):
        copies[k].wait()
        up = up_ref[:, columns[k]]
        cross = 2 * dot(down, held[k][...]) + adapter_scale * (dot(high, up) + dot(low, up))
        cross = jnp.sum(up.astype(f32) * cross, axis=0, keepdims=True)
        stats_ref[pl.ds(order_ref[n + v], 1), :] = sum_of_squares(held[k]) + adapter_scale * cross


def load(vs, order, at, up, weight, half, own=None, before=None):
    n = order.shape[0] // 2
    rank, rows = at.shape
    first = before is None
    tokens = own.shape[0] if first else None
    stats = (n + rank * tokens // half, half) if first else before.shape
    return pl.pallas_call(
        functools.partial(load_kernel, tokens, rank, n, vs, first),
        in_specs=[pl.BlockSpec(memory_space=pltpu.SMEM), vmem(), vmem(), vmem(), anywhere()],
        out_specs=[vmem()] * (len(vs) + 1),
        out_shape=[jax.ShapeDtypeStruct((rows, half), bf16)] * len(vs) + [jax.ShapeDtypeStruct(stats, f32)],
        scratch_shapes=[pltpu.SemaphoreType.DMA((len(vs),))],
        compiler_params=params(),
        cost_estimate=small_cost,
        name="load",
    )(order, own if first else before, at, up, weight)


def forward_kernel(tokens, rank, vs, first, order_ref, *refs):
    if first:
        own_ref, other_ref, at_ref, up_ref, *held, out_ref, lhs_ref, adapter_ref, sem = refs
        copy = pltpu.make_async_copy(other_ref, lhs_ref.at[tokens:], sem)
        copy.start()
        lhs_ref[:tokens, :] = own_ref[...]
        copy.wait()
        high, low = split_pair(dot(lhs_ref[...], at_ref[...], contract_trailing))
        adapter_ref[:, :rank] = high
        adapter_ref[:, rank:] = low
    else:
        lhs_ref, adapter_ref, up_ref, *held, out_ref = refs
    half = out_ref.shape[2]
    for i, v in enumerate(vs):
        up = up_ref[:, pl.ds(pl.multiple_of(order_ref[v] * half, half), half)]
        through = dot(adapter_ref[...], jnp.concatenate([up, up], axis=0))
        out_ref[i] = (dot(lhs_ref[...], held[i][...]) + adapter_scale * through).astype(bf16)


def forward(vs, order, held, up, first=None, later=None):
    rows, half = held[0].shape
    if later is None:
        own, other, at = operands = first
        tokens, rank = own.shape[0], at.shape[0]
        specs = [vmem(), anywhere(), vmem()]
    else:
        lhs, adapter = operands = later
        rank, tokens = adapter.shape[1] // 2, lhs.shape[0] // 2
        specs = [vmem()] * 2
    extra = [((2 * tokens, rows), bf16), ((2 * tokens, 2 * rank), bf16)] if first else []
    return pl.pallas_call(
        functools.partial(forward_kernel, tokens, rank, vs, later is None),
        in_specs=[pl.BlockSpec(memory_space=pltpu.SMEM), *specs] + [vmem()] * (1 + len(held)),
        out_specs=[vmem()] * (1 + len(extra)),
        out_shape=[jax.ShapeDtypeStruct((len(held), 2 * tokens, half), bf16)]
        + [jax.ShapeDtypeStruct(*e) for e in extra],
        scratch_shapes=[pltpu.SemaphoreType.DMA] if first else [],
        compiler_params=params(),
        cost_estimate=small_cost,
        name="forward",
    )(order, *operands, up, *held)


def backward_kernel(tokens, n, start, band, first, order_ref, *refs):
    if first:
        cots, (stats_ref, up_ref, at_ref, *held) = refs[:n], refs[n : 2 * n + 3]
        own_out, other_out, scaled_ref, proj_ref, scales_ref, block_ref = refs[2 * n + 3 :]
    else:
        scaled_ref, proj_ref, at_ref, *held, own_out, other_out = refs
    both = 2 * tokens
    half = held[0].shape[1]
    spans = [slice(k * half, (k + 1) * half) for k in range(n)]

    if first:

        @pl.when(pl.program_id(0) == 0)
        def _():
            projected = jnp.zeros(proj_ref.shape, f32)
            for k in range(n):
                magnitude = jnp.sum(cots[k][both:, :].astype(f32), axis=0, keepdims=True)
                squares = stats_ref[pl.ds(order_ref[n + k], 1), :]
                norm = jnp.sqrt(squares + stability_floor)
                rescale = magnitude / norm
                if k == 0:
                    scales_ref[0:1, :] = norm
                    scales_ref[1:2, :] = rescale
                scaled = (cots[k][:both, :].astype(f32) * rescale).astype(bf16)
                if k == 0:
                    block_ref[...] = scaled
                scaled_ref[:, spans[k]] = scaled
                up = up_ref[:, pl.ds(pl.multiple_of(order_ref[k] * half, half), half)]
                projected = projected + dot(scaled, up, contract_trailing)
            proj_ref[...] = projected

    row = pl.ds(pl.multiple_of((start + pl.program_id(0)) * band, band), band)
    total = adapter_scale * dot(proj_ref[...].astype(bf16), at_ref[:, row])
    for k in range(n):
        total = total + dot(scaled_ref[:, spans[k]], held[k][row, :], contract_trailing)
    own_out[...] = total[:tokens]
    other_out[...] = total[tokens:].astype(bf16)


def backward(order, start, bands, band, at, held, first=None, later=None):
    n = order.shape[0] // 2
    half = held[0].shape[1]
    rank = at.shape[0]
    if later is None:
        cots, stats, up = first
        both = cots[0].shape[0] - pad_rows
        operands = [*cots, stats, up]
        extra = [((both, n * half), bf16), ((both, rank), f32), ((2, half), f32), ((both, half), bf16)]
    else:
        operands, extra = later, []
        both = later[0].shape[0]
    tokens = both // 2
    return pl.pallas_call(
        functools.partial(backward_kernel, tokens, n, start, band, later is None),
        grid=(bands,),
        in_specs=[pl.BlockSpec(memory_space=pltpu.SMEM)] + [vmem()] * (len(operands) + 1 + n),
        out_specs=[pl.BlockSpec((tokens, band), lambda i: (0, i))] * 2 + [vmem()] * len(extra),
        out_shape=[
            jax.ShapeDtypeStruct((tokens, bands * band), f32),
            jax.ShapeDtypeStruct((tokens, bands * band), bf16),
        ]
        + [jax.ShapeDtypeStruct(*e) for e in extra],
        compiler_params=params(),
        cost_estimate=small_cost,
        name="backward",
    )(order, *operands, at, *held)


def core_halves(order_ref, ref, own, other, axis):
    half = own.shape[axis]
    low, high = (slice(None),) * axis + (slice(0, half),), (slice(None),) * axis + (slice(half, 2 * half),)
    core = lax.rem(order_ref[0], 2)

    @pl.when(core == 0)
    def _():
        ref[low] = own
        ref[high] = other

    @pl.when(core == 1)
    def _():
        ref[low] = other
        ref[high] = own


def weights_kernel(tokens, order_ref, proj_ref, from_ref, own_ref, other_ref, up_ref, up_other_ref, down_out, up_out):
    proj_own = (proj_ref[:tokens, :] + from_ref[tokens:, :]).astype(bf16)
    proj_other = (proj_ref[tokens:, :] + from_ref[:tokens, :]).astype(bf16)
    down_out[...] = adapter_scale * (
        dot(proj_own, own_ref[...], contract_first) + dot(proj_other, other_ref[...], contract_first)
    )
    core_halves(order_ref, up_out, up_ref[...], up_other_ref[...], 1)


def hidden_kernel(order_ref, ga_ref, ra_ref, gb_ref, rb_ref, out_ref):
    split = ga_ref.shape[1]
    out_ref[:, :split] = (ga_ref[...] + ra_ref[...].astype(f32)).astype(bf16)
    out_ref[:, split:] = (gb_ref[...] + rb_ref[...].astype(f32)).astype(bf16)


def mixed_kernel(order_ref, m_ref, m_other_ref, g_ref, g_other_ref, mixed_out, magnitude_out):
    tokens = m_other_ref.shape[0]
    core_halves(order_ref, mixed_out, m_ref[:tokens, :], m_other_ref[...], 1)
    rows = g_ref.shape[1] // 128
    stacked = [jnp.concatenate([r[:, i * 128 : (i + 1) * 128] for i in range(rows)]) for r in (g_ref, g_other_ref)]
    core_halves(order_ref, magnitude_out, *stacked, 0)


def finish(kernel, name, out_shape, order, *operands):
    whole = lambda x: pl.BlockSpec(x.shape, lambda i, p: (0,) * len(x.shape))
    return pl.pallas_call(
        kernel,
        grid_spec=pltpu.PrefetchScalarGridSpec(
            num_scalar_prefetch=1,
            grid=(1,),
            in_specs=[vmem()] * len(operands),
            out_specs=[whole(x) for x in out_shape],
        ),
        out_shape=out_shape,
        compiler_params=params(),
        cost_estimate=small_cost,
        name=name,
    )(order, *operands)


def finish_weights(order, proj, from_sibling, own, other, up_half, up_other):
    tokens, rows = own.shape
    rank, half = up_half.shape
    shapes = [jax.ShapeDtypeStruct((rank, rows), f32), jax.ShapeDtypeStruct((rank, 2 * half), f32)]
    kernel = functools.partial(weights_kernel, tokens)
    return finish(kernel, "weights", shapes, order, proj, from_sibling, own, other, up_half, up_other)


def finish_hidden(order, grad_a, got_a, grad_b, got_b):
    tokens = grad_a.shape[0]
    shape = jax.ShapeDtypeStruct((tokens, grad_a.shape[1] + grad_b.shape[1]), bf16)
    return finish(hidden_kernel, "hidden", [shape], order, grad_a, got_a, grad_b, got_b)[0]


def finish_mixed(order, mixed, mixed_other, magnitude, magnitude_other):
    tokens, half = mixed_other.shape
    shapes = [
        jax.ShapeDtypeStruct((tokens, 2 * half), bf16),
        jax.ShapeDtypeStruct((2 * half // 128, 128), f32),
    ]
    return finish(mixed_kernel, "mixed", shapes, order, mixed, mixed_other, magnitude, magnitude_other)


def split_columns(hidden, weight, down, up, magnitude, cotangent):
    n, bits = 8, 3
    tokens = hidden.shape[0]
    half = magnitude.shape[0] // 2
    rows = weight.shape[0]
    me, core = lax.axis_index("tensor"), lax.axis_index("dp")
    swap = lambda x: lax.ppermute(x, "dp", [(0, 1), (1, 0)])
    orders = [[1, 2, 4], [2, 1, 4]]

    def send(x, k):
        pairs = [(2 * t + c, 2 * (t ^ orders[c][k]) + c) for t in range(n) for c in range(2)]
        return lax.ppermute(x, ("tensor", "dp"), pairs)

    def reach(v, c):
        return sum(orders[c][k] for k in range(bits) if v >> (bits - 1 - k) & 1)

    def place(*vs):
        shard = [me ^ jnp.where(core == 0, reach(v, 0), reach(v, 1)) for v in vs]
        return jnp.stack([2 * s + core for s in shard] + shard).astype(jnp.int32)

    tie = lax.optimization_barrier
    at = down.T
    order = place(*range(n))
    low_core = core == 0

    cot_other = swap(cotangent)
    hidden_other = swap(hidden)
    first = lax.reduce_precision(magnitude, 8, 7)
    second = lax.reduce_precision(magnitude - first, 8, 7)
    third = magnitude - first - second
    magnitude_rows = jnp.concatenate(
        [jnp.stack([first, second, third]), jnp.zeros((pad_rows - 3, 2 * half), f32)]
    ).astype(bf16)
    low_core, order, cot_other = tie((low_core, order, cot_other))
    block = own_block(order, cotangent, cot_other, magnitude_rows)

    cots = {0b000: block, 0b001: send(block, 2), 0b010: send(block, 1), 0b100: send(block, 0)}
    across = [(2 * t + c, 2 * (t ^ orders[c][0] ^ orders[c][1]) + c) for t in range(n) for c in range(2)]
    cots[0b110] = lax.ppermute(block, ("tensor", "dp"), across)

    run_load = functools.partial(load, at=at, up=up, weight=weight, half=half)
    block, order = tie((block, order))
    *held, stats = run_load(tuple(range(n)), order, own=hidden)
    near, far = held[: n // 2], held[n // 2 :]
    cots[0b001], cots[0b010], cots[0b100], cots[0b110], stats = tie(
        (cots[0b001], cots[0b010], cots[0b100], cots[0b110], stats)
    )
    cots[0b011], cots[0b101] = send(cots[0b001], 1), send(cots[0b001], 0)
    got = send(stats, 0)
    far1, lhs, adapter = forward((0b110, 0b111), order, far[2:], up, first=(hidden, hidden_other, at))
    run = lambda order, vs, held: forward(vs, order, held, up, later=(lhs, adapter))[0]
    got, cots[0b011], far1, order = tie((got, cots[0b011], far1, order))
    cots[0b111] = send(cots[0b011], 0)
    stats = stats + got
    got = send(stats, 1)
    from1 = send(far1, 0)
    far0 = run(order, (0b100, 0b101), far[:2])
    got, far0, order = tie((got, far0, order))
    stats = stats + got
    got = send(stats, 2)
    from0 = send(far0, 0)
    near1 = run(order, (0b010, 0b011), near[2:])
    got, from1, cots[0b101], cots[0b111], near1, order = tie((got, from1, cots[0b101], cots[0b111], near1, order))
    stats = stats + got
    arrived = send((near1.astype(f32) + from1.astype(f32)).astype(bf16), 1)
    lowrank_rows = stats[n:]
    lowrank_other = swap(lowrank_rows)
    near0 = run(order, (0b000, 0b001), near[:2])
    near0, order = tie((near0, order))

    band = 256
    bands = rows // band
    many = max(bands * 5 // 14, 1)
    run = functools.partial(backward, order, band=band, at=at, held=held)
    grad_a, other_a, scaled, proj, scales, scaled_own = run(0, many, first=([cots[v] for v in range(n)], stats, up))
    got_a = swap(other_a)
    from_sibling = swap(proj)
    arrived, from0, lowrank_other, scaled_own = tie((arrived, from0, lowrank_other, scaled_own))
    kept = near0.astype(f32) + from0.astype(f32) + arrived.astype(f32)
    last = send(kept[1].astype(bf16), 2)
    scaled_own = scaled_own.astype(f32)

    def turned(part):
        lanes = half // tokens
        return jnp.concatenate([part[:, j * tokens : (j + 1) * tokens] for j in range(lanes)])

    up_half = adapter_scale * (
        jnp.dot(turned(lowrank_rows), scaled_own[:tokens], precision=lax.Precision.HIGHEST)
        + jnp.dot(turned(lowrank_other), scaled_own[tokens:], precision=lax.Precision.HIGHEST)
    )
    up_other = swap(up_half)
    grad_b, other_b = backward(order, many, bands - many, band, at, held, later=(scaled, proj))
    got_a, from_sibling, up_other, other_b = tie((got_a, from_sibling, up_other, other_b))
    got_b = swap(other_b)

    down_weight_gradient, up_weight_gradient = finish_weights(
        order, proj, from_sibling, hidden, hidden_other, up_half, up_other
    )

    last, down_weight_gradient = tie((last, down_weight_gradient))
    unscaled = kept[0] + last.astype(f32)
    mixed = (unscaled * scales[1]).astype(bf16)
    magnitude_half = jnp.sum(block[: 2 * tokens].astype(f32) * unscaled, axis=0, keepdims=True) / scales[0:1]
    mixed_other, magnitude_other = swap(mixed[tokens:]), swap(magnitude_half)
    hidden_gradient = finish_hidden(order, grad_a, got_a, grad_b, got_b)
    mixed_other, magnitude_other, hidden_gradient = tie((mixed_other, magnitude_other, hidden_gradient))
    mixed, grad_magnitude = finish_mixed(order, mixed, mixed_other, magnitude_half, magnitude_other)
    down_weight_gradient, grad_magnitude = down_weight_gradient.T, grad_magnitude.reshape(2 * half)
    return (mixed, hidden_gradient, down_weight_gradient, up_weight_gradient, grad_magnitude)


def by_tokens(hidden, frozen_down_weight, adapter_down_weight, adapter_up_weight, magnitude, cotangent):
    column_slice = magnitude.shape[0]
    block_offset = lax.axis_index("tensor") * column_slice
    combined_weight = frozen_down_weight.astype(f32) + adapter_scale * dot(adapter_down_weight, adapter_up_weight)
    squares_part = jnp.sum(combined_weight * combined_weight, axis=0)
    squares, reduced_rank_product = lax.psum((squares_part, dot(hidden, adapter_down_weight)), "tensor")
    norm_all = jnp.sqrt(squares + stability_floor)
    column_length_norm = lax.dynamic_slice_in_dim(norm_all, block_offset, column_slice)
    up_weight_columns = lax.dynamic_slice_in_dim(adapter_up_weight, block_offset, column_slice, 1)
    summed_output = lax.psum_scatter(dot(hidden, frozen_down_weight), "tensor", scatter_dimension=1, tiled=True)
    unscaled_output = summed_output + adapter_scale * jnp.dot(
        reduced_rank_product, up_weight_columns.astype(f32), precision=lax.Precision.HIGHEST
    )
    rescale = magnitude / column_length_norm
    mixed = (unscaled_output * rescale).astype(bf16)
    upstream = cotangent.astype(f32)
    scaled_output = (upstream * rescale).astype(bf16)
    magnitude_part = jnp.sum(upstream * unscaled_output, axis=0) / column_length_norm
    block_input = lax.all_gather(scaled_output, "tensor", axis=1, tiled=True)
    projected_output = dot(block_input, adapter_up_weight, contract_trailing).astype(bf16)
    hidden_gradient = dot(block_input, frozen_down_weight, contract_trailing)
    hidden_gradient = hidden_gradient + adapter_scale * dot(projected_output, adapter_down_weight, contract_trailing)
    hidden_gradient = hidden_gradient.astype(bf16)
    down_gradient_piece = adapter_scale * dot(hidden, projected_output, contract_first)
    up_gradient_piece = adapter_scale * lax.dot_general(
        reduced_rank_product, scaled_output.astype(f32), contract_first, precision=lax.Precision.HIGHEST
    )
    pieces = (down_gradient_piece, up_gradient_piece, magnitude_part)
    pieces = [lax.psum(p.astype(bf16), "dp").astype(f32) for p in pieces]
    return (mixed, hidden_gradient, *pieces)


def solution(mesh):
    n = mesh.shape["tensor"]

    def local(hidden, weight, down, up, magnitude, cotangent):
        aligned = magnitude.shape[0] % 256 == 0 and weight.shape[0] % 256 == 0 and hidden.shape[0] % 128 == 0
        if aligned and mesh.shape["dp"] == 2 and n == 8 and down.shape[1] * hidden.shape[0] % (magnitude.shape[0] // 2 * 8) == 0:
            return split_columns(hidden, weight, down, up, magnitude, cotangent)
        return by_tokens(hidden, weight, down, up, magnitude, cotangent)

    in_specs = (
        P(("parts", "dp"), "tensor"),
        P("tensor", None),
        P(("parts", "tensor"), None),
        P("parts", None),
        P(("parts", "tensor")),
        P(("parts", "dp"), "tensor"),
    )
    out_specs = (
        P(("parts", "dp"), "tensor"),
        P(("parts", "dp"), "tensor"),
        P(("parts", "tensor"), None),
        P("parts", "tensor"),
        P(("parts", "tensor")),
    )
    return jax.shard_map(local, mesh=mesh, in_specs=in_specs, out_specs=out_specs, check_vma=False)
```

```python
import functools

import jax
import jax.numpy as jnp
from jax import lax
from jax.experimental import pallas as pl
from jax.experimental.pallas import tpu as pltpu
from jax.sharding import PartitionSpec as P

adapter_scale = 2.0
stability_floor = 1e-06
pad_rows = 16
vmem_bytes = 8 * 1024 * 1024
f32, bf16 = jnp.float32, jnp.bfloat16
small_cost = pl.CostEstimate(flops=0, bytes_accessed=0, transcendentals=0)
contract_trailing = (((1,), (1,)), ((), ()))
contract_first = (((0,), (0,)), ((), ()))


def dot(a, b, dims=(((1,), (0,)), ((), ()))):
    return lax.dot_general(a, b, dims, preferred_element_type=f32)


def split_pair(x):
    high = x.astype(bf16)
    return high, (x - high.astype(f32)).astype(bf16)


def sum_of_squares(w_ref):
    rows, width = w_ref.shape
    totals = [jnp.zeros((8, width), f32) for _ in range(2)]
    for i in range(rows // 16):
        w = w_ref[i * 16 : (i + 1) * 16, :].astype(f32)
        w = w * w
        totals[0] = totals[0] + w[:8]
        totals[1] = totals[1] + w[8:]
    return jnp.sum(totals[0] + totals[1], axis=0, keepdims=True)


def vmem():
    return pl.BlockSpec(memory_space=pltpu.VMEM)


def anywhere():
    return pl.BlockSpec(memory_space=pl.ANY)


def params():
    return pltpu.CompilerParams(vmem_limit_bytes=vmem_bytes)


def block_kernel(tokens, order_ref, own_ref, other_ref, magnitude_ref, *refs):
    out_ref = refs[-1]
    out_ref[:tokens, :] = own_ref[...]
    out_ref[tokens : 2 * tokens, :] = other_ref[...]
    out_ref[2 * tokens :, :] = magnitude_ref[...]


def own_block(order, cotangent, other, magnitude_rows, *early):
    tokens, columns = cotangent.shape
    half = columns // 2
    padded = 2 * tokens + pad_rows
    return pl.pallas_call(
        functools.partial(block_kernel, tokens),
        grid_spec=pltpu.PrefetchScalarGridSpec(
            num_scalar_prefetch=1,
            grid=(1,),
            in_specs=[
                pl.BlockSpec((tokens, half), lambda i, p: (0, lax.rem(p[0], 2))),
                pl.BlockSpec((tokens, half), lambda i, p: (0, lax.rem(p[0], 2))),
                pl.BlockSpec((pad_rows, half), lambda i, p: (0, lax.rem(p[0], 2))),
                *[vmem()] * len(early),
            ],
            out_specs=pl.BlockSpec((padded, half), lambda i, p: (0, 0)),
        ),
        out_shape=jax.ShapeDtypeStruct((padded, half), bf16),
        compiler_params=params(),
        cost_estimate=small_cost,
        name="own_block",
    )(order, cotangent, other, magnitude_rows, *early)


def load_kernel(tokens, rank, n, vs, first, order_ref, before_ref, at_ref, up_ref, w_hbm, *refs):
    held, (stats_ref, sem) = refs[: len(vs)], refs[len(vs) :]
    half = held[0].shape[1]
    columns = [pl.ds(pl.multiple_of(order_ref[v] * half, half), half) for v in vs]
    copies = [pltpu.make_async_copy(w_hbm.at[:, c], h, sem.at[k]) for k, (c, h) in enumerate(zip(columns, held))]
    for copy in copies:
        copy.start()

    down = at_ref[...]
    high, low = split_pair(dot(down, down, contract_trailing))
    if first:
        turned = dot(down, before_ref[...], contract_trailing)
        lanes = half // tokens
        span = rank // lanes
        stats_ref[:n, :] = jnp.zeros((n, half), f32)
        for j in range(lanes):
            stats_ref[n:, j * tokens : (j + 1) * tokens] = turned[j * span : (j + 1) * span]
    else:
        stats_ref[...] = before_ref[...]
    for k, v in enumerate(vs):
        copies[k].wait()
        up = up_ref[:, columns[k]]
        cross = 2 * dot(down, held[k][...]) + adapter_scale * (dot(high, up) + dot(low, up))
        cross = jnp.sum(up.astype(f32) * cross, axis=0, keepdims=True)
        stats_ref[pl.ds(order_ref[n + v], 1), :] = sum_of_squares(held[k]) + adapter_scale * cross


def load(vs, order, at, up, weight, half, own=None, before=None):
    n = order.shape[0] // 2
    rank, rows = at.shape
    first = before is None
    tokens = own.shape[0] if first else None
    stats = (n + rank * tokens // half, half) if first else before.shape
    return pl.pallas_call(
        functools.partial(load_kernel, tokens, rank, n, vs, first),
        in_specs=[pl.BlockSpec(memory_space=pltpu.SMEM), vmem(), vmem(), vmem(), anywhere()],
        out_specs=[vmem()] * (len(vs) + 1),
        out_shape=[jax.ShapeDtypeStruct((rows, half), bf16)] * len(vs) + [jax.ShapeDtypeStruct(stats, f32)],
        scratch_shapes=[pltpu.SemaphoreType.DMA((len(vs),))],
        compiler_params=params(),
        cost_estimate=small_cost,
        name="load",
    )(order, own if first else before, at, up, weight)


def forward_kernel(tokens, rank, vs, first, order_ref, *refs):
    if first:
        own_ref, other_ref, at_ref, up_ref, *held, out_ref, lhs_ref, adapter_ref, sem = refs
        copy = pltpu.make_async_copy(other_ref, lhs_ref.at[tokens:], sem)
        copy.start()
        lhs_ref[:tokens, :] = own_ref[...]
        copy.wait()
        high, low = split_pair(dot(lhs_ref[...], at_ref[...], contract_trailing))
        adapter_ref[:, :rank] = high
        adapter_ref[:, rank:] = low
    else:
        lhs_ref, adapter_ref, up_ref, *held, out_ref = refs
    half = out_ref.shape[2]
    for i, v in enumerate(vs):
        up = up_ref[:, pl.ds(pl.multiple_of(order_ref[v] * half, half), half)]
        through = dot(adapter_ref[...], jnp.concatenate([up, up], axis=0))
        out_ref[i] = (dot(lhs_ref[...], held[i][...]) + adapter_scale * through).astype(bf16)


def forward(vs, order, held, up, first=None, later=None):
    rows, half = held[0].shape
    if later is None:
        own, other, at = operands = first
        tokens, rank = own.shape[0], at.shape[0]
        specs = [vmem(), anywhere(), vmem()]
    else:
        lhs, adapter = operands = later
        rank, tokens = adapter.shape[1] // 2, lhs.shape[0] // 2
        specs = [vmem()] * 2
    extra = [((2 * tokens, rows), bf16), ((2 * tokens, 2 * rank), bf16)] if first else []
    return pl.pallas_call(
        functools.partial(forward_kernel, tokens, rank, vs, later is None),
        in_specs=[pl.BlockSpec(memory_space=pltpu.SMEM), *specs] + [vmem()] * (1 + len(held)),
        out_specs=[vmem()] * (1 + len(extra)),
        out_shape=[jax.ShapeDtypeStruct((len(held), 2 * tokens, half), bf16)]
        + [jax.ShapeDtypeStruct(*e) for e in extra],
        scratch_shapes=[pltpu.SemaphoreType.DMA] if first else [],
        compiler_params=params(),
        cost_estimate=small_cost,
        name="forward",
    )(order, *operands, up, *held)


def backward_kernel(tokens, n, start, band, first, order_ref, *refs):
    if first:
        cots, (stats_ref, up_ref, at_ref, *held) = refs[:n], refs[n : 2 * n + 3]
        own_out, other_out, scaled_ref, proj_ref, scales_ref, block_ref = refs[2 * n + 3 :]
    else:
        scaled_ref, proj_ref, at_ref, *held, own_out, other_out = refs
    both = 2 * tokens
    half = held[0].shape[1]
    spans = [slice(k * half, (k + 1) * half) for k in range(n)]

    if first:

        @pl.when(pl.program_id(0) == 0)
        def _():
            projected = jnp.zeros(proj_ref.shape, f32)
            for k in range(n):
                magnitude = jnp.sum(cots[k][both:, :].astype(f32), axis=0, keepdims=True)
                squares = stats_ref[pl.ds(order_ref[n + k], 1), :]
                norm = jnp.sqrt(squares + stability_floor)
                rescale = magnitude / norm
                if k == 0:
                    scales_ref[0:1, :] = norm
                    scales_ref[1:2, :] = rescale
                scaled = (cots[k][:both, :].astype(f32) * rescale).astype(bf16)
                if k == 0:
                    block_ref[...] = scaled
                scaled_ref[:, spans[k]] = scaled
                up = up_ref[:, pl.ds(pl.multiple_of(order_ref[k] * half, half), half)]
                projected = projected + dot(scaled, up, contract_trailing)
            proj_ref[...] = projected

    row = pl.ds(pl.multiple_of((start + pl.program_id(0)) * band, band), band)
    total = adapter_scale * dot(proj_ref[...].astype(bf16), at_ref[:, row])
    for k in range(n):
        total = total + dot(scaled_ref[:, spans[k]], held[k][row, :], contract_trailing)
    own_out[...] = total[:tokens]
    other_out[...] = total[tokens:].astype(bf16)


def backward(order, start, bands, band, at, held, first=None, later=None):
    n = order.shape[0] // 2
    half = held[0].shape[1]
    rank = at.shape[0]
    if later is None:
        cots, stats, up = first
        both = cots[0].shape[0] - pad_rows
        operands = [*cots, stats, up]
        extra = [((both, n * half), bf16), ((both, rank), f32), ((2, half), f32), ((both, half), bf16)]
    else:
        operands, extra = later, []
        both = later[0].shape[0]
    tokens = both // 2
    return pl.pallas_call(
        functools.partial(backward_kernel, tokens, n, start, band, later is None),
        grid=(bands,),
        in_specs=[pl.BlockSpec(memory_space=pltpu.SMEM)] + [vmem()] * (len(operands) + 1 + n),
        out_specs=[pl.BlockSpec((tokens, band), lambda i: (0, i))] * 2 + [vmem()] * len(extra),
        out_shape=[
            jax.ShapeDtypeStruct((tokens, bands * band), f32),
            jax.ShapeDtypeStruct((tokens, bands * band), bf16),
        ]
        + [jax.ShapeDtypeStruct(*e) for e in extra],
        compiler_params=params(),
        cost_estimate=small_cost,
        name="backward",
    )(order, *operands, at, *held)


def core_halves(order_ref, ref, own, other, axis):
    half = own.shape[axis]
    low, high = (slice(None),) * axis + (slice(0, half),), (slice(None),) * axis + (slice(half, 2 * half),)
    core = lax.rem(order_ref[0], 2)

    @pl.when(core == 0)
    def _():
        ref[low] = own
        ref[high] = other

    @pl.when(core == 1)
    def _():
        ref[low] = other
        ref[high] = own


def weights_kernel(tokens, order_ref, proj_ref, from_ref, own_ref, other_ref, up_ref, up_other_ref, down_out, up_out):
    proj_own = (proj_ref[:tokens, :] + from_ref[tokens:, :]).astype(bf16)
    proj_other = (proj_ref[tokens:, :] + from_ref[:tokens, :]).astype(bf16)
    down_out[...] = adapter_scale * (
        dot(proj_own, own_ref[...], contract_first) + dot(proj_other, other_ref[...], contract_first)
    )
    core_halves(order_ref, up_out, up_ref[...], up_other_ref[...], 1)


def hidden_kernel(order_ref, ga_ref, ra_ref, gb_ref, rb_ref, out_ref):
    split = ga_ref.shape[1]
    out_ref[:, :split] = (ga_ref[...] + ra_ref[...].astype(f32)).astype(bf16)
    out_ref[:, split:] = (gb_ref[...] + rb_ref[...].astype(f32)).astype(bf16)


def mixed_kernel(order_ref, m_ref, m_other_ref, g_ref, g_other_ref, mixed_out, magnitude_out):
    tokens = m_other_ref.shape[0]
    core_halves(order_ref, mixed_out, m_ref[:tokens, :], m_other_ref[...], 1)
    rows = g_ref.shape[1] // 128
    stacked = [jnp.concatenate([r[:, i * 128 : (i + 1) * 128] for i in range(rows)]) for r in (g_ref, g_other_ref)]
    core_halves(order_ref, magnitude_out, *stacked, 0)


def finish(kernel, name, out_shape, order, *operands):
    whole = lambda x: pl.BlockSpec(x.shape, lambda i, p: (0,) * len(x.shape))
    return pl.pallas_call(
        kernel,
        grid_spec=pltpu.PrefetchScalarGridSpec(
            num_scalar_prefetch=1,
            grid=(1,),
            in_specs=[vmem()] * len(operands),
            out_specs=[whole(x) for x in out_shape],
        ),
        out_shape=out_shape,
        compiler_params=params(),
        cost_estimate=small_cost,
        name=name,
    )(order, *operands)


def finish_weights(order, proj, from_sibling, own, other, up_half, up_other):
    tokens, rows = own.shape
    rank, half = up_half.shape
    shapes = [jax.ShapeDtypeStruct((rank, rows), f32), jax.ShapeDtypeStruct((rank, 2 * half), f32)]
    kernel = functools.partial(weights_kernel, tokens)
    return finish(kernel, "weights", shapes, order, proj, from_sibling, own, other, up_half, up_other)


def finish_hidden(order, grad_a, got_a, grad_b, got_b):
    tokens = grad_a.shape[0]
    shape = jax.ShapeDtypeStruct((tokens, grad_a.shape[1] + grad_b.shape[1]), bf16)
    return finish(hidden_kernel, "hidden", [shape], order, grad_a, got_a, grad_b, got_b)[0]


def finish_mixed(order, mixed, mixed_other, magnitude, magnitude_other):
    tokens, half = mixed_other.shape
    shapes = [
        jax.ShapeDtypeStruct((tokens, 2 * half), bf16),
        jax.ShapeDtypeStruct((2 * half // 128, 128), f32),
    ]
    return finish(mixed_kernel, "mixed", shapes, order, mixed, mixed_other, magnitude, magnitude_other)


def split_columns(hidden, weight, down, up, magnitude, cotangent):
    n, bits = 8, 3
    tokens = hidden.shape[0]
    half = magnitude.shape[0] // 2
    rows = weight.shape[0]
    me, core = lax.axis_index("tensor"), lax.axis_index("dp")
    swap = lambda x: lax.ppermute(x, "dp", [(0, 1), (1, 0)])
    orders = [[1, 2, 4], [2, 1, 4]]

    def send(x, k):
        pairs = [(2 * t + c, 2 * (t ^ orders[c][k]) + c) for t in range(n) for c in range(2)]
        return lax.ppermute(x, ("tensor", "dp"), pairs)

    def reach(v, c):
        return sum(orders[c][k] for k in range(bits) if v >> (bits - 1 - k) & 1)

    def place(*vs):
        shard = [me ^ jnp.where(core == 0, reach(v, 0), reach(v, 1)) for v in vs]
        return jnp.stack([2 * s + core for s in shard] + shard).astype(jnp.int32)

    tie = lax.optimization_barrier
    at = down.T
    order = place(*range(n))
    low_core = core == 0

    cot_other = swap(cotangent)
    hidden_other = swap(hidden)
    first = lax.reduce_precision(magnitude, 8, 7)
    second = lax.reduce_precision(magnitude - first, 8, 7)
    third = magnitude - first - second
    magnitude_rows = jnp.concatenate(
        [jnp.stack([first, second, third]), jnp.zeros((pad_rows - 3, 2 * half), f32)]
    ).astype(bf16)
    low_core, order, cot_other = tie((low_core, order, cot_other))
    block = own_block(order, cotangent, cot_other, magnitude_rows)

    cots = {0b000: block, 0b001: send(block, 2), 0b010: send(block, 1), 0b100: send(block, 0)}
    across = [(2 * t + c, 2 * (t ^ orders[c][0] ^ orders[c][1]) + c) for t in range(n) for c in range(2)]
    cots[0b110] = lax.ppermute(block, ("tensor", "dp"), across)

    run_load = functools.partial(load, at=at, up=up, weight=weight, half=half)
    block, order = tie((block, order))
    *held, stats = run_load(tuple(range(n)), order, own=hidden)
    near, far = held[: n // 2], held[n // 2 :]
    cots[0b001], cots[0b010], cots[0b100], cots[0b110], stats = tie(
        (cots[0b001], cots[0b010], cots[0b100], cots[0b110], stats)
    )
    cots[0b011], cots[0b101] = send(cots[0b001], 1), send(cots[0b001], 0)
    got = send(stats, 0)
    far1, lhs, adapter = forward((0b110, 0b111), order, far[2:], up, first=(hidden, hidden_other, at))
    run = lambda order, vs, held: forward(vs, order, held, up, later=(lhs, adapter))[0]
    got, cots[0b011], far1, order = tie((got, cots[0b011], far1, order))
    cots[0b111] = send(cots[0b011], 0)
    stats = stats + got
    got = send(stats, 1)
    from1 = send(far1, 0)
    far0 = run(order, (0b100, 0b101), far[:2])
    got, far0, order = tie((got, far0, order))
    stats = stats + got
    got = send(stats, 2)
    from0_high, from0_low = send(far0[1], 0), send(far0[0], 0)
    near1 = run(order, (0b010, 0b011), near[2:])
    got, from1, cots[0b101], cots[0b111], near1, order = tie((got, from1, cots[0b101], cots[0b111], near1, order))
    stats = stats + got
    total = (near1.astype(f32) + from1.astype(f32)).astype(bf16)
    high, low = send(total[1], 1), send(total[0], 1)
    lowrank_rows = stats[n:]
    lowrank_other = swap(lowrank_rows)
    near0 = run(order, (0b000, 0b001), near[:2])
    near0, order = tie((near0, order))

    band = 256
    bands = rows // band
    many = max(bands * 3 // 14, 1)
    run = functools.partial(backward, order, band=band, at=at, held=held)
    grad_a, other_a, scaled, proj, scales, scaled_own = run(0, many, first=([cots[v] for v in range(n)], stats, up))
    from_sibling = swap(proj)
    high, from0_high, lowrank_other, scaled_own = tie((high, from0_high, lowrank_other, scaled_own))
    last = send((near0[1].astype(f32) + from0_high.astype(f32) + high.astype(f32)).astype(bf16), 2)
    scaled_own = scaled_own.astype(f32)

    def turned(part):
        lanes = half // tokens
        return jnp.concatenate([part[:, j * tokens : (j + 1) * tokens] for j in range(lanes)])

    up_half = adapter_scale * (
        jnp.dot(turned(lowrank_rows), scaled_own[:tokens], precision=lax.Precision.HIGHEST)
        + jnp.dot(turned(lowrank_other), scaled_own[tokens:], precision=lax.Precision.HIGHEST)
    )
    up_other = swap(up_half)
    grad_b, other_b = backward(order, many, bands - many, band, at, held, later=(scaled, proj))
    other_a, from_sibling, up_other, other_b = tie((other_a, from_sibling, up_other, other_b))
    got_a, got_b = swap(other_a), swap(other_b)

    down_weight_gradient, up_weight_gradient = finish_weights(
        order, proj, from_sibling, hidden, hidden_other, up_half, up_other
    )

    last, low, from0_low, down_weight_gradient = tie((last, low, from0_low, down_weight_gradient))
    unscaled = near0[0].astype(f32) + from0_low.astype(f32) + low.astype(f32) + last.astype(f32)
    mixed = (unscaled * scales[1]).astype(bf16)
    magnitude_half = jnp.sum(block[: 2 * tokens].astype(f32) * unscaled, axis=0, keepdims=True) / scales[0:1]
    mixed_other, magnitude_other = swap(mixed[tokens:]), swap(magnitude_half)
    hidden_gradient = finish_hidden(order, grad_a, got_a, grad_b, got_b)
    mixed_other, magnitude_other, hidden_gradient = tie((mixed_other, magnitude_other, hidden_gradient))
    mixed, grad_magnitude = finish_mixed(order, mixed, mixed_other, magnitude_half, magnitude_other)
    down_weight_gradient, grad_magnitude = down_weight_gradient.T, grad_magnitude.reshape(2 * half)
    return (mixed, hidden_gradient, down_weight_gradient, up_weight_gradient, grad_magnitude)


def by_tokens(hidden, frozen_down_weight, adapter_down_weight, adapter_up_weight, magnitude, cotangent):
    column_slice = magnitude.shape[0]
    block_offset = lax.axis_index("tensor") * column_slice
    combined_weight = frozen_down_weight.astype(f32) + adapter_scale * dot(adapter_down_weight, adapter_up_weight)
    squares_part = jnp.sum(combined_weight * combined_weight, axis=0)
    squares, reduced_rank_product = lax.psum((squares_part, dot(hidden, adapter_down_weight)), "tensor")
    norm_all = jnp.sqrt(squares + stability_floor)
    column_length_norm = lax.dynamic_slice_in_dim(norm_all, block_offset, column_slice)
    up_weight_columns = lax.dynamic_slice_in_dim(adapter_up_weight, block_offset, column_slice, 1)
    summed_output = lax.psum_scatter(dot(hidden, frozen_down_weight), "tensor", scatter_dimension=1, tiled=True)
    unscaled_output = summed_output + adapter_scale * jnp.dot(
        reduced_rank_product, up_weight_columns.astype(f32), precision=lax.Precision.HIGHEST
    )
    rescale = magnitude / column_length_norm
    mixed = (unscaled_output * rescale).astype(bf16)
    upstream = cotangent.astype(f32)
    scaled_output = (upstream * rescale).astype(bf16)
    magnitude_part = jnp.sum(upstream * unscaled_output, axis=0) / column_length_norm
    block_input = lax.all_gather(scaled_output, "tensor", axis=1, tiled=True)
    projected_output = dot(block_input, adapter_up_weight, contract_trailing).astype(bf16)
    hidden_gradient = dot(block_input, frozen_down_weight, contract_trailing)
    hidden_gradient = hidden_gradient + adapter_scale * dot(projected_output, adapter_down_weight, contract_trailing)
    hidden_gradient = hidden_gradient.astype(bf16)
    down_gradient_piece = adapter_scale * dot(hidden, projected_output, contract_first)
    up_gradient_piece = adapter_scale * lax.dot_general(
        reduced_rank_product, scaled_output.astype(f32), contract_first, precision=lax.Precision.HIGHEST
    )
    pieces = (down_gradient_piece, up_gradient_piece, magnitude_part)
    pieces = [lax.psum(p.astype(bf16), "dp").astype(f32) for p in pieces]
    return (mixed, hidden_gradient, *pieces)


def solution(mesh):
    n = mesh.shape["tensor"]

    def local(hidden, weight, down, up, magnitude, cotangent):
        aligned = magnitude.shape[0] % 256 == 0 and weight.shape[0] % 256 == 0 and hidden.shape[0] % 128 == 0
        if aligned and mesh.shape["dp"] == 2 and n == 8 and down.shape[1] * hidden.shape[0] % (magnitude.shape[0] // 2 * 8) == 0:
            return split_columns(hidden, weight, down, up, magnitude, cotangent)
        return by_tokens(hidden, weight, down, up, magnitude, cotangent)

    in_specs = (
        P(("parts", "dp"), "tensor"),
        P("tensor", None),
        P(("parts", "tensor"), None),
        P("parts", None),
        P(("parts", "tensor")),
        P(("parts", "dp"), "tensor"),
    )
    out_specs = (
        P(("parts", "dp"), "tensor"),
        P(("parts", "dp"), "tensor"),
        P(("parts", "tensor"), None),
        P("parts", "tensor"),
        P(("parts", "tensor")),
    )
    return jax.shard_map(local, mesh=mesh, in_specs=in_specs, out_specs=out_specs, check_vma=False)
```

```python
import functools

import jax
import jax.numpy as jnp
from jax import lax
from jax.experimental import pallas as pl
from jax.experimental.pallas import tpu as pltpu
from jax.sharding import PartitionSpec as P

adapter_scale = 2.0
stability_floor = 1e-06
pad_rows = 16
vmem_bytes = 8 * 1024 * 1024
f32, bf16 = jnp.float32, jnp.bfloat16
small_cost = pl.CostEstimate(flops=0, bytes_accessed=0, transcendentals=0)
contract_trailing = (((1,), (1,)), ((), ()))
contract_first = (((0,), (0,)), ((), ()))


def dot(a, b, dims=(((1,), (0,)), ((), ()))):
    return lax.dot_general(a, b, dims, preferred_element_type=f32)


def split_pair(x):
    high = x.astype(bf16)
    return high, (x - high.astype(f32)).astype(bf16)


def sum_of_squares(w_ref):
    rows, width = w_ref.shape
    totals = [jnp.zeros((8, width), f32) for _ in range(2)]
    for i in range(rows // 16):
        w = w_ref[i * 16 : (i + 1) * 16, :].astype(f32)
        w = w * w
        totals[0] = totals[0] + w[:8]
        totals[1] = totals[1] + w[8:]
    return jnp.sum(totals[0] + totals[1], axis=0, keepdims=True)


def vmem():
    return pl.BlockSpec(memory_space=pltpu.VMEM)


def anywhere():
    return pl.BlockSpec(memory_space=pl.ANY)


def params():
    return pltpu.CompilerParams(vmem_limit_bytes=vmem_bytes)


def block_kernel(tokens, order_ref, own_ref, other_ref, magnitude_ref, *refs):
    out_ref = refs[-1]
    out_ref[:tokens, :] = own_ref[...]
    out_ref[tokens : 2 * tokens, :] = other_ref[...]
    out_ref[2 * tokens :, :] = magnitude_ref[...]


def own_block(order, cotangent, other, magnitude_rows, *early):
    tokens, columns = cotangent.shape
    half = columns // 2
    padded = 2 * tokens + pad_rows
    return pl.pallas_call(
        functools.partial(block_kernel, tokens),
        grid_spec=pltpu.PrefetchScalarGridSpec(
            num_scalar_prefetch=1,
            grid=(1,),
            in_specs=[
                pl.BlockSpec((tokens, half), lambda i, p: (0, lax.rem(p[0], 2))),
                pl.BlockSpec((tokens, half), lambda i, p: (0, lax.rem(p[0], 2))),
                pl.BlockSpec((pad_rows, half), lambda i, p: (0, lax.rem(p[0], 2))),
                *[vmem()] * len(early),
            ],
            out_specs=pl.BlockSpec((padded, half), lambda i, p: (0, 0)),
        ),
        out_shape=jax.ShapeDtypeStruct((padded, half), bf16),
        compiler_params=params(),
        cost_estimate=small_cost,
        name="own_block",
    )(order, cotangent, other, magnitude_rows, *early)


def load_kernel(tokens, rank, n, vs, first, order_ref, before_ref, at_ref, up_ref, w_hbm, *refs):
    held, (stats_ref, sem) = refs[: len(vs)], refs[len(vs) :]
    half = held[0].shape[1]
    columns = [pl.ds(pl.multiple_of(order_ref[v] * half, half), half) for v in vs]
    copies = [pltpu.make_async_copy(w_hbm.at[:, c], h, sem.at[k]) for k, (c, h) in enumerate(zip(columns, held))]
    for copy in copies:
        copy.start()

    down = at_ref[...]
    high, low = split_pair(dot(down, down, contract_trailing))
    if first:
        turned = dot(down, before_ref[...], contract_trailing)
        lanes = half // tokens
        span = rank // lanes
        stats_ref[:n, :] = jnp.zeros((n, half), f32)
        for j in range(lanes):
            stats_ref[n:, j * tokens : (j + 1) * tokens] = turned[j * span : (j + 1) * span]
    else:
        stats_ref[...] = before_ref[...]
    for k, v in enumerate(vs):
        copies[k].wait()
        up = up_ref[:, columns[k]]
        cross = 2 * dot(down, held[k][...]) + adapter_scale * (dot(high, up) + dot(low, up))
        cross = jnp.sum(up.astype(f32) * cross, axis=0, keepdims=True)
        stats_ref[pl.ds(order_ref[n + v], 1), :] = sum_of_squares(held[k]) + adapter_scale * cross


def load(vs, order, at, up, weight, half, own=None, before=None):
    n = order.shape[0] // 2
    rank, rows = at.shape
    first = before is None
    tokens = own.shape[0] if first else None
    stats = (n + rank * tokens // half, half) if first else before.shape
    return pl.pallas_call(
        functools.partial(load_kernel, tokens, rank, n, vs, first),
        in_specs=[pl.BlockSpec(memory_space=pltpu.SMEM), vmem(), vmem(), vmem(), anywhere()],
        out_specs=[vmem()] * (len(vs) + 1),
        out_shape=[jax.ShapeDtypeStruct((rows, half), bf16)] * len(vs) + [jax.ShapeDtypeStruct(stats, f32)],
        scratch_shapes=[pltpu.SemaphoreType.DMA((len(vs),))],
        compiler_params=params(),
        cost_estimate=small_cost,
        name="load",
    )(order, own if first else before, at, up, weight)


def forward_kernel(tokens, rank, vs, first, order_ref, *refs):
    if first:
        own_ref, other_ref, at_ref, up_ref, *held, out_ref, lhs_ref, adapter_ref, sem = refs
        copy = pltpu.make_async_copy(other_ref, lhs_ref.at[tokens:], sem)
        copy.start()
        lhs_ref[:tokens, :] = own_ref[...]
        copy.wait()
        high, low = split_pair(dot(lhs_ref[...], at_ref[...], contract_trailing))
        adapter_ref[:, :rank] = high
        adapter_ref[:, rank:] = low
    else:
        lhs_ref, adapter_ref, up_ref, *held, out_ref = refs
    half = out_ref.shape[2]
    for i, v in enumerate(vs):
        up = up_ref[:, pl.ds(pl.multiple_of(order_ref[v] * half, half), half)]
        through = dot(adapter_ref[...], jnp.concatenate([up, up], axis=0))
        out_ref[i] = (dot(lhs_ref[...], held[i][...]) + adapter_scale * through).astype(bf16)


def forward(vs, order, held, up, first=None, later=None):
    rows, half = held[0].shape
    if later is None:
        own, other, at = operands = first
        tokens, rank = own.shape[0], at.shape[0]
        specs = [vmem(), anywhere(), vmem()]
    else:
        lhs, adapter = operands = later
        rank, tokens = adapter.shape[1] // 2, lhs.shape[0] // 2
        specs = [vmem()] * 2
    extra = [((2 * tokens, rows), bf16), ((2 * tokens, 2 * rank), bf16)] if first else []
    return pl.pallas_call(
        functools.partial(forward_kernel, tokens, rank, vs, later is None),
        in_specs=[pl.BlockSpec(memory_space=pltpu.SMEM), *specs] + [vmem()] * (1 + len(held)),
        out_specs=[vmem()] * (1 + len(extra)),
        out_shape=[jax.ShapeDtypeStruct((len(held), 2 * tokens, half), bf16)]
        + [jax.ShapeDtypeStruct(*e) for e in extra],
        scratch_shapes=[pltpu.SemaphoreType.DMA] if first else [],
        compiler_params=params(),
        cost_estimate=small_cost,
        name="forward",
    )(order, *operands, up, *held)


def backward_kernel(tokens, n, start, band, first, order_ref, *refs):
    if first:
        cots, (stats_ref, up_ref, at_ref, *held) = refs[:n], refs[n : 2 * n + 3]
        own_out, other_out, scaled_ref, proj_ref, scales_ref, block_ref = refs[2 * n + 3 :]
    else:
        scaled_ref, proj_ref, at_ref, *held, own_out, other_out = refs
    both = 2 * tokens
    half = held[0].shape[1]
    spans = [slice(k * half, (k + 1) * half) for k in range(n)]

    if first:

        @pl.when(pl.program_id(0) == 0)
        def _():
            projected = jnp.zeros(proj_ref.shape, f32)
            for k in range(n):
                magnitude = jnp.sum(cots[k][both:, :].astype(f32), axis=0, keepdims=True)
                squares = stats_ref[pl.ds(order_ref[n + k], 1), :]
                norm = jnp.sqrt(squares + stability_floor)
                rescale = magnitude / norm
                if k == 0:
                    scales_ref[0:1, :] = norm
                    scales_ref[1:2, :] = rescale
                scaled = (cots[k][:both, :].astype(f32) * rescale).astype(bf16)
                if k == 0:
                    block_ref[...] = scaled
                scaled_ref[:, spans[k]] = scaled
                up = up_ref[:, pl.ds(pl.multiple_of(order_ref[k] * half, half), half)]
                projected = projected + dot(scaled, up, contract_trailing)
            proj_ref[...] = projected

    row = pl.ds(pl.multiple_of((start + pl.program_id(0)) * band, band), band)
    total = adapter_scale * dot(proj_ref[...].astype(bf16), at_ref[:, row])
    for k in range(n):
        total = total + dot(scaled_ref[:, spans[k]], held[k][row, :], contract_trailing)
    own_out[...] = total[:tokens]
    other_out[...] = total[tokens:].astype(bf16)


def backward(order, start, bands, band, at, held, first=None, later=None):
    n = order.shape[0] // 2
    half = held[0].shape[1]
    rank = at.shape[0]
    if later is None:
        cots, stats, up = first
        both = cots[0].shape[0] - pad_rows
        operands = [*cots, stats, up]
        extra = [((both, n * half), bf16), ((both, rank), f32), ((2, half), f32), ((both, half), bf16)]
    else:
        operands, extra = later, []
        both = later[0].shape[0]
    tokens = both // 2
    return pl.pallas_call(
        functools.partial(backward_kernel, tokens, n, start, band, later is None),
        grid=(bands,),
        in_specs=[pl.BlockSpec(memory_space=pltpu.SMEM)] + [vmem()] * (len(operands) + 1 + n),
        out_specs=[pl.BlockSpec((tokens, band), lambda i: (0, i))] * 2 + [vmem()] * len(extra),
        out_shape=[
            jax.ShapeDtypeStruct((tokens, bands * band), f32),
            jax.ShapeDtypeStruct((tokens, bands * band), bf16),
        ]
        + [jax.ShapeDtypeStruct(*e) for e in extra],
        compiler_params=params(),
        cost_estimate=small_cost,
        name="backward",
    )(order, *operands, at, *held)


def core_halves(order_ref, ref, own, other, axis):
    half = own.shape[axis]
    low, high = (slice(None),) * axis + (slice(0, half),), (slice(None),) * axis + (slice(half, 2 * half),)
    core = lax.rem(order_ref[0], 2)

    @pl.when(core == 0)
    def _():
        ref[low] = own
        ref[high] = other

    @pl.when(core == 1)
    def _():
        ref[low] = other
        ref[high] = own


def weights_kernel(tokens, order_ref, proj_ref, from_ref, own_ref, other_ref, up_ref, up_other_ref, down_out, up_out):
    proj_own = (proj_ref[:tokens, :] + from_ref[tokens:, :]).astype(bf16)
    proj_other = (proj_ref[tokens:, :] + from_ref[:tokens, :]).astype(bf16)
    down_out[...] = adapter_scale * (
        dot(proj_own, own_ref[...], contract_first) + dot(proj_other, other_ref[...], contract_first)
    )
    core_halves(order_ref, up_out, up_ref[...], up_other_ref[...], 1)


def hidden_kernel(order_ref, ga_ref, ra_ref, gb_ref, rb_ref, out_ref):
    split = ga_ref.shape[1]
    out_ref[:, :split] = (ga_ref[...] + ra_ref[...].astype(f32)).astype(bf16)
    out_ref[:, split:] = (gb_ref[...] + rb_ref[...].astype(f32)).astype(bf16)


def mixed_kernel(order_ref, m_ref, m_other_ref, g_ref, g_other_ref, mixed_out, magnitude_out):
    tokens = m_other_ref.shape[0]
    core_halves(order_ref, mixed_out, m_ref[:tokens, :], m_other_ref[...], 1)
    rows = g_ref.shape[1] // 128
    stacked = [jnp.concatenate([r[:, i * 128 : (i + 1) * 128] for i in range(rows)]) for r in (g_ref, g_other_ref)]
    core_halves(order_ref, magnitude_out, *stacked, 0)


def finish(kernel, name, out_shape, order, *operands):
    whole = lambda x: pl.BlockSpec(x.shape, lambda i, p: (0,) * len(x.shape))
    return pl.pallas_call(
        kernel,
        grid_spec=pltpu.PrefetchScalarGridSpec(
            num_scalar_prefetch=1,
            grid=(1,),
            in_specs=[vmem()] * len(operands),
            out_specs=[whole(x) for x in out_shape],
        ),
        out_shape=out_shape,
        compiler_params=params(),
        cost_estimate=small_cost,
        name=name,
    )(order, *operands)


def finish_weights(order, proj, from_sibling, own, other, up_half, up_other):
    tokens, rows = own.shape
    rank, half = up_half.shape
    shapes = [jax.ShapeDtypeStruct((rank, rows), f32), jax.ShapeDtypeStruct((rank, 2 * half), f32)]
    kernel = functools.partial(weights_kernel, tokens)
    return finish(kernel, "weights", shapes, order, proj, from_sibling, own, other, up_half, up_other)


def finish_hidden(order, grad_a, got_a, grad_b, got_b):
    tokens = grad_a.shape[0]
    shape = jax.ShapeDtypeStruct((tokens, grad_a.shape[1] + grad_b.shape[1]), bf16)
    return finish(hidden_kernel, "hidden", [shape], order, grad_a, got_a, grad_b, got_b)[0]


def finish_mixed(order, mixed, mixed_other, magnitude, magnitude_other):
    tokens, half = mixed_other.shape
    shapes = [
        jax.ShapeDtypeStruct((tokens, 2 * half), bf16),
        jax.ShapeDtypeStruct((2 * half // 128, 128), f32),
    ]
    return finish(mixed_kernel, "mixed", shapes, order, mixed, mixed_other, magnitude, magnitude_other)


def split_columns(hidden, weight, down, up, magnitude, cotangent):
    n, bits = 8, 3
    tokens = hidden.shape[0]
    half = magnitude.shape[0] // 2
    rows = weight.shape[0]
    me, core = lax.axis_index("tensor"), lax.axis_index("dp")
    swap = lambda x: lax.ppermute(x, "dp", [(0, 1), (1, 0)])
    orders = [[1, 2, 4], [2, 1, 4]]

    def send(x, k):
        pairs = [(2 * t + c, 2 * (t ^ orders[c][k]) + c) for t in range(n) for c in range(2)]
        return lax.ppermute(x, ("tensor", "dp"), pairs)

    def reach(v, c):
        return sum(orders[c][k] for k in range(bits) if v >> (bits - 1 - k) & 1)

    def place(*vs):
        shard = [me ^ jnp.where(core == 0, reach(v, 0), reach(v, 1)) for v in vs]
        return jnp.stack([2 * s + core for s in shard] + shard).astype(jnp.int32)

    tie = lax.optimization_barrier
    at = down.T
    order = place(*range(n))
    low_core = core == 0

    cot_other = swap(cotangent)
    hidden_other = swap(hidden)
    first = lax.reduce_precision(magnitude, 8, 7)
    second = lax.reduce_precision(magnitude - first, 8, 7)
    third = magnitude - first - second
    magnitude_rows = jnp.concatenate(
        [jnp.stack([first, second, third]), jnp.zeros((pad_rows - 3, 2 * half), f32)]
    ).astype(bf16)
    low_core, order, cot_other = tie((low_core, order, cot_other))
    block = own_block(order, cotangent, cot_other, magnitude_rows)

    cots = {0b000: block, 0b001: send(block, 2), 0b010: send(block, 1), 0b100: send(block, 0)}
    across = [(2 * t + c, 2 * (t ^ orders[c][0] ^ orders[c][1]) + c) for t in range(n) for c in range(2)]
    cots[0b110] = lax.ppermute(block, ("tensor", "dp"), across)

    run_load = functools.partial(load, at=at, up=up, weight=weight, half=half)
    block, order = tie((block, order))
    *held, stats = run_load(tuple(range(n)), order, own=hidden)
    near, far = held[: n // 2], held[n // 2 :]
    cots[0b001], cots[0b010], cots[0b100], stats = tie((cots[0b001], cots[0b010], cots[0b100], stats))
    cots[0b011], cots[0b101] = send(cots[0b001], 1), send(cots[0b001], 0)
    got = send(stats, 0)
    far1, lhs, adapter = forward((0b110, 0b111), order, far[2:], up, first=(hidden, hidden_other, at))
    run = lambda order, vs, held: forward(vs, order, held, up, later=(lhs, adapter))[0]
    got, cots[0b011], cots[0b110], far1, order = tie((got, cots[0b011], cots[0b110], far1, order))
    cots[0b111] = send(cots[0b011], 0)
    stats = stats + got
    got = send(stats, 1)
    from1 = send(far1, 0)
    far0 = run(order, (0b100, 0b101), far[:2])
    got, far0, order = tie((got, far0, order))
    stats = stats + got
    got = send(stats, 2)
    from0_high, from0_low = send(far0[1], 0), send(far0[0], 0)
    near1 = run(order, (0b010, 0b011), near[2:])
    got, from1, cots[0b101], cots[0b111], near1, order = tie((got, from1, cots[0b101], cots[0b111], near1, order))
    stats = stats + got
    total = (near1.astype(f32) + from1.astype(f32)).astype(bf16)
    high, low = send(total[1], 1), send(total[0], 1)
    lowrank_rows = stats[n:]
    lowrank_other = swap(lowrank_rows)
    near0 = run(order, (0b000, 0b001), near[:2])
    near0, order = tie((near0, order))

    band = 256
    bands = rows // band
    many = max(bands * 2 // 14, 1)
    run = functools.partial(backward, order, band=band, at=at, held=held)
    grad_a, other_a, scaled, proj, scales, scaled_own = run(0, many, first=([cots[v] for v in range(n)], stats, up))
    from_sibling = swap(proj)
    high, from0_high, lowrank_other, scaled_own = tie((high, from0_high, lowrank_other, scaled_own))
    last = send((near0[1].astype(f32) + from0_high.astype(f32) + high.astype(f32)).astype(bf16), 2)
    scaled_own = scaled_own.astype(f32)

    def turned(part):
        lanes = half // tokens
        return jnp.concatenate([part[:, j * tokens : (j + 1) * tokens] for j in range(lanes)])

    up_half = adapter_scale * (
        jnp.dot(turned(lowrank_rows), scaled_own[:tokens], precision=lax.Precision.HIGHEST)
        + jnp.dot(turned(lowrank_other), scaled_own[tokens:], precision=lax.Precision.HIGHEST)
    )
    up_other = swap(up_half)
    grad_b, other_b = backward(order, many, bands - many, band, at, held, later=(scaled, proj))
    other_a, from_sibling, up_other, other_b = tie((other_a, from_sibling, up_other, other_b))
    got_a, got_b = swap(other_a), swap(other_b)

    down_weight_gradient, up_weight_gradient = finish_weights(
        order, proj, from_sibling, hidden, hidden_other, up_half, up_other
    )

    last, low, from0_low, down_weight_gradient = tie((last, low, from0_low, down_weight_gradient))
    unscaled = near0[0].astype(f32) + from0_low.astype(f32) + low.astype(f32) + last.astype(f32)
    mixed = (unscaled * scales[1]).astype(bf16)
    magnitude_half = jnp.sum(block[: 2 * tokens].astype(f32) * unscaled, axis=0, keepdims=True) / scales[0:1]
    mixed_other, magnitude_other = swap(mixed[tokens:]), swap(magnitude_half)
    hidden_gradient = finish_hidden(order, grad_a, got_a, grad_b, got_b)
    mixed_other, magnitude_other, hidden_gradient = tie((mixed_other, magnitude_other, hidden_gradient))
    mixed, grad_magnitude = finish_mixed(order, mixed, mixed_other, magnitude_half, magnitude_other)
    down_weight_gradient, grad_magnitude = down_weight_gradient.T, grad_magnitude.reshape(2 * half)
    return (mixed, hidden_gradient, down_weight_gradient, up_weight_gradient, grad_magnitude)


def by_tokens(hidden, frozen_down_weight, adapter_down_weight, adapter_up_weight, magnitude, cotangent):
    column_slice = magnitude.shape[0]
    block_offset = lax.axis_index("tensor") * column_slice
    combined_weight = frozen_down_weight.astype(f32) + adapter_scale * dot(adapter_down_weight, adapter_up_weight)
    squares_part = jnp.sum(combined_weight * combined_weight, axis=0)
    squares, reduced_rank_product = lax.psum((squares_part, dot(hidden, adapter_down_weight)), "tensor")
    norm_all = jnp.sqrt(squares + stability_floor)
    column_length_norm = lax.dynamic_slice_in_dim(norm_all, block_offset, column_slice)
    up_weight_columns = lax.dynamic_slice_in_dim(adapter_up_weight, block_offset, column_slice, 1)
    summed_output = lax.psum_scatter(dot(hidden, frozen_down_weight), "tensor", scatter_dimension=1, tiled=True)
    unscaled_output = summed_output + adapter_scale * jnp.dot(
        reduced_rank_product, up_weight_columns.astype(f32), precision=lax.Precision.HIGHEST
    )
    rescale = magnitude / column_length_norm
    mixed = (unscaled_output * rescale).astype(bf16)
    upstream = cotangent.astype(f32)
    scaled_output = (upstream * rescale).astype(bf16)
    magnitude_part = jnp.sum(upstream * unscaled_output, axis=0) / column_length_norm
    block_input = lax.all_gather(scaled_output, "tensor", axis=1, tiled=True)
    projected_output = dot(block_input, adapter_up_weight, contract_trailing).astype(bf16)
    hidden_gradient = dot(block_input, frozen_down_weight, contract_trailing)
    hidden_gradient = hidden_gradient + adapter_scale * dot(projected_output, adapter_down_weight, contract_trailing)
    hidden_gradient = hidden_gradient.astype(bf16)
    down_gradient_piece = adapter_scale * dot(hidden, projected_output, contract_first)
    up_gradient_piece = adapter_scale * lax.dot_general(
        reduced_rank_product, scaled_output.astype(f32), contract_first, precision=lax.Precision.HIGHEST
    )
    pieces = (down_gradient_piece, up_gradient_piece, magnitude_part)
    pieces = [lax.psum(p.astype(bf16), "dp").astype(f32) for p in pieces]
    return (mixed, hidden_gradient, *pieces)


def solution(mesh):
    n = mesh.shape["tensor"]

    def local(hidden, weight, down, up, magnitude, cotangent):
        aligned = magnitude.shape[0] % 256 == 0 and weight.shape[0] % 256 == 0 and hidden.shape[0] % 128 == 0
        if aligned and mesh.shape["dp"] == 2 and n == 8 and down.shape[1] * hidden.shape[0] % (magnitude.shape[0] // 2 * 8) == 0:
            return split_columns(hidden, weight, down, up, magnitude, cotangent)
        return by_tokens(hidden, weight, down, up, magnitude, cotangent)

    in_specs = (
        P(("parts", "dp"), "tensor"),
        P("tensor", None),
        P(("parts", "tensor"), None),
        P("parts", None),
        P(("parts", "tensor")),
        P(("parts", "dp"), "tensor"),
    )
    out_specs = (
        P(("parts", "dp"), "tensor"),
        P(("parts", "dp"), "tensor"),
        P(("parts", "tensor"), None),
        P("parts", "tensor"),
        P(("parts", "tensor")),
    )
    return jax.shard_map(local, mesh=mesh, in_specs=in_specs, out_specs=out_specs, check_vma=False)
```

```python
import functools

import jax
import jax.numpy as jnp
from jax import lax
from jax.experimental import pallas as pl
from jax.experimental.pallas import tpu as pltpu
from jax.sharding import PartitionSpec as P

adapter_scale = 2.0
stability_floor = 1e-06
pad_rows = 16
vmem_bytes = 8 * 1024 * 1024
f32, bf16 = jnp.float32, jnp.bfloat16
small_cost = pl.CostEstimate(flops=0, bytes_accessed=0, transcendentals=0)
contract_trailing = (((1,), (1,)), ((), ()))
contract_first = (((0,), (0,)), ((), ()))


def dot(a, b, dims=(((1,), (0,)), ((), ()))):
    return lax.dot_general(a, b, dims, preferred_element_type=f32)


def split_pair(x):
    high = x.astype(bf16)
    return high, (x - high.astype(f32)).astype(bf16)


def sum_of_squares(w_ref):
    rows, width = w_ref.shape
    totals = [jnp.zeros((8, width), f32) for _ in range(2)]
    for i in range(rows // 16):
        w = w_ref[i * 16 : (i + 1) * 16, :].astype(f32)
        w = w * w
        totals[0] = totals[0] + w[:8]
        totals[1] = totals[1] + w[8:]
    return jnp.sum(totals[0] + totals[1], axis=0, keepdims=True)


def vmem():
    return pl.BlockSpec(memory_space=pltpu.VMEM)


def anywhere():
    return pl.BlockSpec(memory_space=pl.ANY)


def params():
    return pltpu.CompilerParams(vmem_limit_bytes=vmem_bytes)


def block_kernel(tokens, order_ref, own_ref, other_ref, magnitude_ref, *refs):
    out_ref = refs[-1]
    out_ref[:tokens, :] = own_ref[...]
    out_ref[tokens : 2 * tokens, :] = other_ref[...]
    out_ref[2 * tokens :, :] = magnitude_ref[...]


def own_block(order, cotangent, other, magnitude_rows, *early):
    tokens, columns = cotangent.shape
    half = columns // 2
    padded = 2 * tokens + pad_rows
    return pl.pallas_call(
        functools.partial(block_kernel, tokens),
        grid_spec=pltpu.PrefetchScalarGridSpec(
            num_scalar_prefetch=1,
            grid=(1,),
            in_specs=[
                pl.BlockSpec((tokens, half), lambda i, p: (0, lax.rem(p[0], 2))),
                pl.BlockSpec((tokens, half), lambda i, p: (0, lax.rem(p[0], 2))),
                pl.BlockSpec((pad_rows, half), lambda i, p: (0, lax.rem(p[0], 2))),
                *[vmem()] * len(early),
            ],
            out_specs=pl.BlockSpec((padded, half), lambda i, p: (0, 0)),
        ),
        out_shape=jax.ShapeDtypeStruct((padded, half), bf16),
        compiler_params=params(),
        cost_estimate=small_cost,
        name="own_block",
    )(order, cotangent, other, magnitude_rows, *early)


def load_kernel(tokens, rank, n, vs, first, order_ref, before_ref, at_ref, up_ref, w_hbm, *refs):
    held, (stats_ref, sem) = refs[: len(vs)], refs[len(vs) :]
    half = held[0].shape[1]
    columns = [pl.ds(pl.multiple_of(order_ref[v] * half, half), half) for v in vs]
    copies = [pltpu.make_async_copy(w_hbm.at[:, c], h, sem.at[k]) for k, (c, h) in enumerate(zip(columns, held))]
    for copy in copies:
        copy.start()

    down = at_ref[...]
    high, low = split_pair(dot(down, down, contract_trailing))
    if first:
        turned = dot(down, before_ref[...], contract_trailing)
        lanes = half // tokens
        span = rank // lanes
        stats_ref[:n, :] = jnp.zeros((n, half), f32)
        for j in range(lanes):
            stats_ref[n:, j * tokens : (j + 1) * tokens] = turned[j * span : (j + 1) * span]
    else:
        stats_ref[...] = before_ref[...]
    for k, v in enumerate(vs):
        copies[k].wait()
        up = up_ref[:, columns[k]]
        cross = 2 * dot(down, held[k][...]) + adapter_scale * (dot(high, up) + dot(low, up))
        cross = jnp.sum(up.astype(f32) * cross, axis=0, keepdims=True)
        stats_ref[pl.ds(order_ref[n + v], 1), :] = sum_of_squares(held[k]) + adapter_scale * cross


def load(vs, order, at, up, weight, half, own=None, before=None):
    n = order.shape[0] // 2
    rank, rows = at.shape
    first = before is None
    tokens = own.shape[0] if first else None
    stats = (n + rank * tokens // half, half) if first else before.shape
    return pl.pallas_call(
        functools.partial(load_kernel, tokens, rank, n, vs, first),
        in_specs=[pl.BlockSpec(memory_space=pltpu.SMEM), vmem(), vmem(), vmem(), anywhere()],
        out_specs=[vmem()] * (len(vs) + 1),
        out_shape=[jax.ShapeDtypeStruct((rows, half), bf16)] * len(vs) + [jax.ShapeDtypeStruct(stats, f32)],
        scratch_shapes=[pltpu.SemaphoreType.DMA((len(vs),))],
        compiler_params=params(),
        cost_estimate=small_cost,
        name="load",
    )(order, own if first else before, at, up, weight)


def forward_kernel(tokens, rank, vs, first, order_ref, *refs):
    if first:
        own_ref, other_ref, at_ref, up_ref, *held, out_ref, lhs_ref, adapter_ref, sem = refs
        copy = pltpu.make_async_copy(other_ref, lhs_ref.at[tokens:], sem)
        copy.start()
        lhs_ref[:tokens, :] = own_ref[...]
        copy.wait()
        high, low = split_pair(dot(lhs_ref[...], at_ref[...], contract_trailing))
        adapter_ref[:, :rank] = high
        adapter_ref[:, rank:] = low
    else:
        lhs_ref, adapter_ref, up_ref, *held, out_ref = refs
    half = out_ref.shape[2]
    for i, v in enumerate(vs):
        up = up_ref[:, pl.ds(pl.multiple_of(order_ref[v] * half, half), half)]
        through = dot(adapter_ref[...], jnp.concatenate([up, up], axis=0))
        out_ref[i] = (dot(lhs_ref[...], held[i][...]) + adapter_scale * through).astype(bf16)


def forward(vs, order, held, up, first=None, later=None):
    rows, half = held[0].shape
    if later is None:
        own, other, at = operands = first
        tokens, rank = own.shape[0], at.shape[0]
        specs = [vmem(), anywhere(), vmem()]
    else:
        lhs, adapter = operands = later
        rank, tokens = adapter.shape[1] // 2, lhs.shape[0] // 2
        specs = [vmem()] * 2
    extra = [((2 * tokens, rows), bf16), ((2 * tokens, 2 * rank), bf16)] if first else []
    return pl.pallas_call(
        functools.partial(forward_kernel, tokens, rank, vs, later is None),
        in_specs=[pl.BlockSpec(memory_space=pltpu.SMEM), *specs] + [vmem()] * (1 + len(held)),
        out_specs=[vmem()] * (1 + len(extra)),
        out_shape=[jax.ShapeDtypeStruct((len(held), 2 * tokens, half), bf16)]
        + [jax.ShapeDtypeStruct(*e) for e in extra],
        scratch_shapes=[pltpu.SemaphoreType.DMA] if first else [],
        compiler_params=params(),
        cost_estimate=small_cost,
        name="forward",
    )(order, *operands, up, *held)


def backward_kernel(tokens, n, start, band, first, order_ref, *refs):
    if first:
        cots, (stats_ref, up_ref, at_ref, *held) = refs[:n], refs[n : 2 * n + 3]
        own_out, other_out, scaled_ref, proj_ref, scales_ref, block_ref = refs[2 * n + 3 :]
    else:
        scaled_ref, proj_ref, at_ref, *held, own_out, other_out = refs
    both = 2 * tokens
    half = held[0].shape[1]
    spans = [slice(k * half, (k + 1) * half) for k in range(n)]

    if first:

        @pl.when(pl.program_id(0) == 0)
        def _():
            projected = jnp.zeros(proj_ref.shape, f32)
            for k in range(n):
                magnitude = jnp.sum(cots[k][both:, :].astype(f32), axis=0, keepdims=True)
                squares = stats_ref[pl.ds(order_ref[n + k], 1), :]
                norm = jnp.sqrt(squares + stability_floor)
                rescale = magnitude / norm
                if k == 0:
                    scales_ref[0:1, :] = norm
                    scales_ref[1:2, :] = rescale
                scaled = (cots[k][:both, :].astype(f32) * rescale).astype(bf16)
                if k == 0:
                    block_ref[...] = scaled
                scaled_ref[:, spans[k]] = scaled
                up = up_ref[:, pl.ds(pl.multiple_of(order_ref[k] * half, half), half)]
                projected = projected + dot(scaled, up, contract_trailing)
            proj_ref[...] = projected

    row = pl.ds(pl.multiple_of((start + pl.program_id(0)) * band, band), band)
    total = adapter_scale * dot(proj_ref[...].astype(bf16), at_ref[:, row])
    for k in range(n):
        total = total + dot(scaled_ref[:, spans[k]], held[k][row, :], contract_trailing)
    own_out[...] = total[:tokens]
    other_out[...] = total[tokens:].astype(bf16)


def backward(order, start, bands, band, at, held, first=None, later=None):
    n = order.shape[0] // 2
    half = held[0].shape[1]
    rank = at.shape[0]
    if later is None:
        cots, stats, up = first
        both = cots[0].shape[0] - pad_rows
        operands = [*cots, stats, up]
        extra = [((both, n * half), bf16), ((both, rank), f32), ((2, half), f32), ((both, half), bf16)]
    else:
        operands, extra = later, []
        both = later[0].shape[0]
    tokens = both // 2
    return pl.pallas_call(
        functools.partial(backward_kernel, tokens, n, start, band, later is None),
        grid=(bands,),
        in_specs=[pl.BlockSpec(memory_space=pltpu.SMEM)] + [vmem()] * (len(operands) + 1 + n),
        out_specs=[pl.BlockSpec((tokens, band), lambda i: (0, i))] * 2 + [vmem()] * len(extra),
        out_shape=[
            jax.ShapeDtypeStruct((tokens, bands * band), f32),
            jax.ShapeDtypeStruct((tokens, bands * band), bf16),
        ]
        + [jax.ShapeDtypeStruct(*e) for e in extra],
        compiler_params=params(),
        cost_estimate=small_cost,
        name="backward",
    )(order, *operands, at, *held)


def core_halves(order_ref, ref, own, other, axis):
    half = own.shape[axis]
    low, high = (slice(None),) * axis + (slice(0, half),), (slice(None),) * axis + (slice(half, 2 * half),)
    core = lax.rem(order_ref[0], 2)

    @pl.when(core == 0)
    def _():
        ref[low] = own
        ref[high] = other

    @pl.when(core == 1)
    def _():
        ref[low] = other
        ref[high] = own


def weights_kernel(tokens, order_ref, proj_ref, from_ref, own_ref, other_ref, up_ref, up_other_ref, down_out, up_out):
    proj_own = (proj_ref[:tokens, :] + from_ref[tokens:, :]).astype(bf16)
    proj_other = (proj_ref[tokens:, :] + from_ref[:tokens, :]).astype(bf16)
    down_out[...] = adapter_scale * (
        dot(proj_own, own_ref[...], contract_first) + dot(proj_other, other_ref[...], contract_first)
    )
    core_halves(order_ref, up_out, up_ref[...], up_other_ref[...], 1)


def hidden_kernel(order_ref, ga_ref, ra_ref, gb_ref, rb_ref, out_ref):
    split = ga_ref.shape[1]
    out_ref[:, :split] = (ga_ref[...] + ra_ref[...].astype(f32)).astype(bf16)
    out_ref[:, split:] = (gb_ref[...] + rb_ref[...].astype(f32)).astype(bf16)


def mixed_kernel(order_ref, m_ref, m_other_ref, g_ref, g_other_ref, mixed_out, magnitude_out):
    tokens = m_other_ref.shape[0]
    core_halves(order_ref, mixed_out, m_ref[:tokens, :], m_other_ref[...], 1)
    rows = g_ref.shape[1] // 128
    stacked = [jnp.concatenate([r[:, i * 128 : (i + 1) * 128] for i in range(rows)]) for r in (g_ref, g_other_ref)]
    core_halves(order_ref, magnitude_out, *stacked, 0)


def finish(kernel, name, out_shape, order, *operands):
    whole = lambda x: pl.BlockSpec(x.shape, lambda i, p: (0,) * len(x.shape))
    return pl.pallas_call(
        kernel,
        grid_spec=pltpu.PrefetchScalarGridSpec(
            num_scalar_prefetch=1,
            grid=(1,),
            in_specs=[vmem()] * len(operands),
            out_specs=[whole(x) for x in out_shape],
        ),
        out_shape=out_shape,
        compiler_params=params(),
        cost_estimate=small_cost,
        name=name,
    )(order, *operands)


def finish_weights(order, proj, from_sibling, own, other, up_half, up_other):
    tokens, rows = own.shape
    rank, half = up_half.shape
    shapes = [jax.ShapeDtypeStruct((rank, rows), f32), jax.ShapeDtypeStruct((rank, 2 * half), f32)]
    kernel = functools.partial(weights_kernel, tokens)
    return finish(kernel, "weights", shapes, order, proj, from_sibling, own, other, up_half, up_other)


def finish_hidden(order, grad_a, got_a, grad_b, got_b):
    tokens = grad_a.shape[0]
    shape = jax.ShapeDtypeStruct((tokens, grad_a.shape[1] + grad_b.shape[1]), bf16)
    return finish(hidden_kernel, "hidden", [shape], order, grad_a, got_a, grad_b, got_b)[0]


def finish_mixed(order, mixed, mixed_other, magnitude, magnitude_other):
    tokens, half = mixed_other.shape
    shapes = [
        jax.ShapeDtypeStruct((tokens, 2 * half), bf16),
        jax.ShapeDtypeStruct((2 * half // 128, 128), f32),
    ]
    return finish(mixed_kernel, "mixed", shapes, order, mixed, mixed_other, magnitude, magnitude_other)


def split_columns(hidden, weight, down, up, magnitude, cotangent):
    n, bits = 8, 3
    tokens = hidden.shape[0]
    half = magnitude.shape[0] // 2
    rows = weight.shape[0]
    me, core = lax.axis_index("tensor"), lax.axis_index("dp")
    swap = lambda x: lax.ppermute(x, "dp", [(0, 1), (1, 0)])
    orders = [[1, 2, 4], [2, 1, 4]]

    def send(x, k):
        pairs = [(2 * t + c, 2 * (t ^ orders[c][k]) + c) for t in range(n) for c in range(2)]
        return lax.ppermute(x, ("tensor", "dp"), pairs)

    def reach(v, c):
        return sum(orders[c][k] for k in range(bits) if v >> (bits - 1 - k) & 1)

    def place(*vs):
        shard = [me ^ jnp.where(core == 0, reach(v, 0), reach(v, 1)) for v in vs]
        return jnp.stack([2 * s + core for s in shard] + shard).astype(jnp.int32)

    tie = lax.optimization_barrier
    at = down.T
    order = place(*range(n))
    low_core = core == 0

    cot_other = swap(cotangent)
    hidden_other = swap(hidden)
    first = lax.reduce_precision(magnitude, 8, 7)
    second = lax.reduce_precision(magnitude - first, 8, 7)
    third = magnitude - first - second
    magnitude_rows = jnp.concatenate(
        [jnp.stack([first, second, third]), jnp.zeros((pad_rows - 3, 2 * half), f32)]
    ).astype(bf16)
    low_core, order, cot_other = tie((low_core, order, cot_other))
    block = own_block(order, cotangent, cot_other, magnitude_rows)

    cots = {0b000: block, 0b001: send(block, 2), 0b010: send(block, 1), 0b100: send(block, 0)}
    across = [(2 * t + c, 2 * (t ^ orders[c][0] ^ orders[c][1]) + c) for t in range(n) for c in range(2)]
    cots[0b110] = lax.ppermute(block, ("tensor", "dp"), across)

    run_load = functools.partial(load, at=at, up=up, weight=weight, half=half)
    block, order = tie((block, order))
    *held, stats = run_load(tuple(range(n)), order, own=hidden)
    near, far = held[: n // 2], held[n // 2 :]
    cots[0b001], cots[0b010], cots[0b100], stats = tie((cots[0b001], cots[0b010], cots[0b100], stats))
    cots[0b011], cots[0b101] = send(cots[0b001], 1), send(cots[0b001], 0)
    got = send(stats, 0)
    far1, lhs, adapter = forward((0b110, 0b111), order, far[2:], up, first=(hidden, hidden_other, at))
    run = lambda order, vs, held: forward(vs, order, held, up, later=(lhs, adapter))[0]
    got, cots[0b011], cots[0b110], far1, order = tie((got, cots[0b011], cots[0b110], far1, order))
    cots[0b111] = send(cots[0b011], 0)
    stats = stats + got
    got = send(stats, 1)
    from1 = send(far1, 0)
    far0 = run(order, (0b100, 0b101), far[:2])
    got, far0, order = tie((got, far0, order))
    stats = stats + got
    got = send(stats, 2)
    from0_high, from0_low = send(far0[1], 0), send(far0[0], 0)
    near1 = run(order, (0b010, 0b011), near[2:])
    got, from1, cots[0b101], cots[0b111], near1, order = tie((got, from1, cots[0b101], cots[0b111], near1, order))
    stats = stats + got
    total = (near1.astype(f32) + from1.astype(f32)).astype(bf16)
    high, low = send(total[1], 1), send(total[0], 1)
    lowrank_rows = stats[n:]
    lowrank_other = swap(lowrank_rows)
    near0 = run(order, (0b000, 0b001), near[:2])
    near0, order = tie((near0, order))

    band = 256
    bands = rows // band
    many = max(bands * 3 // 14, 1)
    run = functools.partial(backward, order, band=band, at=at, held=held)
    grad_a, other_a, scaled, proj, scales, scaled_own = run(0, many, first=([cots[v] for v in range(n)], stats, up))
    high, from0_high, lowrank_other, scaled_own, scaled = tie((high, from0_high, lowrank_other, scaled_own, scaled))
    last = send((near0[1].astype(f32) + from0_high.astype(f32) + high.astype(f32)).astype(bf16), 2)
    scaled_own = scaled_own.astype(f32)

    def turned(part):
        lanes = half // tokens
        return jnp.concatenate([part[:, j * tokens : (j + 1) * tokens] for j in range(lanes)])

    up_half = adapter_scale * (
        jnp.dot(turned(lowrank_rows), scaled_own[:tokens], precision=lax.Precision.HIGHEST)
        + jnp.dot(turned(lowrank_other), scaled_own[tokens:], precision=lax.Precision.HIGHEST)
    )
    grad_b, other_b = backward(order, many, bands - many, band, at, held, later=(scaled, proj))
    other_a, proj, up_half, other_b = tie((other_a, proj, up_half, other_b))
    from_sibling, up_other = swap(proj), swap(up_half)
    got_a, got_b = swap(other_a), swap(other_b)

    down_weight_gradient, up_weight_gradient = finish_weights(
        order, proj, from_sibling, hidden, hidden_other, up_half, up_other
    )

    last, low, from0_low, down_weight_gradient = tie((last, low, from0_low, down_weight_gradient))
    unscaled = near0[0].astype(f32) + from0_low.astype(f32) + low.astype(f32) + last.astype(f32)
    mixed = (unscaled * scales[1]).astype(bf16)
    magnitude_half = jnp.sum(block[: 2 * tokens].astype(f32) * unscaled, axis=0, keepdims=True) / scales[0:1]
    mixed_other, magnitude_other = swap(mixed[tokens:]), swap(magnitude_half)
    hidden_gradient = finish_hidden(order, grad_a, got_a, grad_b, got_b)
    mixed_other, magnitude_other, hidden_gradient = tie((mixed_other, magnitude_other, hidden_gradient))
    mixed, grad_magnitude = finish_mixed(order, mixed, mixed_other, magnitude_half, magnitude_other)
    down_weight_gradient, grad_magnitude = down_weight_gradient.T, grad_magnitude.reshape(2 * half)
    return (mixed, hidden_gradient, down_weight_gradient, up_weight_gradient, grad_magnitude)


def by_tokens(hidden, frozen_down_weight, adapter_down_weight, adapter_up_weight, magnitude, cotangent):
    column_slice = magnitude.shape[0]
    block_offset = lax.axis_index("tensor") * column_slice
    combined_weight = frozen_down_weight.astype(f32) + adapter_scale * dot(adapter_down_weight, adapter_up_weight)
    squares_part = jnp.sum(combined_weight * combined_weight, axis=0)
    squares, reduced_rank_product = lax.psum((squares_part, dot(hidden, adapter_down_weight)), "tensor")
    norm_all = jnp.sqrt(squares + stability_floor)
    column_length_norm = lax.dynamic_slice_in_dim(norm_all, block_offset, column_slice)
    up_weight_columns = lax.dynamic_slice_in_dim(adapter_up_weight, block_offset, column_slice, 1)
    summed_output = lax.psum_scatter(dot(hidden, frozen_down_weight), "tensor", scatter_dimension=1, tiled=True)
    unscaled_output = summed_output + adapter_scale * jnp.dot(
        reduced_rank_product, up_weight_columns.astype(f32), precision=lax.Precision.HIGHEST
    )
    rescale = magnitude / column_length_norm
    mixed = (unscaled_output * rescale).astype(bf16)
    upstream = cotangent.astype(f32)
    scaled_output = (upstream * rescale).astype(bf16)
    magnitude_part = jnp.sum(upstream * unscaled_output, axis=0) / column_length_norm
    block_input = lax.all_gather(scaled_output, "tensor", axis=1, tiled=True)
    projected_output = dot(block_input, adapter_up_weight, contract_trailing).astype(bf16)
    hidden_gradient = dot(block_input, frozen_down_weight, contract_trailing)
    hidden_gradient = hidden_gradient + adapter_scale * dot(projected_output, adapter_down_weight, contract_trailing)
    hidden_gradient = hidden_gradient.astype(bf16)
    down_gradient_piece = adapter_scale * dot(hidden, projected_output, contract_first)
    up_gradient_piece = adapter_scale * lax.dot_general(
        reduced_rank_product, scaled_output.astype(f32), contract_first, precision=lax.Precision.HIGHEST
    )
    pieces = (down_gradient_piece, up_gradient_piece, magnitude_part)
    pieces = [lax.psum(p.astype(bf16), "dp").astype(f32) for p in pieces]
    return (mixed, hidden_gradient, *pieces)


def solution(mesh):
    n = mesh.shape["tensor"]

    def local(hidden, weight, down, up, magnitude, cotangent):
        aligned = magnitude.shape[0] % 256 == 0 and weight.shape[0] % 256 == 0 and hidden.shape[0] % 128 == 0
        if aligned and mesh.shape["dp"] == 2 and n == 8 and down.shape[1] * hidden.shape[0] % (magnitude.shape[0] // 2 * 8) == 0:
            return split_columns(hidden, weight, down, up, magnitude, cotangent)
        return by_tokens(hidden, weight, down, up, magnitude, cotangent)

    in_specs = (
        P(("parts", "dp"), "tensor"),
        P("tensor", None),
        P(("parts", "tensor"), None),
        P("parts", None),
        P(("parts", "tensor")),
        P(("parts", "dp"), "tensor"),
    )
    out_specs = (
        P(("parts", "dp"), "tensor"),
        P(("parts", "dp"), "tensor"),
        P(("parts", "tensor"), None),
        P("parts", "tensor"),
        P(("parts", "tensor")),
    )
    return jax.shard_map(local, mesh=mesh, in_specs=in_specs, out_specs=out_specs, check_vma=False)
```
